32 devices in a mesh: seq: 8 (over y, x, core), head: 4 (over z).
Axes of the slice: x: 2, y: 2, z: 4, core: 2. Of those that a mesh axis runs over, the one named last changes fastest.
Arguments:
- hidden: bfloat16 [768, 4096], P('seq'), may hold values from -6 to 6
- norm_gain: float32 [4096], replicated, may hold values from 0.5 to 1.5
- w_query: bfloat16 [4096, 4096], P(None, 'head'), may hold values from -0.09375 to 0.09375
- w_key: bfloat16 [4096, 1024], P(None, 'head'), may hold values from -0.25 to 0.25
- w_value: bfloat16 [4096, 1024], P(None, 'head'), may hold values from -0.09375 to 0.09375
- w_out: bfloat16 [4096, 4096], P('head'), may hold values from -0.09375 to 0.09375
- stored_kv: bfloat16 [8192, 2, 8, 128], P('seq', None, 'head'), may hold values from -720 to 720
- selected: int32 [768], replicated, may hold values from 0 to 8191, as said below
- prompt_order: int32 [2], replicated, may hold values from 0 to 1, each once
- store_slot: int32 [2], replicated, may hold values from 0 to 1, each once
Outputs:
- attn_out: bfloat16 [768, 4096], P('seq', 'head')
- new_kv: bfloat16 [768, 2, 8, 128], P('seq', None, 'head')
The draws below stay inside these ranges and needn't reach their ends.
Inputs may be any that keep to these rules, and one draw needn't show every extreme that they name: `selected`: each block of 1024 prompt positions holds exactly 96 distinct entries, which stand together in that block's place of the list, increasing.
All inputs are finite; a program needn't handle non-finite values.
Results may differ from the reference program's by a relative error of at most 0.02.
The reference program's roundings to bfloat16 on the way (of `normed`, `query`, `cache`, `weights` and `context`) count: a program that leaves them out, or rounds other values in their place, can miss the bound.
Values may be sent and summed in bfloat16 or wider, within the bound.
No kernel may reach another device: no remote copies, remote signals or barrier semaphores. Data moves between devices by JAX's collectives and lax.ppermute only.
A program may use at most 192 MiB of HBM per device.

```python
import jax
import jax.numpy as jnp
from jax import lax

D = 4096
HEADS = 32
KV_HEADS = 8
HEAD_DIM = 128
PASSAGE = 4096
TOK_DEV = 1024
SEL = 96
SEQ_LEN = 8192
PASSAGES = 2
ROWS = 768
N_SEQ = 8


def draw_stored_kv(key, part):
    first = jax.random.fold_in(jax.random.fold_in(key, 11), 0)
    shape = (SEQ_LEN, 2, KV_HEADS, HEAD_DIM)
    base = jnp.clip(jax.random.normal(first, shape, jnp.float32), -6.0, 6.0)
    scale = jnp.array([3.0, 1.0], jnp.float32)[None, :, None, None]
    return (base * scale).astype(jnp.bfloat16)


def draw_selected(key, part):
    blocks = SEQ_LEN // TOK_DEV
    scores = jax.random.randint(jax.random.fold_in(key, 23), (blocks, TOK_DEV), 0, 1 << 18)
    scores = scores * TOK_DEV + jnp.arange(TOK_DEV, dtype=jnp.int32)[None, :]
    _, picked = lax.top_k(scores, SEL)
    picked = jnp.sort(picked, axis=1)
    offsets = jnp.arange(blocks, dtype=jnp.int32)[:, None] * TOK_DEV
    return (picked + offsets).reshape(-1).astype(jnp.int32)


def steps_of(key, dims, cuts, least, top_value):
    def one(axis_at, parts):
        steps = jax.random.uniform(jax.random.fold_in(jax.random.fold_in(key, 6), axis_at), (parts,), jnp.float32, least / len(cuts), top_value / len(cuts))
        return jnp.repeat(jnp.exp(steps), dims[axis_at] // parts).reshape((-1,) + (1,) * (len(dims) - axis_at - 1))

    level = one(*cuts[0])
    for cut in cuts[1:]:
        level = level * one(*cut)
    return level


def normal_values(own_key, shape, width, limit, cuts=(), kind=jnp.bfloat16):
    values = width * jax.random.normal(own_key, shape, jnp.float32)
    if cuts:
        values = values * steps_of(own_key, shape, cuts, -0.22, 0.18)
    return jnp.clip(values, -limit, limit).astype(kind)


def setup_inputs(seed: int = 0) -> dict:
    key_of = jax.random.split(jax.random.key(seed), 11)
    hidden = normal_values(key_of[0], (ROWS, D), 1.0, 6.0, ((0, 8),))
    norm_gain = jnp.clip(1.0 + 0.1 * jax.random.normal(key_of[1], (D,), jnp.float32), 0.5, 1.5)
    w_query = normal_values(key_of[2], (D, HEADS * HEAD_DIM), D ** -0.5, 0.09375, ((1, 4),))
    w_key = normal_values(key_of[3], (D, KV_HEADS * HEAD_DIM), (D // 9) ** -0.5, 0.25, ((1, 4),))
    w_value = normal_values(key_of[4], (D, KV_HEADS * HEAD_DIM), D ** -0.5, 0.09375, ((1, 4),))
    w_out = normal_values(key_of[5], (HEADS * HEAD_DIM, D), (HEADS * HEAD_DIM) ** -0.5, 0.09375, ((0, 4),))
    stored_kv = draw_stored_kv(jax.random.fold_in(key_of[10], 71), 0)
    selected = draw_selected(jax.random.fold_in(key_of[10], 71), 0)
    prompt_order = jax.random.permutation(key_of[8], PASSAGES).astype(jnp.int32)
    store_slot = jax.random.permutation(key_of[9], PASSAGES).astype(jnp.int32)
    return dict(hidden=hidden, norm_gain=norm_gain, w_query=w_query, w_key=w_key, w_value=w_value, w_out=w_out, stored_kv=stored_kv, selected=selected, prompt_order=prompt_order, store_slot=store_slot)


def rope(x, pos):
    half = HEAD_DIM // 2
    freq = 500000.0 ** (-(jnp.arange(half, dtype=jnp.float32) * 2.0 / HEAD_DIM))
    angle = pos.astype(jnp.float32)[:, None] * freq[None, :]
    cosine = jnp.cos(angle)[:, None, :]
    sine = jnp.sin(angle)[:, None, :]
    first = x[..., :half]
    second = x[..., half:]
    return jnp.concatenate([first * cosine - second * sine, second * cosine + first * sine], -1)

def reference(hidden, norm_gain, w_query, w_key, w_value, w_out, stored_kv, selected, prompt_order, store_slot):
    group = HEADS // KV_HEADS
    widened = hidden.astype(jnp.float32)
    normed = (widened * lax.rsqrt(lax.optimization_barrier(jnp.mean(widened * widened, -1, keepdims=True)) + 1e-05) * norm_gain).astype(jnp.bfloat16)
    query = rope(jnp.dot(normed, w_query, preferred_element_type=jnp.float32).reshape(ROWS, HEADS, HEAD_DIM), selected).astype(jnp.bfloat16)
    fresh_key = rope(jnp.dot(normed, w_key, preferred_element_type=jnp.float32).reshape(ROWS, KV_HEADS, HEAD_DIM), selected)
    fresh_value = jnp.dot(normed, w_value, preferred_element_type=jnp.float32).reshape(ROWS, KV_HEADS, HEAD_DIM)
    new_kv = jnp.stack([fresh_key, fresh_value], 1).astype(jnp.bfloat16)
    slot_of_prompt = store_slot[prompt_order].astype(jnp.int32)
    stored = stored_kv.reshape(PASSAGES, PASSAGE, 2, KV_HEADS, HEAD_DIM)[slot_of_prompt]
    cache = stored.reshape(SEQ_LEN, 2, KV_HEADS, HEAD_DIM).at[selected].set(new_kv)
    keys = cache[:, 0]
    values = cache[:, 1]
    key_pos = jnp.arange(SEQ_LEN, dtype=jnp.int32)
    blocks = query.reshape(N_SEQ, SEL, HEADS, HEAD_DIM)
    pos_blocks = selected.reshape(N_SEQ, SEL)
    scale = 1.0 / HEAD_DIM ** 0.5

    def one_head(head):
        key_head = lax.dynamic_index_in_dim(keys, head // group, 1, False)
        value_head = lax.dynamic_index_in_dim(values, head // group, 1, False)

        def one_block(index):
            block = lax.dynamic_index_in_dim(blocks, index, 0, False)
            query_head = lax.dynamic_index_in_dim(block, head, 1, False)
            positions = lax.dynamic_index_in_dim(pos_blocks, index, 0, False)
            scores = jnp.dot(query_head, key_head.T, preferred_element_type=jnp.float32) * scale
            valid = key_pos[None, :] <= positions[:, None]
            scores = jnp.where(valid, scores, -1e+30)
            top = lax.optimization_barrier(jnp.max(scores, -1, keepdims=True))
            weights = jnp.where(valid, jnp.exp(scores - top), 0.0)
            total = lax.optimization_barrier(jnp.sum(weights, -1, keepdims=True))
            summed = jnp.dot(weights.astype(jnp.bfloat16), value_head, preferred_element_type=jnp.float32)
            return summed / total
        return lax.map(one_block, jnp.arange(N_SEQ, dtype=jnp.int32))
    context = lax.map(one_head, jnp.arange(HEADS, dtype=jnp.int32))
    context = context.transpose(1, 2, 0, 3).reshape(ROWS, HEADS * HEAD_DIM).astype(jnp.bfloat16)
    attn_out = jnp.dot(context, w_out, preferred_element_type=jnp.float32).astype(jnp.bfloat16)
    return (attn_out, new_kv)
```

```python
import functools
import math

import jax
import jax.numpy as jnp
import numpy as np
from jax import lax
from jax.experimental import pallas as pl
from jax.experimental.pallas import tpu as pltpu
from jax.sharding import PartitionSpec as P

HEADS = 32
KV_HEADS = 8
HEAD_DIM = 128
PASSAGE = 4096
GROUP = HEADS // KV_HEADS
MASKED = -1e30
LANES = 128
MIB = 1024 * 1024

bf16 = jnp.bfloat16
f32 = jnp.float32
NT = (((1,), (1,)), ((), ()))


def iota(shape, dim):
    return lax.broadcasted_iota(jnp.int32, shape, dim)


def column_of(row):
    n = row.shape[1]
    eye = iota((n, n), 0) == iota((n, n), 1)
    return jnp.sum(jnp.where(eye, row.astype(f32), 0.0), 1, keepdims=True)


def project_kernel(
    width, hidden_any, gain, selected, freq, wq_any, wk_any, wv_any, query, kv,
    hidden, normed, weights, sem,
):
    rows, feat = hidden.shape
    q_cols, k_cols, v_cols = wq_any.shape[1], wk_any.shape[1], wv_any.shape[1]
    first = pltpu.make_async_copy(hidden_any, hidden, sem.at[0])
    first.start()
    chunks = []
    for source, count, base in ((wk_any, k_cols, 0), (wq_any, q_cols, k_cols), (wv_any, v_cols, k_cols + q_cols)):
        for at in range(0, count, width):
            chunks.append((source, at, base + at))
    copies = []
    for number, (source, at, place) in enumerate(chunks):
        copy = pltpu.make_async_copy(
            source.at[:, at : at + width], weights.at[:, place : place + width], sem.at[number + 1]
        )
        copy.start()
        copies.append(copy)
    total = selected.shape[1]
    me = lax.axis_index("seq")
    mine = iota((rows, total), 1) == iota((rows, total), 0) + me * rows
    positions = jnp.sum(jnp.where(mine, selected[...].astype(f32), 0.0), 1, keepdims=True)
    angle = positions * freq[...]
    cosine = jnp.cos(angle)
    sine = jnp.sin(angle)
    sine = jnp.where(iota(sine.shape, 1) < HEAD_DIM // 2, -sine, sine)
    first.wait()
    step = 16
    for at in range(0, rows, step):
        wide = hidden[at : at + step, :].astype(f32)
        mean = jnp.sum(wide * wide, 1, keepdims=True) * (1.0 / feat)
        normed[at : at + step, :] = (wide * lax.rsqrt(mean + 1e-5) * gain[...]).astype(bf16)
    for (source, at, place), copy in zip(chunks, copies):
        copy.wait()
        out = jnp.dot(normed[...], weights[:, place : place + width], preferred_element_type=f32)
        for head in range(0, width, HEAD_DIM):
            part = out[:, head : head + HEAD_DIM]
            if source is not wv_any:
                part = part * cosine + pltpu.roll(part, HEAD_DIM // 2, 1) * sine
            part = part.astype(bf16)
            if source is wq_any:
                query[:, at + head : at + head + HEAD_DIM] = part
            else:
                col = at + head + (0 if source is wk_any else k_cols)
                kv[:, col : col + HEAD_DIM] = part


def project(hidden, gain, selected, wq, wk, wv):
    rows, feat = hidden.shape
    cols = wq.shape[1] + wk.shape[1] + wv.shape[1]
    width = math.gcd(math.gcd(wq.shape[1], wk.shape[1]), 256)
    freq = 500000.0 ** (-(np.arange(HEAD_DIM // 2, dtype=np.float32) * np.float32(2.0 / HEAD_DIM)))
    freq = jnp.asarray(np.concatenate([freq, freq])[None, :].astype(np.float32))
    vmem = pl.BlockSpec(memory_space=pltpu.VMEM)
    hbm = pl.BlockSpec(memory_space=pl.ANY)
    return pl.pallas_call(
        functools.partial(project_kernel, width),
        out_shape=(
            jax.ShapeDtypeStruct((rows, wq.shape[1]), bf16),
            jax.ShapeDtypeStruct((rows, wk.shape[1] + wv.shape[1]), bf16),
        ),
        in_specs=[hbm, vmem, vmem, vmem, hbm, hbm, hbm],
        out_specs=(vmem, vmem),
        scratch_shapes=[
            pltpu.VMEM((rows, feat), bf16),
            pltpu.VMEM((rows, feat), bf16),
            pltpu.VMEM((feat, cols), bf16),
            pltpu.SemaphoreType.DMA((1 + cols // width,)),
        ],
        compiler_params=pltpu.CompilerParams(vmem_limit_bytes=28 * MIB),
        cost_estimate=pl.CostEstimate(
            flops=2 * rows * feat * cols, bytes_accessed=2 * feat * (cols + rows), transcendentals=0
        ),
        name="project",
    )(hidden, gain.reshape(1, feat), selected.reshape(1, -1), freq, wq, wk, wv)


def block_of(index, shard, order, slot):
    per = PASSAGE // shard
    own = index // per
    place = jnp.int32(0)
    for at in range(order.shape[0]):
        place = jnp.where(slot[order[at]] == own, at, place)
    return place * per + lax.rem(index, per)


def merge_kernel(order, slot, selected, stored, kv, cache, key_pos):
    shard, cols = stored.shape
    rows = kv.shape[0]
    me = lax.axis_index("seq")
    for half in range(2):
        index = me if half == 0 else me ^ 1
        block = block_of(index, shard, order, slot)
        holes = selected[pl.ds(block, 1), :] - block * shard
        offsets = column_of(selected[pl.ds(index, 1), :] - index * shard)
        high = jnp.floor(offsets * (1.0 / 32))
        low = offsets - 32 * high
        wide = (LANES, LANES)
        given = iota((LANES, 1), 0) < rows
        sources = [
            jnp.broadcast_to(jnp.where(given, value, 0.0), wide).astype(bf16)
            for value in (jnp.ones_like(high), high, low)
        ]
        if half == 0:
            fresh = kv[...]
            if rows < LANES:
                fresh = jnp.concatenate([fresh, jnp.zeros((LANES - rows, cols), bf16)], 0)
            sources.append(fresh)
        source = jnp.concatenate(sources, 1)
        step = 128
        for at in range(0, shard, step):
            places = iota((step, LANES), 0) + at
            hit = (places == holes).astype(f32).astype(bf16)
            picked = jnp.dot(hit, source, preferred_element_type=f32)
            hole = picked[:, :LANES] > 0.5
            fresh_pos = picked[:, LANES : 2 * LANES] * 32 + picked[:, 2 * LANES : 3 * LANES]
            key_pos[half * shard + at : half * shard + at + step, :] = jnp.where(
                hole,
                fresh_pos + (index * shard).astype(f32),
                (places + block * shard).astype(f32),
            )
            if half == 0:
                for col in range(0, cols, LANES):
                    cache[at : at + step, col : col + LANES] = jnp.where(
                        hole,
                        picked[:, 3 * LANES + col : 4 * LANES + col],
                        stored[at : at + step, col : col + LANES].astype(f32),
                    ).astype(bf16)


def merge(order, slot, selected, stored, kv):
    shard, cols = stored.shape
    smem = pl.BlockSpec(memory_space=pltpu.SMEM)
    vmem = pl.BlockSpec(memory_space=pltpu.VMEM)
    return pl.pallas_call(
        merge_kernel,
        out_shape=(
            jax.ShapeDtypeStruct((shard, cols), bf16),
            jax.ShapeDtypeStruct((2 * shard, LANES), f32),
        ),
        in_specs=[smem, smem, vmem, vmem, vmem],
        out_specs=(vmem, vmem),
        compiler_params=pltpu.CompilerParams(vmem_limit_bytes=16 * MIB),
        cost_estimate=pl.CostEstimate(
            flops=4 * shard * cols * LANES, bytes_accessed=4 * shard * cols, transcendentals=0
        ),
        name="merge",
    )(order, slot, selected, stored, kv)


def attend_kernel(partners, *refs):
    count = len(partners)
    caches = refs[:2]
    key_pos, selected = refs[2:4]
    queries = refs[4 : 4 + count]
    outs = refs[4 + count : 4 + 2 * count]
    left, right, value, scores, weights, sem = refs[4 + 2 * count :]
    shard, cols = caches[0].shape
    rows = queries[0].shape[0]
    kv_heads = cols // (2 * HEAD_DIM)
    tall = GROUP * rows
    keys = 2 * shard
    scale = math.log2(math.e) / HEAD_DIM**0.5
    me = lax.axis_index("seq")
    copies = {}
    for half in range(2):
        for kind in range(2):
            for head in range(kv_heads):
                col = (kind * kv_heads + head) * HEAD_DIM
                target = (right, value)[kind]
                copy = pltpu.make_async_copy(
                    caches[half].at[:, col : col + HEAD_DIM],
                    target.at[head, half * shard : (half + 1) * shard, 0:HEAD_DIM],
                    sem.at[half, kind, head],
                )
                copy.start()
                copies[half, kind, head] = copy
    one_hot = (iota((rows, LANES), 0) == iota((rows, LANES), 1)).astype(f32).astype(bf16)
    for head in range(kv_heads):
        for member in range(GROUP):
            left[head, member * rows : (member + 1) * rows, HEAD_DIM : HEAD_DIM + LANES] = one_hot
        value[head, :, HEAD_DIM : HEAD_DIM + LANES] = jnp.ones((keys, LANES), bf16)

    def mask(at, head):
        row = selected[pl.ds(me ^ partners[at], 1), :].astype(f32)
        for place in range(0, keys, 256):
            right[head, place : place + 256, HEAD_DIM : HEAD_DIM + LANES] = jnp.where(
                key_pos[place : place + 256, :] <= row, 0.0, MASKED
            ).astype(bf16)

    def fill(at, head):
        for member in range(GROUP):
            col = (head * GROUP + member) * HEAD_DIM
            left[head, member * rows : (member + 1) * rows, 0:HEAD_DIM] = queries[at][:, col : col + HEAD_DIM]

    units = [(at, head) for at in range(count) for head in range(kv_heads)]
    step = 256
    best = {}
    for number in range(len(units) + 1):
        if number < len(units):
            at, head = units[number]
            if at == 0:
                for half in range(2):
                    copies[half, 0, head].wait()
            mask(at, head)
            fill(at, head)
        if number:
            old_at, old_head = units[number - 1]
            if old_at == 0:
                for half in range(2):
                    copies[half, 1, old_head].wait()
            top = jnp.max(best.pop(number - 1), 1, keepdims=True) * scale
        running = None
        for place in range(0, keys, step):
            if number < len(units):
                score = lax.dot_general(
                    left[head], right[head, place : place + step, :], NT, preferred_element_type=f32
                )
                scores[number % 2, :, place : place + step] = score
                for col in range(0, step, LANES):
                    part = score[:, col : col + LANES]
                    running = part if running is None else jnp.maximum(running, part)
            if number:
                slot = (number - 1) % 2
                weights[:, place : place + step] = jnp.exp2(
                    scores[slot, :, place : place + step] * scale - top
                ).astype(bf16)
        if number < len(units):
            best[number] = running
        if number:
            summed = jnp.dot(weights[...], value[old_head], preferred_element_type=f32)
            total = summed[:, HEAD_DIM : HEAD_DIM + LANES]
            context = (summed[:, :HEAD_DIM] / total).astype(bf16)
            level = top + jnp.log2(total)
            high = level.astype(bf16).astype(f32)
            middle = (level - high).astype(bf16).astype(f32)
            low = level - high - middle
            lane = iota((rows, LANES), 1)
            heads = kv_heads * GROUP
            out = outs[old_at]
            packed = jnp.zeros((rows, LANES), f32)
            for member in range(GROUP):
                which = old_head * GROUP + member
                span = slice(member * rows, (member + 1) * rows)
                out[:, which * HEAD_DIM : (which + 1) * HEAD_DIM] = context[span]
                for piece, source in enumerate((high, middle, low)):
                    packed = jnp.where(lane == piece * heads + which, source[span], packed)
            tail = slice(heads * HEAD_DIM, heads * HEAD_DIM + LANES)
            if old_head:
                packed = packed + out[:, tail].astype(f32)
            out[:, tail] = packed.astype(bf16)


def attend(partners, caches, key_pos, selected, queries):
    shard, cols = caches[0].shape
    rows, q_cols = queries[0].shape
    kv_heads = cols // (2 * HEAD_DIM)
    tall = GROUP * rows
    keys = 2 * shard
    count = len(queries)
    vmem = pl.BlockSpec(memory_space=pltpu.VMEM)
    hbm = pl.BlockSpec(memory_space=pl.ANY)
    out = pl.pallas_call(
        functools.partial(attend_kernel, partners),
        out_shape=[jax.ShapeDtypeStruct((rows, q_cols + LANES), bf16)] * count,
        in_specs=[hbm, hbm, vmem, vmem] + [vmem] * count,
        out_specs=[vmem] * count,
        scratch_shapes=[
            pltpu.VMEM((kv_heads, tall, HEAD_DIM + LANES), bf16),
            pltpu.VMEM((kv_heads, keys, HEAD_DIM + LANES), bf16),
            pltpu.VMEM((kv_heads, keys, HEAD_DIM + LANES), bf16),
            pltpu.VMEM((2, tall, keys), f32),
            pltpu.VMEM((tall, keys), bf16),
            pltpu.SemaphoreType.DMA((2, 2, kv_heads)),
        ],
        compiler_params=pltpu.CompilerParams(vmem_limit_bytes=32 * MIB),
        cost_estimate=pl.CostEstimate(
            flops=8 * count * kv_heads * tall * keys * HEAD_DIM,
            bytes_accessed=8 * shard * cols,
            transcendentals=count * kv_heads * tall * keys,
        ),
        name="attend",
    )(*caches, key_pos, selected, *queries)
    return list(out)


def finish_kernel(count, size, *refs):
    parts = refs[:count]
    w_any = refs[count]
    outs = refs[count + 1 : count + 1 + size]
    context, weights, sem = refs[count + 1 + size :]
    rows, feat = context.shape
    heads = feat // HEAD_DIM
    width = w_any.shape[1] // size
    me = lax.axis_index("head")
    copies = []
    for turn in range(size):
        target = lax.rem(me + turn, size) if size & (size - 1) else me ^ turn
        copy = pltpu.make_async_copy(
            w_any.at[:, pl.ds(pl.multiple_of(target * width, width), width)],
            weights.at[turn],
            sem.at[turn],
        )
        copies.append(copy)
    for copy in reversed(copies):
        copy.start()
    tails = [part[:, feat : feat + LANES].astype(f32) for part in parts]
    for head in range(heads):
        levels = []
        for tail in tails:
            pieces = [tail[:, piece * heads + head : piece * heads + head + 1] for piece in range(3)]
            levels.append(pieces[0] + pieces[1] + pieces[2])
        top = functools.reduce(jnp.maximum, levels)
        shares = [jnp.exp2(level - top) for level in levels]
        whole = functools.reduce(jnp.add, shares)
        span = slice(head * HEAD_DIM, (head + 1) * HEAD_DIM)
        mixed = functools.reduce(
            jnp.add, [(share / whole) * part[:, span].astype(f32) for share, part in zip(shares, parts)]
        )
        context[:, span] = mixed.astype(bf16)
    for turn in reversed(range(size)):
        copies[turn].wait()
        step = 256 if width % 256 == 0 else width
        for at in range(0, width, step):
            outs[turn][:, at : at + step] = jnp.dot(
                context[...], weights[turn, :, at : at + step], preferred_element_type=f32
            ).astype(outs[turn].dtype)


def finish(parts, w_out, size):
    rows = parts[0].shape[0]
    feat, cols = w_out.shape
    width = cols // size
    vmem = pl.BlockSpec(memory_space=pltpu.VMEM)
    hbm = pl.BlockSpec(memory_space=pl.ANY)
    return pl.pallas_call(
        functools.partial(finish_kernel, len(parts), size),
        out_shape=[jax.ShapeDtypeStruct((rows, width), f32 if turn == 0 else bf16) for turn in range(size)],
        in_specs=[vmem] * len(parts) + [hbm],
        out_specs=[vmem] * size,
        scratch_shapes=[
            pltpu.VMEM((rows, feat), bf16),
            pltpu.VMEM((size, feat, width), bf16),
            pltpu.SemaphoreType.DMA((size,)),
        ],
        compiler_params=pltpu.CompilerParams(vmem_limit_bytes=24 * MIB),
        cost_estimate=pl.CostEstimate(
            flops=2 * rows * feat * cols, bytes_accessed=2 * feat * cols, transcendentals=0
        ),
        name="finish",
    )(*parts, w_out)


def swap(value, axis, turn, size):
    return lax.ppermute(value, axis, [(at, at ^ turn) for at in range(size)])


def body(
    hidden, norm_gain, w_query, w_key, w_value, w_out, stored_kv, selected, prompt_order, store_slot
):
    seq_count = lax.axis_size("seq")
    head_count = lax.axis_size("head")
    rows = hidden.shape[0]
    shard, _, local_kv, _ = stored_kv.shape
    stored = stored_kv.reshape(shard, -1)
    table = jnp.pad(selected.reshape(seq_count, rows), ((0, 0), (0, LANES - rows)), constant_values=-1)
    query, kv = project(hidden, norm_gain, selected, w_query, w_key, w_value)
    turns = list(range(2, seq_count, 2))
    far_first = sorted(turns, key=lambda turn: (-bin(turn).count("1"), turn))
    queries = {turn: swap(query, "seq", turn, seq_count) for turn in far_first}
    queries[0] = query
    cache, key_pos = merge(prompt_order, store_slot, table, stored, kv)
    other = swap(cache, "seq", 1, seq_count)
    caches = (cache, other)
    parts = attend((0,), caches, key_pos, table, [query])
    near_first = far_first[::-1]
    for at in range(0, len(near_first), 2):
        some = near_first[at : at + 2]
        done = attend(tuple(some), caches, key_pos, table, [queries[turn] for turn in some])
        parts += [swap(part, "seq", turn, seq_count) for turn, part in zip(some, done)]
    blocks = finish(parts, w_out, head_count)
    total = blocks[0]
    arrived = [swap(blocks[turn], "head", turn, head_count) for turn in range(1, head_count)]
    for block in arrived:
        total = total + block.astype(f32)
    new_kv = kv.reshape(rows, 2, local_kv, HEAD_DIM)
    return (total.astype(bf16), new_kv)


def solution(mesh):
    in_specs = (
        P("seq", None),
        P(),
        P(None, "head"),
        P(None, "head"),
        P(None, "head"),
        P("head", None),
        P("seq", None, "head", None),
        P(),
        P(),
        P(),
    )
    out_specs = (P("seq", "head"), P("seq", None, "head", None))
    return jax.shard_map(body, mesh=mesh, in_specs=in_specs, out_specs=out_specs, check_vma=False)
```

```python
import functools
import math

import jax
import jax.numpy as jnp
import numpy as np
from jax import lax
from jax.experimental import pallas as pl
from jax.experimental.pallas import tpu as pltpu
from jax.sharding import PartitionSpec as P

HEADS = 32
KV_HEADS = 8
HEAD_DIM = 128
PASSAGE = 4096
GROUP = HEADS // KV_HEADS
MASKED = -1e30
LANES = 128
MIB = 1024 * 1024

bf16 = jnp.bfloat16
f32 = jnp.float32
NT = (((1,), (1,)), ((), ()))


def iota(shape, dim):
    return lax.broadcasted_iota(jnp.int32, shape, dim)


def column_of(row):
    n = row.shape[1]
    eye = iota((n, n), 0) == iota((n, n), 1)
    return jnp.sum(jnp.where(eye, row.astype(f32), 0.0), 1, keepdims=True)


def project_kernel(
    width, hidden_any, gain, selected, freq, wq_any, wk_any, wv_any, query, kv, table,
    hidden, normed, weights, sem,
):
    rows, feat = hidden.shape
    q_cols, k_cols, v_cols = wq_any.shape[1], wk_any.shape[1], wv_any.shape[1]
    first = pltpu.make_async_copy(hidden_any, hidden, sem.at[0])
    first.start()
    chunks = []
    for source, count, base in ((wk_any, k_cols, 0), (wq_any, q_cols, k_cols), (wv_any, v_cols, k_cols + q_cols)):
        for at in range(0, count, width):
            chunks.append((source, at, base + at))
    copies = []
    for number, (source, at, place) in enumerate(chunks):
        copy = pltpu.make_async_copy(
            source.at[:, at : at + width], weights.at[:, place : place + width], sem.at[number + 1]
        )
        copy.start()
        copies.append(copy)
    total = selected.shape[0]
    me = lax.axis_index("seq")
    mine = iota((rows, total), 1) == iota((rows, total), 0) + me * rows
    listed = selected[...].reshape(1, total)
    positions = jnp.sum(jnp.where(mine, listed.astype(f32), 0.0), 1, keepdims=True)
    table[...] = jnp.full(table.shape, -1, jnp.int32)
    for at in range(total // rows):
        table[at : at + 1, 0:rows] = listed[:, at * rows : (at + 1) * rows]
    angle = positions * freq[...]
    cosine = jnp.cos(angle)
    sine = jnp.sin(angle)
    sine = jnp.where(iota(sine.shape, 1) < HEAD_DIM // 2, -sine, sine)
    first.wait()
    step = 16
    for at in range(0, rows, step):
        wide = hidden[at : at + step, :].astype(f32)
        mean = jnp.sum(wide * wide, 1, keepdims=True) * (1.0 / feat)
        normed[at : at + step, :] = (wide * lax.rsqrt(mean + 1e-5) * gain[...]).astype(bf16)
    for (source, at, place), copy in zip(chunks, copies):
        copy.wait()
        out = jnp.dot(normed[...], weights[:, place : place + width], preferred_element_type=f32)
        for head in range(0, width, HEAD_DIM):
            part = out[:, head : head + HEAD_DIM]
            if source is not wv_any:
                part = part * cosine + pltpu.roll(part, HEAD_DIM // 2, 1) * sine
            part = part.astype(bf16)
            if source is wq_any:
                query[:, at + head : at + head + HEAD_DIM] = part
            else:
                col = at + head + (0 if source is wk_any else k_cols)
                kv[:, col : col + HEAD_DIM] = part


def project(hidden, gain, selected, wq, wk, wv):
    rows, feat = hidden.shape
    cols = wq.shape[1] + wk.shape[1] + wv.shape[1]
    width = math.gcd(math.gcd(wq.shape[1], wk.shape[1]), 256)
    freq = 500000.0 ** (-(np.arange(HEAD_DIM // 2, dtype=np.float32) * np.float32(2.0 / HEAD_DIM)))
    freq = jnp.asarray(np.concatenate([freq, freq])[None, :].astype(np.float32))
    vmem = pl.BlockSpec(memory_space=pltpu.VMEM)
    hbm = pl.BlockSpec(memory_space=pl.ANY)
    return pl.pallas_call(
        functools.partial(project_kernel, width),
        out_shape=(
            jax.ShapeDtypeStruct((rows, wq.shape[1]), bf16),
            jax.ShapeDtypeStruct((rows, wk.shape[1] + wv.shape[1]), bf16),
            jax.ShapeDtypeStruct((selected.shape[0] // rows, LANES), jnp.int32),
        ),
        in_specs=[hbm, vmem, vmem, vmem, hbm, hbm, hbm],
        out_specs=(vmem, vmem, vmem),
        scratch_shapes=[
            pltpu.VMEM((rows, feat), bf16),
            pltpu.VMEM((rows, feat), bf16),
            pltpu.VMEM((feat, cols), bf16),
            pltpu.SemaphoreType.DMA((1 + cols // width,)),
        ],
        compiler_params=pltpu.CompilerParams(vmem_limit_bytes=56 * MIB),
        cost_estimate=pl.CostEstimate(
            flops=2 * rows * feat * cols, bytes_accessed=2 * feat * (cols + rows), transcendentals=0
        ),
        name="project",
    )(hidden, gain.reshape(1, feat), selected, freq, wq, wk, wv)


def block_of(index, shard, order, slot):
    per = PASSAGE // shard
    own = index // per
    place = jnp.int32(0)
    for at in range(order.shape[0]):
        place = jnp.where(slot[order[at]] == own, at, place)
    return place * per + lax.rem(index, per)


def merge_kernel(order, slot, selected, stored, kv, cache, key_pos):
    shard, cols = cache.shape
    kinds = cols // LANES
    rows = kv.shape[0]
    step = 128
    me = lax.axis_index("seq")
    spread = iota((step, kinds * step), 1) - kinds * iota((step, kinds * step), 0)
    takes = [(spread == kind).astype(f32).astype(bf16) for kind in range(kinds)]
    for half in range(2):
        index = me if half == 0 else me ^ 1
        block = block_of(index, shard, order, slot)
        holes = selected[pl.ds(block, 1), :] - block * shard
        offsets = column_of(selected[pl.ds(index, 1), :] - index * shard)
        high = jnp.floor(offsets * (1.0 / 32))
        low = offsets - 32 * high
        wide = (LANES, LANES)
        given = iota((LANES, 1), 0) < rows
        sources = [
            jnp.broadcast_to(jnp.where(given, value, 0.0), wide).astype(bf16)
            for value in (jnp.ones_like(high), high, low)
        ]
        if half == 0:
            fresh = kv[...]
            if rows < LANES:
                fresh = jnp.concatenate([fresh, jnp.zeros((LANES - rows, cols), bf16)], 0)
            sources.append(fresh)
        source = jnp.concatenate(sources, 1)
        for at in range(0, shard, step):
            places = iota((step, LANES), 0) + at
            hit = (places == holes).astype(f32).astype(bf16)
            picked = jnp.dot(hit, source, preferred_element_type=f32)
            hole = picked[:, :LANES] > 0.5
            fresh_pos = picked[:, LANES : 2 * LANES] * 32 + picked[:, 2 * LANES : 3 * LANES]
            key_pos[half * shard + at : half * shard + at + step, :] = jnp.where(
                hole,
                fresh_pos + (index * shard).astype(f32),
                (places + block * shard).astype(f32),
            )
            if half == 0:
                mixed = stored[at * kinds : (at + step) * kinds, :]
                for kind in range(kinds):
                    col = kind * LANES
                    cache[at : at + step, col : col + LANES] = jnp.where(
                        hole,
                        picked[:, 3 * LANES + col : 4 * LANES + col],
                        jnp.dot(takes[kind], mixed, preferred_element_type=f32),
                    ).astype(bf16)


def merge(order, slot, selected, stored, kv):
    cols = kv.shape[1]
    shard = stored.shape[0] * LANES // cols
    smem = pl.BlockSpec(memory_space=pltpu.SMEM)
    vmem = pl.BlockSpec(memory_space=pltpu.VMEM)
    return pl.pallas_call(
        merge_kernel,
        out_shape=(
            jax.ShapeDtypeStruct((shard, cols), bf16),
            jax.ShapeDtypeStruct((2 * shard, LANES), f32),
        ),
        in_specs=[smem, smem, vmem, vmem, vmem],
        out_specs=(vmem, vmem),
        compiler_params=pltpu.CompilerParams(vmem_limit_bytes=16 * MIB),
        cost_estimate=pl.CostEstimate(flops=1000, bytes_accessed=1000, transcendentals=0),
        name="merge",
    )(order, slot, selected, stored, kv)


def attend_kernel(partners, *refs):
    count = len(partners)
    caches = refs[:2]
    key_pos, selected = refs[2:4]
    queries = refs[4 : 4 + count]
    outs = refs[4 + count : 4 + 2 * count]
    left, right, value, scores, weights, sem = refs[4 + 2 * count :]
    shard, cols = caches[0].shape
    rows = queries[0].shape[0]
    kv_heads = cols // (2 * HEAD_DIM)
    tall = GROUP * rows
    keys = 2 * shard
    scale = math.log2(math.e) / HEAD_DIM**0.5
    me = lax.axis_index("seq")
    copies = {}
    for half in range(2):
        for kind in range(2):
            for head in range(kv_heads):
                col = (kind * kv_heads + head) * HEAD_DIM
                target = (right, value)[kind]
                copy = pltpu.make_async_copy(
                    caches[half].at[:, col : col + HEAD_DIM],
                    target.at[head, half * shard : (half + 1) * shard, 0:HEAD_DIM],
                    sem.at[half, kind, head],
                )
                copy.start()
                copies[half, kind, head] = copy
    one_hot = (iota((rows, LANES), 0) == iota((rows, LANES), 1)).astype(f32).astype(bf16)
    for head in range(kv_heads):
        for member in range(GROUP):
            left[head, member * rows : (member + 1) * rows, HEAD_DIM : HEAD_DIM + LANES] = one_hot
        value[head, :, HEAD_DIM : HEAD_DIM + LANES] = jnp.ones((keys, LANES), bf16)

    def mask(at, head):
        row = selected[pl.ds(me ^ partners[at], 1), :].astype(f32)
        for place in range(0, keys, 256):
            right[head, place : place + 256, HEAD_DIM : HEAD_DIM + LANES] = jnp.where(
                key_pos[place : place + 256, :] <= row, 0.0, MASKED
            ).astype(bf16)

    def fill(at, head):
        for member in range(GROUP):
            col = (head * GROUP + member) * HEAD_DIM
            left[head, member * rows : (member + 1) * rows, 0:HEAD_DIM] = queries[at][:, col : col + HEAD_DIM]

    units = [(at, head) for at in range(count) for head in range(kv_heads)]
    step = 256
    best = {}
    for number in range(len(units) + 1):
        if number < len(units):
            at, head = units[number]
            if at == 0:
                for half in range(2):
                    copies[half, 0, head].wait()
            mask(at, head)
            fill(at, head)
        if number:
            old_at, old_head = units[number - 1]
            if old_at == 0:
                for half in range(2):
                    copies[half, 1, old_head].wait()
            top = jnp.max(best.pop(number - 1), 1, keepdims=True) * scale
        running = None
        for place in range(0, keys, step):
            if number < len(units):
                score = lax.dot_general(
                    left[head], right[head, place : place + step, :], NT, preferred_element_type=f32
                )
                scores[number % 2, :, place : place + step] = score
                for col in range(0, step, LANES):
                    part = score[:, col : col + LANES]
                    running = part if running is None else jnp.maximum(running, part)
            if number:
                slot = (number - 1) % 2
                weights[:, place : place + step] = jnp.exp2(
                    scores[slot, :, place : place + step] * scale - top
                ).astype(bf16)
        if number < len(units):
            best[number] = running
        if number:
            summed = jnp.dot(weights[...], value[old_head], preferred_element_type=f32)
            total = summed[:, HEAD_DIM : HEAD_DIM + LANES]
            context = (summed[:, :HEAD_DIM] / total).astype(bf16)
            level = top + jnp.log2(total)
            high = level.astype(bf16).astype(f32)
            middle = (level - high).astype(bf16).astype(f32)
            low = level - high - middle
            lane = iota((rows, LANES), 1)
            heads = kv_heads * GROUP
            out = outs[old_at]
            packed = jnp.zeros((rows, LANES), f32)
            for member in range(GROUP):
                which = old_head * GROUP + member
                span = slice(member * rows, (member + 1) * rows)
                out[:, which * HEAD_DIM : (which + 1) * HEAD_DIM] = context[span]
                for piece, source in enumerate((high, middle, low)):
                    packed = jnp.where(lane == piece * heads + which, source[span], packed)
            tail = slice(heads * HEAD_DIM, heads * HEAD_DIM + LANES)
            if old_head:
                packed = packed + out[:, tail].astype(f32)
            out[:, tail] = packed.astype(bf16)


def attend(partners, caches, key_pos, selected, queries):
    shard, cols = caches[0].shape
    rows, q_cols = queries[0].shape
    kv_heads = cols // (2 * HEAD_DIM)
    tall = GROUP * rows
    keys = 2 * shard
    count = len(queries)
    vmem = pl.BlockSpec(memory_space=pltpu.VMEM)
    hbm = pl.BlockSpec(memory_space=pl.ANY)
    out = pl.pallas_call(
        functools.partial(attend_kernel, partners),
        out_shape=[jax.ShapeDtypeStruct((rows, q_cols + LANES), bf16)] * count,
        in_specs=[hbm, hbm, vmem, vmem] + [vmem] * count,
        out_specs=[vmem] * count,
        scratch_shapes=[
            pltpu.VMEM((kv_heads, tall, HEAD_DIM + LANES), bf16),
            pltpu.VMEM((kv_heads, keys, HEAD_DIM + LANES), bf16),
            pltpu.VMEM((kv_heads, keys, HEAD_DIM + LANES), bf16),
            pltpu.VMEM((2, tall, keys), f32),
            pltpu.VMEM((tall, keys), bf16),
            pltpu.SemaphoreType.DMA((2, 2, kv_heads)),
        ],
        compiler_params=pltpu.CompilerParams(vmem_limit_bytes=32 * MIB),
        cost_estimate=pl.CostEstimate(
            flops=8 * count * kv_heads * tall * keys * HEAD_DIM,
            bytes_accessed=8 * shard * cols,
            transcendentals=count * kv_heads * tall * keys,
        ),
        name="attend",
    )(*caches, key_pos, selected, *queries)
    return list(out)


def finish_kernel(count, size, *refs):
    parts = refs[:count]
    weights = refs[count]
    outs = refs[count + 1 : count + 1 + size]
    (context,) = refs[count + 1 + size :]
    rows, feat = context.shape
    heads = feat // HEAD_DIM
    width = weights.shape[1] // size
    me = lax.axis_index("head")
    tails = [part[:, feat : feat + LANES].astype(f32) for part in parts]
    for head in range(heads):
        levels = []
        for tail in tails:
            pieces = [tail[:, piece * heads + head : piece * heads + head + 1] for piece in range(3)]
            levels.append(pieces[0] + pieces[1] + pieces[2])
        top = functools.reduce(jnp.maximum, levels)
        shares = [jnp.exp2(level - top) for level in levels]
        whole = functools.reduce(jnp.add, shares)
        span = slice(head * HEAD_DIM, (head + 1) * HEAD_DIM)
        mixed = functools.reduce(
            jnp.add, [(share / whole) * part[:, span].astype(f32) for share, part in zip(shares, parts)]
        )
        context[:, span] = mixed.astype(bf16)
    for turn in range(size):
        start = (me ^ turn) * width
        step = 256 if width % 256 == 0 else width
        for at in range(0, width, step):
            part = weights[:, pl.ds(pl.multiple_of(start + at, step), step)]
            outs[turn][:, at : at + step] = jnp.dot(
                context[...], part, preferred_element_type=f32
            ).astype(outs[turn].dtype)


def finish(parts, w_out, size):
    rows = parts[0].shape[0]
    feat, cols = w_out.shape
    width = cols // size
    vmem = pl.BlockSpec(memory_space=pltpu.VMEM)
    return pl.pallas_call(
        functools.partial(finish_kernel, len(parts), size),
        out_shape=[jax.ShapeDtypeStruct((rows, width), f32 if turn == 0 else bf16) for turn in range(size)],
        in_specs=[vmem] * (len(parts) + 1),
        out_specs=[vmem] * size,
        scratch_shapes=[
            pltpu.VMEM((rows, feat), bf16),
        ],
        compiler_params=pltpu.CompilerParams(vmem_limit_bytes=24 * MIB),
        cost_estimate=pl.CostEstimate(
            flops=2 * rows * feat * cols, bytes_accessed=2 * feat * cols, transcendentals=0
        ),
        name="finish",
    )(*parts, w_out)


def swap(value, axis, turn, size):
    return lax.ppermute(value, axis, [(at, at ^ turn) for at in range(size)])


def body(
    hidden, norm_gain, w_query, w_key, w_value, w_out, stored_kv, selected, prompt_order, store_slot
):
    seq_count = lax.axis_size("seq")
    head_count = lax.axis_size("head")
    rows = hidden.shape[0]
    shard, _, local_kv, _ = stored_kv.shape
    stored = stored_kv.reshape(-1, HEAD_DIM)
    query, kv, table = project(hidden, norm_gain, selected, w_query, w_key, w_value)
    turns = list(range(2, seq_count, 2))
    far_first = sorted(turns, key=lambda turn: (-bin(turn).count("1"), turn))
    queries = {turn: swap(query, "seq", turn, seq_count) for turn in far_first}
    cache, key_pos = merge(prompt_order, store_slot, table, stored, kv)
    other = swap(cache, "seq", 1, seq_count)
    caches = (cache, other)
    parts = attend((0,), caches, key_pos, table, [query])
    near_first = far_first[::-1]
    for at in range(0, len(near_first), 2):
        some = near_first[at : at + 2]
        done = attend(tuple(some), caches, key_pos, table, [queries[turn] for turn in some])
        parts += [swap(part, "seq", turn, seq_count) for turn, part in zip(some, done)]
    blocks = finish(parts, w_out, head_count)
    total = blocks[0]
    arrived = [swap(blocks[turn], "head", turn, head_count) for turn in range(1, head_count)]
    for block in arrived:
        total = total + block.astype(f32)
    new_kv = kv.reshape(rows, 2, local_kv, HEAD_DIM)
    return (total.astype(bf16), new_kv)


def solution(mesh):
    in_specs = (
        P("seq", None),
        P(),
        P(None, "head"),
        P(None, "head"),
        P(None, "head"),
        P("head", None),
        P("seq", None, "head", None),
        P(),
        P(),
        P(),
    )
    out_specs = (P("seq", "head"), P("seq", None, "head", None))
    return jax.shard_map(body, mesh=mesh, in_specs=in_specs, out_specs=out_specs, check_vma=False)
```

```python
import functools
import math

import jax
import jax.numpy as jnp
import numpy as np
from jax import lax
from jax.experimental import pallas as pl
from jax.experimental.pallas import tpu as pltpu
from jax.sharding import PartitionSpec as P

HEADS = 32
KV_HEADS = 8
HEAD_DIM = 128
PASSAGE = 4096
GROUP = HEADS // KV_HEADS
MASKED = -1e30
LANES = 128
MIB = 1024 * 1024

bf16 = jnp.bfloat16
f32 = jnp.float32
NT = (((1,), (1,)), ((), ()))


def iota(shape, dim):
    return lax.broadcasted_iota(jnp.int32, shape, dim)


def column_of(row):
    n = row.shape[1]
    eye = iota((n, n), 0) == iota((n, n), 1)
    return jnp.sum(jnp.where(eye, row.astype(f32), 0.0), 1, keepdims=True)


def project_kernel(
    width, hidden_any, gain, selected, freq, wq_any, wk_any, wv_any, query, kv, table,
    hidden, normed, weights, sem,
):
    rows, feat = hidden.shape
    q_cols, k_cols, v_cols = wq_any.shape[1], wk_any.shape[1], wv_any.shape[1]
    first = pltpu.make_async_copy(hidden_any, hidden, sem.at[0])
    first.start()
    chunks = []
    for source, count, base in ((wk_any, k_cols, 0), (wq_any, q_cols, k_cols), (wv_any, v_cols, k_cols + q_cols)):
        for at in range(0, count, width):
            chunks.append((source, at, base + at))
    copies = []
    for number, (source, at, place) in enumerate(chunks):
        copy = pltpu.make_async_copy(
            source.at[:, at : at + width], weights.at[:, place : place + width], sem.at[number + 1]
        )
        copy.start()
        copies.append(copy)
    total = selected.shape[0]
    me = lax.axis_index("seq")
    mine = iota((rows, total), 1) == iota((rows, total), 0) + me * rows
    listed = selected[...].reshape(1, total)
    positions = jnp.sum(jnp.where(mine, listed.astype(f32), 0.0), 1, keepdims=True)
    table[...] = jnp.full(table.shape, -1, jnp.int32)
    for at in range(total // rows):
        table[at : at + 1, 0:rows] = listed[:, at * rows : (at + 1) * rows]
    angle = positions * freq[...]
    cosine = jnp.cos(angle)
    sine = jnp.sin(angle)
    sine = jnp.where(iota(sine.shape, 1) < HEAD_DIM // 2, -sine, sine)
    first.wait()
    step = 16
    for at in range(0, rows, step):
        wide = hidden[at : at + step, :].astype(f32)
        mean = jnp.sum(wide * wide, 1, keepdims=True) * (1.0 / feat)
        normed[at : at + step, :] = (wide * lax.rsqrt(mean + 1e-5) * gain[...]).astype(bf16)
    for (source, at, place), copy in zip(chunks, copies):
        copy.wait()
        out = jnp.dot(normed[...], weights[:, place : place + width], preferred_element_type=f32)
        for head in range(0, width, HEAD_DIM):
            part = out[:, head : head + HEAD_DIM]
            if source is not wv_any:
                part = part * cosine + pltpu.roll(part, HEAD_DIM // 2, 1) * sine
            part = part.astype(bf16)
            if source is wq_any:
                query[:, at + head : at + head + HEAD_DIM] = part
            else:
                col = at + head + (0 if source is wk_any else k_cols)
                kv[:, col : col + HEAD_DIM] = part


def project(hidden, gain, selected, wq, wk, wv):
    rows, feat = hidden.shape
    cols = wq.shape[1] + wk.shape[1] + wv.shape[1]
    width = math.gcd(math.gcd(wq.shape[1], wk.shape[1]), 256)
    freq = 500000.0 ** (-(np.arange(HEAD_DIM // 2, dtype=np.float32) * np.float32(2.0 / HEAD_DIM)))
    freq = jnp.asarray(np.concatenate([freq, freq])[None, :].astype(np.float32))
    vmem = pl.BlockSpec(memory_space=pltpu.VMEM)
    hbm = pl.BlockSpec(memory_space=pl.ANY)
    return pl.pallas_call(
        functools.partial(project_kernel, width),
        out_shape=(
            jax.ShapeDtypeStruct((rows, wq.shape[1]), bf16),
            jax.ShapeDtypeStruct((rows, wk.shape[1] + wv.shape[1]), bf16),
            jax.ShapeDtypeStruct((selected.shape[0] // rows, LANES), jnp.int32),
        ),
        in_specs=[hbm, vmem, vmem, vmem, hbm, hbm, hbm],
        out_specs=(vmem, vmem, vmem),
        scratch_shapes=[
            pltpu.VMEM((rows, feat), bf16),
            pltpu.VMEM((rows, feat), bf16),
            pltpu.VMEM((feat, cols), bf16),
            pltpu.SemaphoreType.DMA((1 + cols // width,)),
        ],
        compiler_params=pltpu.CompilerParams(vmem_limit_bytes=52 * MIB),
        cost_estimate=pl.CostEstimate(
            flops=2 * rows * feat * cols, bytes_accessed=2 * feat * (cols + rows), transcendentals=0
        ),
        name="project",
    )(hidden, gain.reshape(1, feat), selected, freq, wq, wk, wv)


def block_of(index, shard, order, slot):
    per = PASSAGE // shard
    own = index // per
    place = jnp.int32(0)
    for at in range(order.shape[0]):
        place = jnp.where(slot[order[at]] == own, at, place)
    return place * per + lax.rem(index, per)


def merge_kernel(order, slot, selected, stored, stored_other, kv, kv_other, cache, key_pos, wide):
    _, shard, cols = cache.shape
    kinds = cols // LANES
    rows = kv.shape[0]
    step = 128
    me = lax.axis_index("seq")
    for half in range(2):
        index = me ^ half
        block = block_of(index, shard, order, slot)
        holes = selected[pl.ds(block, 1), :] - block * shard
        offsets = column_of(selected[pl.ds(index, 1), :] - index * shard)
        high = jnp.floor(offsets * (1.0 / 32))
        low = offsets - 32 * high
        given = iota((LANES, 1), 0) < rows
        sources = [
            jnp.broadcast_to(jnp.where(given, value, 0.0), (LANES, LANES)).astype(bf16)
            for value in (high, low + 1)
        ]
        fresh = (kv, kv_other)[half][...]
        if rows < LANES:
            fresh = jnp.concatenate([fresh, jnp.zeros((LANES - rows, cols), bf16)], 0)
        source = jnp.concatenate(sources + [fresh], 1)
        for at in range(0, shard, step):
            places = iota((step, LANES), 0) + at
            hit = (places == holes).astype(f32).astype(bf16)
            picked = jnp.dot(hit, source, preferred_element_type=f32)
            mark = picked[:, LANES : 2 * LANES]
            hole = mark > 0.5
            key_pos[half * shard + at : half * shard + at + step, :] = jnp.where(
                hole,
                picked[:, :LANES] * 32 + (mark - 1) + (index * shard).astype(f32),
                (places + block * shard).astype(f32),
            )
            slot_at = (at // step) % 2
            wide[slot_at] = (stored, stored_other)[half][at * kinds : (at + step) * kinds, :].astype(f32)
            for kind in range(kinds):
                col = kind * LANES
                cache[half, at : at + step, col : col + LANES] = jnp.where(
                    hole,
                    picked[:, 2 * LANES + col : 3 * LANES + col],
                    wide[slot_at, pl.ds(kind, step, stride=kinds), :],
                ).astype(bf16)


def merge(order, slot, selected, stored, stored_other, kv, kv_other):
    cols = kv.shape[1]
    shard = stored.shape[0] * LANES // cols
    smem = pl.BlockSpec(memory_space=pltpu.SMEM)
    vmem = pl.BlockSpec(memory_space=pltpu.VMEM)
    return pl.pallas_call(
        merge_kernel,
        out_shape=(
            jax.ShapeDtypeStruct((2, shard, cols), bf16),
            jax.ShapeDtypeStruct((2 * shard, LANES), f32),
        ),
        in_specs=[smem, smem] + [vmem] * 5,
        out_specs=(vmem, vmem),
        scratch_shapes=[pltpu.VMEM((2, 128 * cols // LANES, LANES), f32)],
        compiler_params=pltpu.CompilerParams(vmem_limit_bytes=16 * MIB),
        cost_estimate=pl.CostEstimate(flops=1000, bytes_accessed=1000, transcendentals=0),
        name="merge",
    )(order, slot, selected, stored, stored_other, kv, kv_other)


def attend_kernel(partners, *refs):
    count = len(partners)
    cache, key_pos, selected = refs[:3]
    queries = refs[3 : 3 + count]
    outs = refs[3 + count : 3 + 2 * count]
    scores, weights, masks = refs[3 + 2 * count :]
    _, shard, cols = cache.shape
    rows = queries[0].shape[0]
    kv_heads = cols // (2 * HEAD_DIM)
    heads = kv_heads * GROUP
    keys = 2 * shard
    step = 256
    scale = math.log2(math.e) / HEAD_DIM**0.5
    me = lax.axis_index("seq")
    one_hot = (iota((rows, LANES), 0) == iota((rows, LANES), 1)).astype(f32).astype(bf16)
    ones = jnp.ones((keys, LANES), bf16)

    def mask(at):
        row = selected[pl.ds(me ^ partners[at], 1), :].astype(f32)
        for place in range(0, keys, step):
            masks[at % 2, place : place + step, :] = jnp.where(
                key_pos[place : place + step, :] <= row, 0.0, MASKED
            ).astype(bf16)

    def left(at, head):
        parts = []
        for member in range(GROUP):
            col = (head * GROUP + member) * HEAD_DIM
            parts.append(jnp.concatenate([queries[at][:, col : col + HEAD_DIM], one_hot], 1))
        return jnp.concatenate(parts, 0)

    def cached(place, size, kind, head):
        col = (kind * kv_heads + head) * HEAD_DIM
        return cache[place // shard, place % shard : place % shard + size, col : col + HEAD_DIM]

    units = [(at, head) for at in range(count) for head in range(kv_heads)]
    best = {}
    for number in range(len(units) + 1):
        if number < len(units):
            at, head = units[number]
            if head == 0:
                mask(at)
            stream = left(at, head)
        if number:
            old_at, old_head = units[number - 1]
            top = jnp.max(best.pop(number - 1), 1, keepdims=True) * scale
        running = None
        for place in range(0, keys, step):
            if number < len(units):
                right = jnp.concatenate(
                    [cached(place, step, 0, head), masks[at % 2, place : place + step, :]], 1
                )
                score = lax.dot_general(stream, right, NT, preferred_element_type=f32)
                scores[number % 2, :, place : place + step] = score
                for col in range(0, step, LANES):
                    part = score[:, col : col + LANES]
                    running = part if running is None else jnp.maximum(running, part)
            if number:
                slot = (number - 1) % 2
                weights[:, place : place + step] = jnp.exp2(
                    scores[slot, :, place : place + step] * scale - top
                ).astype(bf16)
        if number < len(units):
            best[number] = running
        if number:
            value = jnp.concatenate([cached(half * shard, shard, 1, old_head) for half in range(2)], 0)
            summed = jnp.dot(
                weights[...], jnp.concatenate([value, ones], 1), preferred_element_type=f32
            )
            total = summed[:, HEAD_DIM : HEAD_DIM + LANES]
            context = (summed[:, :HEAD_DIM] / total).astype(bf16)
            level = top + jnp.log2(total)
            high = level.astype(bf16).astype(f32)
            middle = (level - high).astype(bf16).astype(f32)
            low = level - high - middle
            lane = iota((rows, LANES), 1)
            out = outs[old_at]
            packed = jnp.zeros((rows, LANES), f32)
            for member in range(GROUP):
                which = old_head * GROUP + member
                span = slice(member * rows, (member + 1) * rows)
                out[:, which * HEAD_DIM : (which + 1) * HEAD_DIM] = context[span]
                for piece, source in enumerate((high, middle, low)):
                    packed = jnp.where(lane == piece * heads + which, source[span], packed)
            tail = slice(heads * HEAD_DIM, heads * HEAD_DIM + LANES)
            if old_head:
                packed = packed + out[:, tail].astype(f32)
            out[:, tail] = packed.astype(bf16)


def attend(partners, cache, key_pos, selected, queries):
    _, shard, cols = cache.shape
    rows, q_cols = queries[0].shape
    kv_heads = cols // (2 * HEAD_DIM)
    tall = GROUP * rows
    keys = 2 * shard
    count = len(queries)
    vmem = pl.BlockSpec(memory_space=pltpu.VMEM)
    out = pl.pallas_call(
        functools.partial(attend_kernel, partners),
        out_shape=[jax.ShapeDtypeStruct((rows, q_cols + LANES), bf16)] * count,
        in_specs=[vmem] * (3 + count),
        out_specs=[vmem] * count,
        scratch_shapes=[
            pltpu.VMEM((2, tall, keys), f32),
            pltpu.VMEM((tall, keys), bf16),
            pltpu.VMEM((2, keys, LANES), bf16),
        ],
        compiler_params=pltpu.CompilerParams(vmem_limit_bytes=24 * MIB),
        cost_estimate=pl.CostEstimate(
            flops=8 * count * kv_heads * tall * keys * HEAD_DIM,
            bytes_accessed=8 * shard * cols,
            transcendentals=count * kv_heads * tall * keys,
        ),
        name="attend",
    )(cache, key_pos, selected, *queries)
    return list(out)


def finish_kernel(count, size, *refs):
    parts = refs[:count]
    weights = refs[count]
    outs = refs[count + 1 : count + 1 + size]
    (context,) = refs[count + 1 + size :]
    rows, feat = context.shape
    heads = feat // HEAD_DIM
    width = weights.shape[1] // size
    me = lax.axis_index("head")
    tails = [part[:, feat : feat + LANES].astype(f32) for part in parts]
    for head in range(heads):
        levels = []
        for tail in tails:
            pieces = [tail[:, piece * heads + head : piece * heads + head + 1] for piece in range(3)]
            levels.append(pieces[0] + pieces[1] + pieces[2])
        top = functools.reduce(jnp.maximum, levels)
        shares = [jnp.exp2(level - top) for level in levels]
        whole = functools.reduce(jnp.add, shares)
        span = slice(head * HEAD_DIM, (head + 1) * HEAD_DIM)
        mixed = functools.reduce(
            jnp.add, [(share / whole) * part[:, span].astype(f32) for share, part in zip(shares, parts)]
        )
        context[:, span] = mixed.astype(bf16)
    for turn in range(size):
        start = (me ^ turn) * width
        step = 256 if width % 256 == 0 else width
        for at in range(0, width, step):
            part = weights[:, pl.ds(pl.multiple_of(start + at, step), step)]
            outs[turn][:, at : at + step] = jnp.dot(
                context[...], part, preferred_element_type=f32
            ).astype(outs[turn].dtype)


def finish(parts, w_out, size):
    rows = parts[0].shape[0]
    feat, cols = w_out.shape
    width = cols // size
    vmem = pl.BlockSpec(memory_space=pltpu.VMEM)
    return pl.pallas_call(
        functools.partial(finish_kernel, len(parts), size),
        out_shape=[jax.ShapeDtypeStruct((rows, width), f32 if turn == 0 else bf16) for turn in range(size)],
        in_specs=[vmem] * (len(parts) + 1),
        out_specs=[vmem] * size,
        scratch_shapes=[
            pltpu.VMEM((rows, feat), bf16),
        ],
        compiler_params=pltpu.CompilerParams(vmem_limit_bytes=24 * MIB),
        cost_estimate=pl.CostEstimate(
            flops=2 * rows * feat * cols, bytes_accessed=2 * feat * cols, transcendentals=0
        ),
        name="finish",
    )(*parts, w_out)


def swap(value, axis, turn, size):
    return lax.ppermute(value, axis, [(at, at ^ turn) for at in range(size)])


def body(
    hidden, norm_gain, w_query, w_key, w_value, w_out, stored_kv, selected, prompt_order, store_slot
):
    seq_count = lax.axis_size("seq")
    head_count = lax.axis_size("head")
    rows = hidden.shape[0]
    shard, _, local_kv, _ = stored_kv.shape
    stored = stored_kv.reshape(-1, HEAD_DIM)
    stored_other = swap(stored, "seq", 1, seq_count)
    query, kv, table = project(hidden, norm_gain, selected, w_query, w_key, w_value)
    turns = list(range(2, seq_count, 2))
    near_first = sorted(turns, key=lambda turn: (bin(turn).count("1"), turn))
    queries = {turn: swap(query, "seq", turn, seq_count) for turn in near_first}
    kv_other = swap(kv, "seq", 1, seq_count)
    cache, key_pos = merge(prompt_order, store_slot, table, stored, stored_other, kv, kv_other)
    parts = attend((0,), cache, key_pos, table, [query])
    for turn in near_first:
        (part,) = attend((turn,), cache, key_pos, table, [queries[turn]])
        parts.append(swap(part, "seq", turn, seq_count))
    blocks = finish(parts, w_out, head_count)
    total = blocks[0]
    arrived = [swap(blocks[turn], "head", turn, head_count) for turn in range(1, head_count)]
    for block in arrived:
        total = total + block.astype(f32)
    new_kv = kv.reshape(rows, 2, local_kv, HEAD_DIM)
    return (total.astype(bf16), new_kv)


def solution(mesh):
    in_specs = (
        P("seq", None),
        P(),
        P(None, "head"),
        P(None, "head"),
        P(None, "head"),
        P("head", None),
        P("seq", None, "head", None),
        P(),
        P(),
        P(),
    )
    out_specs = (P("seq", "head"), P("seq", None, "head", None))
    return jax.shard_map(body, mesh=mesh, in_specs=in_specs, out_specs=out_specs, check_vma=False)
```

```python
import functools
import math

import jax
import jax.numpy as jnp
import numpy as np
from jax import lax
from jax.experimental import pallas as pl
from jax.experimental.pallas import tpu as pltpu
from jax.sharding import PartitionSpec as P

HEADS = 32
KV_HEADS = 8
HEAD_DIM = 128
PASSAGE = 4096
GROUP = HEADS // KV_HEADS
MASKED = -1e30
LANES = 128
MIB = 1024 * 1024

bf16 = jnp.bfloat16
f32 = jnp.float32
NT = (((1,), (1,)), ((), ()))


def iota(shape, dim):
    return lax.broadcasted_iota(jnp.int32, shape, dim)


def column_of(row):
    n = row.shape[1]
    eye = iota((n, n), 0) == iota((n, n), 1)
    return jnp.sum(jnp.where(eye, row.astype(f32), 0.0), 1, keepdims=True)


def project_kernel(
    width, hidden_any, gain_any, selected_any, freq_any, wq_any, wk_any, wv_any, query, kv, table,
    hidden, gain, selected, freq, normed, weights, first_sem, sem,
):
    rows, feat = hidden.shape
    q_cols, k_cols, v_cols = wq_any.shape[1], wk_any.shape[1], wv_any.shape[1]
    pairs = ((hidden_any, hidden), (gain_any, gain), (selected_any, selected), (freq_any, freq))
    firsts = [
        pltpu.make_async_copy(source, target, first_sem.at[number])
        for number, (source, target) in enumerate(pairs)
    ]
    for copy in firsts:
        copy.start()
    chunks = []
    for source, count, base in ((wk_any, k_cols, 0), (wq_any, q_cols, k_cols), (wv_any, v_cols, k_cols + q_cols)):
        for at in range(0, count, width):
            chunks.append((source, at, base + at))
    copies = []
    for number, (source, at, place) in enumerate(chunks):
        copy = pltpu.make_async_copy(
            source.at[:, at : at + width], weights.at[:, place : place + width], sem.at[number]
        )
        copy.start()
        copies.append(copy)
    for copy in firsts[1:]:
        copy.wait()
    total = selected.shape[0]
    me = lax.axis_index("seq")
    mine = iota((rows, total), 1) == iota((rows, total), 0) + me * rows
    listed = selected[...].reshape(1, total)
    positions = jnp.sum(jnp.where(mine, listed.astype(f32), 0.0), 1, keepdims=True)
    table[...] = jnp.full(table.shape, -1, jnp.int32)
    for at in range(total // rows):
        table[at : at + 1, 0:rows] = listed[:, at * rows : (at + 1) * rows]
    angle = positions * freq[...]
    cosine = jnp.cos(angle)
    sine = jnp.sin(angle)
    sine = jnp.where(iota(sine.shape, 1) < HEAD_DIM // 2, -sine, sine)
    firsts[0].wait()
    step = 16
    for at in range(0, rows, step):
        wide = hidden[at : at + step, :].astype(f32)
        mean = jnp.sum(wide * wide, 1, keepdims=True) * (1.0 / feat)
        normed[at : at + step, :] = (wide * lax.rsqrt(mean + 1e-5) * gain[...]).astype(bf16)
    for (source, at, place), copy in zip(chunks, copies):
        copy.wait()
        out = jnp.dot(normed[...], weights[:, place : place + width], preferred_element_type=f32)
        for head in range(0, width, HEAD_DIM):
            part = out[:, head : head + HEAD_DIM]
            if source is not wv_any:
                part = part * cosine + pltpu.roll(part, HEAD_DIM // 2, 1) * sine
            part = part.astype(bf16)
            if source is wq_any:
                query[:, at + head : at + head + HEAD_DIM] = part
            else:
                col = at + head + (0 if source is wk_any else k_cols)
                kv[:, col : col + HEAD_DIM] = part


def project(hidden, gain, selected, wq, wk, wv):
    rows, feat = hidden.shape
    cols = wq.shape[1] + wk.shape[1] + wv.shape[1]
    width = math.gcd(math.gcd(wq.shape[1], wk.shape[1]), 256)
    freq = 500000.0 ** (-(np.arange(HEAD_DIM // 2, dtype=np.float32) * np.float32(2.0 / HEAD_DIM)))
    freq = jnp.asarray(np.concatenate([freq, freq])[None, :].astype(np.float32))
    vmem = pl.BlockSpec(memory_space=pltpu.VMEM)
    hbm = pl.BlockSpec(memory_space=pltpu.HBM)
    return pl.pallas_call(
        functools.partial(project_kernel, width),
        out_shape=(
            jax.ShapeDtypeStruct((rows, wq.shape[1]), bf16),
            jax.ShapeDtypeStruct((rows, wk.shape[1] + wv.shape[1]), bf16),
            jax.ShapeDtypeStruct((selected.shape[0] // rows, LANES), jnp.int32),
        ),
        in_specs=[hbm] * 7,
        out_specs=(vmem, vmem, vmem),
        scratch_shapes=[
            pltpu.VMEM((rows, feat), bf16),
            pltpu.VMEM((1, feat), f32),
            pltpu.VMEM(selected.shape, jnp.int32),
            pltpu.VMEM((1, HEAD_DIM), f32),
            pltpu.VMEM((rows, feat), bf16),
            pltpu.VMEM((feat, cols), bf16),
            pltpu.SemaphoreType.DMA((4,)),
            pltpu.SemaphoreType.DMA((cols // width,)),
        ],
        compiler_params=pltpu.CompilerParams(vmem_limit_bytes=48 * MIB),
        cost_estimate=pl.CostEstimate(
            flops=2 * rows * feat * cols, bytes_accessed=2 * feat * (cols + rows), transcendentals=0
        ),
        name="project",
    )(*[
        pltpu.with_memory_space_constraint(operand, pltpu.HBM)
        for operand in (hidden, gain.reshape(1, feat), selected, freq, wq, wk, wv)
    ])


def block_of(index, shard, order, slot):
    per = PASSAGE // shard
    own = index // per
    place = jnp.int32(0)
    for at in range(order.shape[0]):
        place = jnp.where(slot[order[at]] == own, at, place)
    return place * per + lax.rem(index, per)


def merge_kernel(order, slot, selected, stored, stored_other, kv, kv_other, cache, key_pos, wide):
    _, shard, cols = cache.shape
    kinds = cols // LANES
    rows = kv.shape[0]
    step = 128
    me = lax.axis_index("seq")
    for half in range(2):
        index = me ^ half
        block = block_of(index, shard, order, slot)
        holes = selected[pl.ds(block, 1), :] - block * shard
        offsets = column_of(selected[pl.ds(index, 1), :] - index * shard)
        high = jnp.floor(offsets * (1.0 / 32))
        low = offsets - 32 * high
        given = iota((LANES, 1), 0) < rows
        sources = [
            jnp.broadcast_to(jnp.where(given, value, 0.0), (LANES, LANES)).astype(bf16)
            for value in (high, low + 1)
        ]
        fresh = (kv, kv_other)[half][...]
        if rows < LANES:
            fresh = jnp.concatenate([fresh, jnp.zeros((LANES - rows, cols), bf16)], 0)
        source = jnp.concatenate(sources + [fresh], 1)
        for at in range(0, shard, step):
            places = iota((step, LANES), 0) + at
            hit = (places == holes).astype(f32).astype(bf16)
            picked = jnp.dot(hit, source, preferred_element_type=f32)
            mark = picked[:, LANES : 2 * LANES]
            hole = mark > 0.5
            key_pos[half * shard + at : half * shard + at + step, :] = jnp.where(
                hole,
                picked[:, :LANES] * 32 + (mark - 1) + (index * shard).astype(f32),
                (places + block * shard).astype(f32),
            )
            slot_at = (at // step) % 2
            wide[slot_at] = (stored, stored_other)[half][at * kinds : (at + step) * kinds, :].astype(f32)
            for kind in range(kinds):
                col = kind * LANES
                cache[half, at : at + step, col : col + LANES] = jnp.where(
                    hole,
                    picked[:, 2 * LANES + col : 3 * LANES + col],
                    wide[slot_at, pl.ds(kind, step, stride=kinds), :],
                ).astype(bf16)


def merge(order, slot, selected, stored, stored_other, kv, kv_other):
    cols = kv.shape[1]
    shard = stored.shape[0] * LANES // cols
    smem = pl.BlockSpec(memory_space=pltpu.SMEM)
    vmem = pl.BlockSpec(memory_space=pltpu.VMEM)
    return pl.pallas_call(
        merge_kernel,
        out_shape=(
            jax.ShapeDtypeStruct((2, shard, cols), bf16),
            jax.ShapeDtypeStruct((2 * shard, LANES), f32),
        ),
        in_specs=[smem, smem] + [vmem] * 5,
        out_specs=(vmem, vmem),
        scratch_shapes=[pltpu.VMEM((2, 128 * cols // LANES, LANES), f32)],
        compiler_params=pltpu.CompilerParams(vmem_limit_bytes=16 * MIB),
        cost_estimate=pl.CostEstimate(flops=1000, bytes_accessed=1000, transcendentals=0),
        name="merge",
    )(order, slot, selected, stored, stored_other, kv, kv_other)


def attend_kernel(partners, served, *refs):
    count = len(partners)
    cache, key_pos, selected = refs[:3]
    queries = refs[3 : 3 + count]
    outs = refs[-3 - count : -3]
    scores, weights, masks = refs[-3:]
    _, shard, cols = cache.shape
    rows = queries[0].shape[0]
    kv_heads = cols // (2 * HEAD_DIM)
    heads = len(served) * GROUP
    keys = 2 * shard
    step = 256
    scale = math.log2(math.e) / HEAD_DIM**0.5
    me = lax.axis_index("seq")
    one_hot = (iota((rows, LANES), 0) == iota((rows, LANES), 1)).astype(f32).astype(bf16)
    ones = jnp.ones((keys, LANES), bf16)

    def mask(at):
        row = selected[pl.ds(me ^ partners[at], 1), :].astype(f32)
        for place in range(0, keys, step):
            masks[at % 2, place : place + step, :] = jnp.where(
                key_pos[place : place + step, :] <= row, 0.0, MASKED
            ).astype(bf16)

    def left(at, head):
        parts = []
        for member in range(GROUP):
            col = (head * GROUP + member) * HEAD_DIM
            parts.append(jnp.concatenate([queries[at][:, col : col + HEAD_DIM], one_hot], 1))
        return jnp.concatenate(parts, 0)

    def cached(place, size, kind, head):
        col = (kind * kv_heads + head) * HEAD_DIM
        return cache[place // shard, place % shard : place % shard + size, col : col + HEAD_DIM]

    units = [(at, head) for at in range(count) for head in served]
    best = {}
    for number in range(len(units) + 1):
        if number < len(units):
            at, head = units[number]
            if head == served[0]:
                mask(at)
            stream = left(at, head)
        if number:
            old_at, old_head = units[number - 1]
            top = jnp.max(best.pop(number - 1), 1, keepdims=True) * scale
        running = None
        for place in range(0, keys, step):
            if number < len(units):
                right = jnp.concatenate(
                    [cached(place, step, 0, head), masks[at % 2, place : place + step, :]], 1
                )
                score = lax.dot_general(stream, right, NT, preferred_element_type=f32)
                scores[number % 2, :, place : place + step] = score
                for col in range(0, step, LANES):
                    part = score[:, col : col + LANES]
                    running = part if running is None else jnp.maximum(running, part)
            if number:
                slot = (number - 1) % 2
                weights[:, place : place + step] = jnp.exp2(
                    scores[slot, :, place : place + step] * scale - top
                ).astype(bf16)
        if number < len(units):
            best[number] = running
        if number:
            value = jnp.concatenate([cached(half * shard, shard, 1, old_head) for half in range(2)], 0)
            summed = jnp.dot(
                weights[...], jnp.concatenate([value, ones], 1), preferred_element_type=f32
            )
            total = summed[:, HEAD_DIM : HEAD_DIM + LANES]
            context = (summed[:, :HEAD_DIM] / total).astype(bf16)
            level = top + jnp.log2(total)
            high = level.astype(bf16).astype(f32)
            middle = (level - high).astype(bf16).astype(f32)
            low = level - high - middle
            lane = iota((rows, LANES), 1)
            out = outs[old_at]
            packed = jnp.zeros((rows, LANES), f32)
            for member in range(GROUP):
                which = served.index(old_head) * GROUP + member
                span = slice(member * rows, (member + 1) * rows)
                out[:, which * HEAD_DIM : (which + 1) * HEAD_DIM] = context[span]
                for piece, source in enumerate((high, middle, low)):
                    packed = jnp.where(lane == piece * heads + which, source[span], packed)
            tail = slice(heads * HEAD_DIM, heads * HEAD_DIM + LANES)
            if old_head != served[0]:
                packed = packed + out[:, tail].astype(f32)
            out[:, tail] = packed.astype(bf16)


def attend(partners, served, cache, key_pos, selected, queries, earlier):
    _, shard, cols = cache.shape
    rows = queries[0].shape[0]
    out_cols = len(served) * GROUP * HEAD_DIM + LANES
    tall = GROUP * rows
    keys = 2 * shard
    count = len(queries)
    vmem = pl.BlockSpec(memory_space=pltpu.VMEM)
    out = pl.pallas_call(
        functools.partial(attend_kernel, partners, served),
        out_shape=[jax.ShapeDtypeStruct((rows, out_cols), bf16)] * count,
        in_specs=[vmem] * (3 + count) + [pl.BlockSpec(memory_space=pl.ANY)] * len(earlier),
        out_specs=[vmem] * count,
        scratch_shapes=[
            pltpu.VMEM((2, tall, keys), f32),
            pltpu.VMEM((tall, keys), bf16),
            pltpu.VMEM((2, keys, LANES), bf16),
        ],
        compiler_params=pltpu.CompilerParams(vmem_limit_bytes=24 * MIB),
        cost_estimate=pl.CostEstimate(
            flops=8 * count * len(served) * tall * keys * HEAD_DIM,
            bytes_accessed=8 * shard * cols,
            transcendentals=count * len(served) * tall * keys,
        ),
        name="attend",
    )(cache, key_pos, selected, *queries, *earlier)
    return list(out)


def finish_kernel(groups, size, *refs):
    count = sum(len(group) for group in groups)
    parts = refs[:count]
    weights = refs[count]
    outs = refs[count + 1 : count + 1 + size]
    (context,) = refs[count + 1 + size :]
    width = weights.shape[1] // size
    me = lax.axis_index("head")
    found = {}
    at = 0
    for group in groups:
        for served in group:
            part = parts[at]
            at += 1
            heads = len(served) * GROUP
            tail = part[:, heads * HEAD_DIM : heads * HEAD_DIM + LANES].astype(f32)
            for number in range(heads):
                head = served[number // GROUP] * GROUP + number % GROUP
                pieces = [tail[:, piece * heads + number : piece * heads + number + 1] for piece in range(3)]
                level = pieces[0] + pieces[1] + pieces[2]
                found.setdefault(head, []).append((level, part, slice(number * HEAD_DIM, (number + 1) * HEAD_DIM)))
    for head, entries in found.items():
        top = functools.reduce(jnp.maximum, [level for level, _, _ in entries])
        shares = [jnp.exp2(level - top) for level, _, _ in entries]
        whole = functools.reduce(jnp.add, shares)
        mixed = functools.reduce(
            jnp.add,
            [(share / whole) * part[:, span].astype(f32) for share, (_, part, span) in zip(shares, entries)],
        )
        context[:, head * HEAD_DIM : (head + 1) * HEAD_DIM] = mixed.astype(bf16)
    for turn in range(size):
        start = (me ^ turn) * width
        step = 256 if width % 256 == 0 else width
        for at in range(0, width, step):
            part = weights[:, pl.ds(pl.multiple_of(start + at, step), step)]
            outs[turn][:, at : at + step] = jnp.dot(
                context[...], part, preferred_element_type=f32
            ).astype(outs[turn].dtype)


def finish(groups, w_out, size):
    parts = [part for group in groups for _, part in group]
    served = [[which for which, _ in group] for group in groups]
    rows = parts[0].shape[0]
    feat, cols = w_out.shape
    width = cols // size
    vmem = pl.BlockSpec(memory_space=pltpu.VMEM)
    return pl.pallas_call(
        functools.partial(finish_kernel, served, size),
        out_shape=[jax.ShapeDtypeStruct((rows, width), f32 if turn == 0 else bf16) for turn in range(size)],
        in_specs=[vmem] * (len(parts) + 1),
        out_specs=[vmem] * size,
        scratch_shapes=[
            pltpu.VMEM((rows, feat), bf16),
        ],
        compiler_params=pltpu.CompilerParams(vmem_limit_bytes=24 * MIB),
        cost_estimate=pl.CostEstimate(
            flops=2 * rows * feat * cols, bytes_accessed=2 * feat * cols, transcendentals=0
        ),
        name="finish",
    )(*parts, w_out)


def swap(value, axis, turn, size):
    return lax.ppermute(value, axis, [(at, at ^ turn) for at in range(size)])


def body(
    hidden, norm_gain, w_query, w_key, w_value, w_out, stored_kv, selected, prompt_order, store_slot
):
    seq_count = lax.axis_size("seq")
    head_count = lax.axis_size("head")
    rows = hidden.shape[0]
    shard, _, local_kv, _ = stored_kv.shape
    stored = stored_kv.reshape(-1, HEAD_DIM)
    stored_other = swap(stored, "seq", 1, seq_count)
    query, kv, table = project(hidden, norm_gain, selected, w_query, w_key, w_value)
    turns = sorted(range(2, seq_count, 2), key=lambda turn: (-bin(turn).count("1"), turn))
    queries = {turn: swap(query, "seq", turn, seq_count) for turn in turns}
    kv_other = swap(kv, "seq", 1, seq_count)
    cache, key_pos = merge(prompt_order, store_slot, table, stored, stored_other, kv, kv_other)
    every = tuple(range(local_kv))
    groups = []
    done = []
    far, near = turns[:-2], turns[-2:]
    for turn in far:
        done = attend((turn,), every, cache, key_pos, table, [queries[turn]], done)
        groups.append([(every, swap(done[0], "seq", turn, seq_count))])
    split = {turn: [] for turn in near}
    for head in every:
        done = attend(tuple(near), (head,), cache, key_pos, table, [queries[turn] for turn in near], done)
        for turn, part in zip(near, done):
            split[turn].append(((head,), swap(part, "seq", turn, seq_count)))
    groups += list(split.values())
    groups.append([(every, attend((0,), every, cache, key_pos, table, [query], done)[0])])
    blocks = finish(groups, w_out, head_count)
    total = blocks[0]
    arrived = [swap(blocks[turn], "head", turn, head_count) for turn in range(1, head_count)]
    for block in arrived:
        total = total + block.astype(f32)
    new_kv = kv.reshape(rows, 2, local_kv, HEAD_DIM)
    return (total.astype(bf16), new_kv)


def solution(mesh):
    in_specs = (
        P("seq", None),
        P(),
        P(None, "head"),
        P(None, "head"),
        P(None, "head"),
        P("head", None),
        P("seq", None, "head", None),
        P(),
        P(),
        P(),
    )
    out_specs = (P("seq", "head"), P("seq", None, "head", None))
    return jax.shard_map(body, mesh=mesh, in_specs=in_specs, out_specs=out_specs, check_vma=False)
```

```python
import functools
import math

import jax
import jax.numpy as jnp
import numpy as np
from jax import lax
from jax.experimental import pallas as pl
from jax.experimental.pallas import tpu as pltpu
from jax.sharding import PartitionSpec as P

HEADS = 32
KV_HEADS = 8
HEAD_DIM = 128
PASSAGE = 4096
GROUP = HEADS // KV_HEADS
MASKED = -1e30
LANES = 128
MIB = 1024 * 1024

bf16 = jnp.bfloat16
f32 = jnp.float32
NT = (((1,), (1,)), ((), ()))


def iota(shape, dim):
    return lax.broadcasted_iota(jnp.int32, shape, dim)


def column_of(row):
    n = row.shape[1]
    eye = iota((n, n), 0) == iota((n, n), 1)
    return jnp.sum(jnp.where(eye, row.astype(f32), 0.0), 1, keepdims=True)


def project_kernel(
    width, hidden_any, gain_any, selected_any, freq_any, wq_any, wk_any, wv_any, query, kv, table,
    hidden, gain, selected, freq, normed, weights, first_sem, sem,
):
    rows, feat = hidden.shape
    q_cols, k_cols, v_cols = wq_any.shape[1], wk_any.shape[1], wv_any.shape[1]
    pairs = ((hidden_any, hidden), (gain_any, gain), (selected_any, selected), (freq_any, freq))
    firsts = [
        pltpu.make_async_copy(source, target, first_sem.at[number])
        for number, (source, target) in enumerate(pairs)
    ]
    for copy in firsts:
        copy.start()
    chunks = []
    for source, count, base in ((wk_any, k_cols, 0), (wq_any, q_cols, k_cols), (wv_any, v_cols, k_cols + q_cols)):
        for at in range(0, count, width):
            chunks.append((source, at, base + at))
    copies = []
    for number, (source, at, place) in enumerate(chunks):
        copy = pltpu.make_async_copy(
            source.at[:, at : at + width], weights.at[:, place : place + width], sem.at[number]
        )
        copy.start(priority=1)
        copies.append(copy)
    for copy in firsts[1:]:
        copy.wait()
    total = selected.shape[0]
    me = lax.axis_index("seq")
    mine = iota((rows, total), 1) == iota((rows, total), 0) + me * rows
    listed = selected[...].reshape(1, total)
    positions = jnp.sum(jnp.where(mine, listed.astype(f32), 0.0), 1, keepdims=True)
    table[...] = jnp.full(table.shape, -1, jnp.int32)
    for at in range(total // rows):
        table[at : at + 1, 0:rows] = listed[:, at * rows : (at + 1) * rows]
    angle = positions * freq[...]
    cosine = jnp.cos(angle)
    sine = jnp.sin(angle)
    sine = jnp.where(iota(sine.shape, 1) < HEAD_DIM // 2, -sine, sine)
    firsts[0].wait()
    step = 16
    for at in range(0, rows, step):
        wide = hidden[at : at + step, :].astype(f32)
        mean = jnp.sum(wide * wide, 1, keepdims=True) * (1.0 / feat)
        normed[at : at + step, :] = (wide * lax.rsqrt(mean + 1e-5) * gain[...]).astype(bf16)
    for (source, at, place), copy in zip(chunks, copies):
        copy.wait()
        out = jnp.dot(normed[...], weights[:, place : place + width], preferred_element_type=f32)
        for head in range(0, width, HEAD_DIM):
            part = out[:, head : head + HEAD_DIM]
            if source is not wv_any:
                part = part * cosine + pltpu.roll(part, HEAD_DIM // 2, 1) * sine
            part = part.astype(bf16)
            if source is wq_any:
                query[:, at + head : at + head + HEAD_DIM] = part
            else:
                col = at + head + (0 if source is wk_any else k_cols)
                kv[:, col : col + HEAD_DIM] = part


def project(hidden, gain, selected, wq, wk, wv):
    rows, feat = hidden.shape
    cols = wq.shape[1] + wk.shape[1] + wv.shape[1]
    width = math.gcd(math.gcd(wq.shape[1], wk.shape[1]), 256)
    freq = 500000.0 ** (-(np.arange(HEAD_DIM // 2, dtype=np.float32) * np.float32(2.0 / HEAD_DIM)))
    freq = jnp.asarray(np.concatenate([freq, freq])[None, :].astype(np.float32))
    vmem = pl.BlockSpec(memory_space=pltpu.VMEM)
    hbm = pl.BlockSpec(memory_space=pltpu.HBM)
    return pl.pallas_call(
        functools.partial(project_kernel, width),
        out_shape=(
            jax.ShapeDtypeStruct((rows, wq.shape[1]), bf16),
            jax.ShapeDtypeStruct((rows, wk.shape[1] + wv.shape[1]), bf16),
            jax.ShapeDtypeStruct((selected.shape[0] // rows, LANES), jnp.int32),
        ),
        in_specs=[hbm] * 7,
        out_specs=(vmem, vmem, vmem),
        scratch_shapes=[
            pltpu.VMEM((rows, feat), bf16),
            pltpu.VMEM((1, feat), f32),
            pltpu.VMEM(selected.shape, jnp.int32),
            pltpu.VMEM((1, HEAD_DIM), f32),
            pltpu.VMEM((rows, feat), bf16),
            pltpu.VMEM((feat, cols), bf16),
            pltpu.SemaphoreType.DMA((4,)),
            pltpu.SemaphoreType.DMA((cols // width,)),
        ],
        compiler_params=pltpu.CompilerParams(vmem_limit_bytes=48 * MIB),
        cost_estimate=pl.CostEstimate(
            flops=2 * rows * feat * cols, bytes_accessed=2 * feat * (cols + rows), transcendentals=0
        ),
        name="project",
    )(*[
        pltpu.with_memory_space_constraint(operand, pltpu.HBM)
        for operand in (hidden, gain.reshape(1, feat), selected, freq, wq, wk, wv)
    ])


def block_of(index, shard, order, slot):
    per = PASSAGE // shard
    own = index // per
    place = jnp.int32(0)
    for at in range(order.shape[0]):
        place = jnp.where(slot[order[at]] == own, at, place)
    return place * per + lax.rem(index, per)


def merge_kernel(order, slot, selected, stored, stored_other, kv, kv_other, cache, key_pos, wide):
    _, shard, cols = cache.shape
    kinds = cols // LANES
    rows = kv.shape[0]
    step = 128
    me = lax.axis_index("seq")
    for half in range(2):
        index = me ^ half
        block = block_of(index, shard, order, slot)
        holes = selected[pl.ds(block, 1), :] - block * shard
        offsets = column_of(selected[pl.ds(index, 1), :] - index * shard)
        high = jnp.floor(offsets * (1.0 / 32))
        low = offsets - 32 * high
        given = iota((LANES, 1), 0) < rows
        sources = [
            jnp.broadcast_to(jnp.where(given, value, 0.0), (LANES, LANES)).astype(bf16)
            for value in (high, low + 1)
        ]
        fresh = (kv, kv_other)[half][...]
        if rows < LANES:
            fresh = jnp.concatenate([fresh, jnp.zeros((LANES - rows, cols), bf16)], 0)
        source = jnp.concatenate(sources + [fresh], 1)
        for at in range(0, shard, step):
            places = iota((step, LANES), 0) + at
            hit = (places == holes).astype(f32).astype(bf16)
            picked = jnp.dot(hit, source, preferred_element_type=f32)
            mark = picked[:, LANES : 2 * LANES]
            hole = mark > 0.5
            key_pos[half * shard + at : half * shard + at + step, :] = jnp.where(
                hole,
                picked[:, :LANES] * 32 + (mark - 1) + (index * shard).astype(f32),
                (places + block * shard).astype(f32),
            )
            slot_at = (at // step) % 2
            wide[slot_at] = (stored, stored_other)[half][at * kinds : (at + step) * kinds, :].astype(f32)
            for kind in range(kinds):
                col = kind * LANES
                cache[half, at : at + step, col : col + LANES] = jnp.where(
                    hole,
                    picked[:, 2 * LANES + col : 3 * LANES + col],
                    wide[slot_at, pl.ds(kind, step, stride=kinds), :],
                ).astype(bf16)


def merge(order, slot, selected, stored, stored_other, kv, kv_other):
    cols = kv.shape[1]
    shard = stored.shape[0] * LANES // cols
    smem = pl.BlockSpec(memory_space=pltpu.SMEM)
    vmem = pl.BlockSpec(memory_space=pltpu.VMEM)
    return pl.pallas_call(
        merge_kernel,
        out_shape=(
            jax.ShapeDtypeStruct((2, shard, cols), bf16),
            jax.ShapeDtypeStruct((2 * shard, LANES), f32),
        ),
        in_specs=[smem, smem] + [vmem] * 5,
        out_specs=(vmem, vmem),
        scratch_shapes=[pltpu.VMEM((2, 128 * cols // LANES, LANES), f32)],
        compiler_params=pltpu.CompilerParams(vmem_limit_bytes=16 * MIB),
        cost_estimate=pl.CostEstimate(flops=1000, bytes_accessed=1000, transcendentals=0),
        name="merge",
    )(order, slot, selected, stored, stored_other, kv, kv_other)


def attend_kernel(partners, carried, *refs):
    count = len(partners)
    cache, key_pos, selected = refs[:3]
    queries = refs[3 : 3 + count]
    scores, weights, masks = refs[-3:]
    for source, target in zip(refs[3 + count :], refs[3 + count + carried : -3 - count]):
        target[...] = source[...]
    outs = refs[-3 - count : -3]
    _, shard, cols = cache.shape
    rows = queries[0].shape[0]
    kv_heads = cols // (2 * HEAD_DIM)
    heads = kv_heads * GROUP
    keys = 2 * shard
    step = 256
    scale = math.log2(math.e) / HEAD_DIM**0.5
    me = lax.axis_index("seq")
    one_hot = (iota((rows, LANES), 0) == iota((rows, LANES), 1)).astype(f32).astype(bf16)
    ones = jnp.ones((keys, LANES), bf16)

    def mask(at):
        row = selected[pl.ds(me ^ partners[at], 1), :].astype(f32)
        for place in range(0, keys, step):
            masks[at % 2, place : place + step, :] = jnp.where(
                key_pos[place : place + step, :] <= row, 0.0, MASKED
            ).astype(bf16)

    def left(at, head):
        parts = []
        for member in range(GROUP):
            col = (head * GROUP + member) * HEAD_DIM
            parts.append(jnp.concatenate([queries[at][:, col : col + HEAD_DIM], one_hot], 1))
        return jnp.concatenate(parts, 0)

    def cached(place, size, kind, head):
        col = (kind * kv_heads + head) * HEAD_DIM
        return cache[place // shard, place % shard : place % shard + size, col : col + HEAD_DIM]

    units = [(at, head) for at in range(count) for head in range(kv_heads)]
    best = {}
    for number in range(len(units) + 1):
        if number < len(units):
            at, head = units[number]
            if head == 0:
                mask(at)
            stream = left(at, head)
        if number:
            old_at, old_head = units[number - 1]
            top = jnp.max(best.pop(number - 1), 1, keepdims=True) * scale
        running = None
        for place in range(0, keys, step):
            if number < len(units):
                right = jnp.concatenate(
                    [cached(place, step, 0, head), masks[at % 2, place : place + step, :]], 1
                )
                score = lax.dot_general(stream, right, NT, preferred_element_type=f32)
                scores[number % 2, :, place : place + step] = score
                for col in range(0, step, LANES):
                    part = score[:, col : col + LANES]
                    running = part if running is None else jnp.maximum(running, part)
            if number:
                slot = (number - 1) % 2
                weights[:, place : place + step] = jnp.exp2(
                    scores[slot, :, place : place + step] * scale - top
                ).astype(bf16)
        if number < len(units):
            best[number] = running
        if number:
            value = jnp.concatenate([cached(half * shard, shard, 1, old_head) for half in range(2)], 0)
            summed = jnp.dot(
                weights[...], jnp.concatenate([value, ones], 1), preferred_element_type=f32
            )
            total = summed[:, HEAD_DIM : HEAD_DIM + LANES]
            context = (summed[:, :HEAD_DIM] / total).astype(bf16)
            level = top + jnp.log2(total)
            high = level.astype(bf16).astype(f32)
            middle = (level - high).astype(bf16).astype(f32)
            low = level - high - middle
            lane = iota((rows, LANES), 1)
            out = outs[old_at]
            packed = jnp.zeros((rows, LANES), f32)
            for member in range(GROUP):
                which = old_head * GROUP + member
                span = slice(member * rows, (member + 1) * rows)
                out[:, which * HEAD_DIM : (which + 1) * HEAD_DIM] = context[span]
                for piece, source in enumerate((high, middle, low)):
                    packed = jnp.where(lane == piece * heads + which, source[span], packed)
            tail = slice(heads * HEAD_DIM, heads * HEAD_DIM + LANES)
            if old_head:
                packed = packed + out[:, tail].astype(f32)
            out[:, tail] = packed.astype(bf16)


def attend(partners, cache, key_pos, selected, queries, earlier=()):
    _, shard, cols = cache.shape
    rows = queries[0].shape[0]
    kv_heads = cols // (2 * HEAD_DIM)
    out_cols = queries[0].shape[1] + LANES
    tall = GROUP * rows
    keys = 2 * shard
    count = len(queries)
    vmem = pl.BlockSpec(memory_space=pltpu.VMEM)
    out = pl.pallas_call(
        functools.partial(attend_kernel, partners, len(earlier)),
        out_shape=[jax.ShapeDtypeStruct((rows, out_cols), bf16)] * (len(earlier) + count),
        in_specs=[vmem] * (3 + count + len(earlier)),
        out_specs=[vmem] * (len(earlier) + count),
        scratch_shapes=[
            pltpu.VMEM((2, tall, keys), f32),
            pltpu.VMEM((tall, keys), bf16),
            pltpu.VMEM((2, keys, LANES), bf16),
        ],
        compiler_params=pltpu.CompilerParams(vmem_limit_bytes=24 * MIB),
        cost_estimate=pl.CostEstimate(flops=1000, bytes_accessed=1000, transcendentals=0),
        name="attend",
    )(cache, key_pos, selected, *queries, *earlier)
    return list(out)


def finish_kernel(count, size, *refs):
    parts = refs[:count]
    weights = refs[count]
    outs = refs[count + 1 : count + 1 + size]
    (context,) = refs[count + 1 + size :]
    feat = context.shape[1]
    heads = feat // HEAD_DIM
    width = weights.shape[1] // size
    me = lax.axis_index("head")
    tails = [part[:, feat : feat + LANES].astype(f32) for part in parts]
    for head in range(heads):
        levels = []
        for tail in tails:
            pieces = [tail[:, piece * heads + head : piece * heads + head + 1] for piece in range(3)]
            levels.append(pieces[0] + pieces[1] + pieces[2])
        top = functools.reduce(jnp.maximum, levels)
        shares = [jnp.exp2(level - top) for level in levels]
        whole = functools.reduce(jnp.add, shares)
        span = slice(head * HEAD_DIM, (head + 1) * HEAD_DIM)
        mixed = functools.reduce(
            jnp.add, [(share / whole) * part[:, span].astype(f32) for share, part in zip(shares, parts)]
        )
        context[:, span] = mixed.astype(bf16)
    for turn in range(size):
        start = (me ^ turn) * width
        step = 256 if width % 256 == 0 else width
        for at in range(0, width, step):
            part = weights[:, pl.ds(pl.multiple_of(start + at, step), step)]
            outs[turn][:, at : at + step] = jnp.dot(
                context[...], part, preferred_element_type=f32
            ).astype(outs[turn].dtype)


def finish(parts, w_out, size):
    rows = parts[0].shape[0]
    feat, cols = w_out.shape
    width = cols // size
    vmem = pl.BlockSpec(memory_space=pltpu.VMEM)
    return pl.pallas_call(
        functools.partial(finish_kernel, len(parts), size),
        out_shape=[jax.ShapeDtypeStruct((rows, width), f32 if turn == 0 else bf16) for turn in range(size)],
        in_specs=[vmem] * (len(parts) + 1),
        out_specs=[vmem] * size,
        scratch_shapes=[
            pltpu.VMEM((rows, feat), bf16),
        ],
        compiler_params=pltpu.CompilerParams(vmem_limit_bytes=24 * MIB),
        cost_estimate=pl.CostEstimate(
            flops=2 * rows * feat * cols, bytes_accessed=2 * feat * cols, transcendentals=0
        ),
        name="finish",
    )(*parts, w_out)


def swap(value, axis, turn, size):
    return lax.ppermute(value, axis, [(at, at ^ turn) for at in range(size)])


def body(
    hidden, norm_gain, w_query, w_key, w_value, w_out, stored_kv, selected, prompt_order, store_slot
):
    seq_count = lax.axis_size("seq")
    head_count = lax.axis_size("head")
    rows = hidden.shape[0]
    shard, _, local_kv, _ = stored_kv.shape
    stored = stored_kv.reshape(-1, HEAD_DIM)
    query, kv, table = project(hidden, norm_gain, selected, w_query, w_key, w_value)
    turns = sorted(range(2, seq_count, 2), key=lambda turn: (bin(turn).count("1"), turn))
    queries = {turn: swap(query, "seq", turn, seq_count) for turn in turns}
    stored, kv = lax.optimization_barrier((stored, kv))
    stored_other, kv_other = (swap(value, "seq", 1, seq_count) for value in (stored, kv))
    cache, key_pos = merge(prompt_order, store_slot, table, stored, stored_other, kv, kv_other)
    first, second = turns[:2]
    parts = [attend((0,), cache, key_pos, table, [query])[0]]
    for turn in turns[2:]:
        (part,) = attend((turn,), cache, key_pos, table, [queries[turn]])
        parts.append(swap(part, "seq", turn, seq_count))
    done = attend((first,), cache, key_pos, table, [queries[first]])
    done = attend((second,), cache, key_pos, table, [queries[second]], done)
    parts += [swap(part, "seq", turn, seq_count) for turn, part in zip((first, second), done)]
    blocks = finish(parts, w_out, head_count)
    total = blocks[0]
    arrived = [
        swap(blocks[turn], "head", turn, head_count) for turn in (*range(2, head_count), 1)
    ]
    for block in arrived:
        total = total + block.astype(f32)
    new_kv = kv.reshape(rows, 2, local_kv, HEAD_DIM)
    return (total.astype(bf16), new_kv)


def solution(mesh):
    in_specs = (
        P("seq", None),
        P(),
        P(None, "head"),
        P(None, "head"),
        P(None, "head"),
        P("head", None),
        P("seq", None, "head", None),
        P(),
        P(),
        P(),
    )
    out_specs = (P("seq", "head"), P("seq", None, "head", None))
    return jax.shard_map(body, mesh=mesh, in_specs=in_specs, out_specs=out_specs, check_vma=False)
```

```python
import functools
import math

import jax
import jax.numpy as jnp
import numpy as np
from jax import lax
from jax.experimental import pallas as pl
from jax.experimental.pallas import tpu as pltpu
from jax.sharding import PartitionSpec as P

HEADS = 32
KV_HEADS = 8
HEAD_DIM = 128
PASSAGE = 4096
GROUP = HEADS // KV_HEADS
MASKED = -1e30
LANES = 128
MIB = 1024 * 1024

bf16 = jnp.bfloat16
f32 = jnp.float32
NT = (((1,), (1,)), ((), ()))


def iota(shape, dim):
    return lax.broadcasted_iota(jnp.int32, shape, dim)


def column_of(row):
    n = row.shape[1]
    eye = iota((n, n), 0) == iota((n, n), 1)
    return jnp.sum(jnp.where(eye, row.astype(f32), 0.0), 1, keepdims=True)


def project_kernel(
    width, hidden_any, gain_any, selected_any, freq_any, wq_any, wk_any, wv_any, query, kv, table,
    hidden, gain, selected, freq, normed, weights, first_sem, sem,
):
    rows, feat = hidden.shape
    q_cols, k_cols, v_cols = wq_any.shape[1], wk_any.shape[1], wv_any.shape[1]
    pairs = ((hidden_any, hidden), (gain_any, gain), (selected_any, selected), (freq_any, freq))
    firsts = [
        pltpu.make_async_copy(source, target, first_sem.at[number])
        for number, (source, target) in enumerate(pairs)
    ]
    for copy in firsts:
        copy.start()
    chunks = []
    for source, count, base in ((wk_any, k_cols, 0), (wq_any, q_cols, k_cols), (wv_any, v_cols, k_cols + q_cols)):
        for at in range(0, count, width):
            chunks.append((source, at, base + at))
    copies = []
    for number, (source, at, place) in enumerate(chunks):
        copy = pltpu.make_async_copy(
            source.at[:, at : at + width], weights.at[:, place : place + width], sem.at[number]
        )
        copy.start(priority=1)
        copies.append(copy)
    for copy in firsts[1:]:
        copy.wait()
    total = selected.shape[0]
    me = lax.axis_index("seq")
    mine = iota((rows, total), 1) == iota((rows, total), 0) + me * rows
    listed = selected[...].reshape(1, total)
    positions = jnp.sum(jnp.where(mine, listed.astype(f32), 0.0), 1, keepdims=True)
    table[...] = jnp.full(table.shape, -1, jnp.int32)
    for at in range(total // rows):
        table[at : at + 1, 0:rows] = listed[:, at * rows : (at + 1) * rows]
    angle = positions * freq[...]
    cosine = jnp.cos(angle)
    sine = jnp.sin(angle)
    sine = jnp.where(iota(sine.shape, 1) < HEAD_DIM // 2, -sine, sine)
    firsts[0].wait()
    step = 16
    for at in range(0, rows, step):
        wide = hidden[at : at + step, :].astype(f32)
        mean = jnp.sum(wide * wide, 1, keepdims=True) * (1.0 / feat)
        normed[at : at + step, :] = (wide * lax.rsqrt(mean + 1e-5) * gain[...]).astype(bf16)
    for (source, at, place), copy in zip(chunks, copies):
        copy.wait()
        out = jnp.dot(normed[...], weights[:, place : place + width], preferred_element_type=f32)
        for head in range(0, width, HEAD_DIM):
            part = out[:, head : head + HEAD_DIM]
            if source is not wv_any:
                part = part * cosine + pltpu.roll(part, HEAD_DIM // 2, 1) * sine
            part = part.astype(bf16)
            if source is wq_any:
                query[:, at + head : at + head + HEAD_DIM] = part
            else:
                col = at + head + (0 if source is wk_any else k_cols)
                kv[:, col : col + HEAD_DIM] = part


def project(hidden, gain, selected, wq, wk, wv):
    rows, feat = hidden.shape
    cols = wq.shape[1] + wk.shape[1] + wv.shape[1]
    width = math.gcd(math.gcd(wq.shape[1], wk.shape[1]), 256)
    freq = 500000.0 ** (-(np.arange(HEAD_DIM // 2, dtype=np.float32) * np.float32(2.0 / HEAD_DIM)))
    freq = jnp.asarray(np.concatenate([freq, freq])[None, :].astype(np.float32))
    vmem = pl.BlockSpec(memory_space=pltpu.VMEM)
    hbm = pl.BlockSpec(memory_space=pltpu.HBM)
    return pl.pallas_call(
        functools.partial(project_kernel, width),
        out_shape=(
            jax.ShapeDtypeStruct((rows, wq.shape[1]), bf16),
            jax.ShapeDtypeStruct((rows, wk.shape[1] + wv.shape[1]), bf16),
            jax.ShapeDtypeStruct((selected.shape[0] // rows, LANES), jnp.int32),
        ),
        in_specs=[hbm] * 7,
        out_specs=(vmem, vmem, vmem),
        scratch_shapes=[
            pltpu.VMEM((rows, feat), bf16),
            pltpu.VMEM((1, feat), f32),
            pltpu.VMEM(selected.shape, jnp.int32),
            pltpu.VMEM((1, HEAD_DIM), f32),
            pltpu.VMEM((rows, feat), bf16),
            pltpu.VMEM((feat, cols), bf16),
            pltpu.SemaphoreType.DMA((4,)),
            pltpu.SemaphoreType.DMA((cols // width,)),
        ],
        compiler_params=pltpu.CompilerParams(vmem_limit_bytes=48 * MIB),
        cost_estimate=pl.CostEstimate(
            flops=2 * rows * feat * cols, bytes_accessed=2 * feat * (cols + rows), transcendentals=0
        ),
        name="project",
    )(*[
        pltpu.with_memory_space_constraint(operand, pltpu.HBM)
        for operand in (hidden, gain.reshape(1, feat), selected, freq, wq, wk, wv)
    ])


def block_of(index, shard, order, slot):
    per = PASSAGE // shard
    own = index // per
    place = jnp.int32(0)
    for at in range(order.shape[0]):
        place = jnp.where(slot[order[at]] == own, at, place)
    return place * per + lax.rem(index, per)


def merge_kernel(
    order, slot, selected, stored, stored_other, kv, kv_other, query, cache, key_pos, passed, wide
):
    passed[...] = query[...]
    _, shard, cols = cache.shape
    kinds = cols // LANES
    rows = kv.shape[0]
    step = 128
    me = lax.axis_index("seq")
    for half in range(2):
        index = me ^ half
        block = block_of(index, shard, order, slot)
        holes = selected[pl.ds(block, 1), :] - block * shard
        offsets = column_of(selected[pl.ds(index, 1), :] - index * shard)
        high = jnp.floor(offsets * (1.0 / 32))
        low = offsets - 32 * high
        given = iota((LANES, 1), 0) < rows
        sources = [
            jnp.broadcast_to(jnp.where(given, value, 0.0), (LANES, LANES)).astype(bf16)
            for value in (high, low + 1)
        ]
        fresh = (kv, kv_other)[half][...]
        if rows < LANES:
            fresh = jnp.concatenate([fresh, jnp.zeros((LANES - rows, cols), bf16)], 0)
        source = jnp.concatenate(sources + [fresh], 1)
        for at in range(0, shard, step):
            places = iota((step, LANES), 0) + at
            hit = (places == holes).astype(f32).astype(bf16)
            picked = jnp.dot(hit, source, preferred_element_type=f32)
            mark = picked[:, LANES : 2 * LANES]
            hole = mark > 0.5
            key_pos[half * shard + at : half * shard + at + step, :] = jnp.where(
                hole,
                picked[:, :LANES] * 32 + (mark - 1) + (index * shard).astype(f32),
                (places + block * shard).astype(f32),
            )
            slot_at = (at // step) % 2
            wide[slot_at] = (stored, stored_other)[half][at * kinds : (at + step) * kinds, :].astype(f32)
            for kind in range(kinds):
                col = kind * LANES
                cache[half, at : at + step, col : col + LANES] = jnp.where(
                    hole,
                    picked[:, 2 * LANES + col : 3 * LANES + col],
                    wide[slot_at, pl.ds(kind, step, stride=kinds), :],
                ).astype(bf16)


def merge(order, slot, selected, stored, stored_other, kv, kv_other, query):
    cols = kv.shape[1]
    shard = stored.shape[0] * LANES // cols
    smem = pl.BlockSpec(memory_space=pltpu.SMEM)
    vmem = pl.BlockSpec(memory_space=pltpu.VMEM)
    return pl.pallas_call(
        merge_kernel,
        out_shape=(
            jax.ShapeDtypeStruct((2, shard, cols), bf16),
            jax.ShapeDtypeStruct((2 * shard, LANES), f32),
            jax.ShapeDtypeStruct(query.shape, query.dtype),
        ),
        in_specs=[smem, smem] + [vmem] * 6,
        out_specs=(vmem, vmem, vmem),
        scratch_shapes=[pltpu.VMEM((2, 128 * cols // LANES, LANES), f32)],
        compiler_params=pltpu.CompilerParams(vmem_limit_bytes=16 * MIB),
        cost_estimate=pl.CostEstimate(flops=1000, bytes_accessed=1000, transcendentals=0),
        name="merge",
    )(order, slot, selected, stored, stored_other, kv, kv_other, query)


def attend_kernel(partners, carried, *refs):
    count = len(partners)
    cache, key_pos, selected = refs[:3]
    queries = refs[3 : 3 + count]
    scores, weights, masks = refs[-3:]
    for source, target in zip(refs[3 + count :], refs[3 + count + carried : -3 - count]):
        target[...] = source[...]
    outs = refs[-3 - count : -3]
    _, shard, cols = cache.shape
    rows = queries[0].shape[0]
    kv_heads = cols // (2 * HEAD_DIM)
    heads = kv_heads * GROUP
    keys = 2 * shard
    step = 256
    scale = math.log2(math.e) / HEAD_DIM**0.5
    me = lax.axis_index("seq")
    one_hot = (iota((rows, LANES), 0) == iota((rows, LANES), 1)).astype(f32).astype(bf16)
    ones = jnp.ones((keys, LANES), bf16)

    def mask(at):
        row = selected[pl.ds(me ^ partners[at], 1), :].astype(f32)
        for place in range(0, keys, step):
            masks[at % 2, place : place + step, :] = jnp.where(
                key_pos[place : place + step, :] <= row, 0.0, MASKED
            ).astype(bf16)

    def left(at, head):
        parts = []
        for member in range(GROUP):
            col = (head * GROUP + member) * HEAD_DIM
            parts.append(jnp.concatenate([queries[at][:, col : col + HEAD_DIM], one_hot], 1))
        return jnp.concatenate(parts, 0)

    def cached(place, size, kind, head):
        col = (kind * kv_heads + head) * HEAD_DIM
        return cache[place // shard, place % shard : place % shard + size, col : col + HEAD_DIM]

    units = [(at, head) for at in range(count) for head in range(kv_heads)]
    best = {}
    for number in range(len(units) + 1):
        if number < len(units):
            at, head = units[number]
            if head == 0:
                mask(at)
            stream = left(at, head)
        if number:
            old_at, old_head = units[number - 1]
            top = jnp.max(best.pop(number - 1), 1, keepdims=True) * scale
        running = None
        for place in range(0, keys, step):
            if number < len(units):
                right = jnp.concatenate(
                    [cached(place, step, 0, head), masks[at % 2, place : place + step, :]], 1
                )
                score = lax.dot_general(stream, right, NT, preferred_element_type=f32)
                scores[number % 2, :, place : place + step] = score
                for col in range(0, step, LANES):
                    part = score[:, col : col + LANES]
                    running = part if running is None else jnp.maximum(running, part)
            if number:
                slot = (number - 1) % 2
                weights[:, place : place + step] = jnp.exp2(
                    scores[slot, :, place : place + step] * scale - top
                ).astype(bf16)
        if number < len(units):
            best[number] = running
        if number:
            value = jnp.concatenate([cached(half * shard, shard, 1, old_head) for half in range(2)], 0)
            summed = jnp.dot(
                weights[...], jnp.concatenate([value, ones], 1), preferred_element_type=f32
            )
            total = summed[:, HEAD_DIM : HEAD_DIM + LANES]
            context = (summed[:, :HEAD_DIM] / total).astype(bf16)
            level = top + jnp.log2(total)
            high = level.astype(bf16).astype(f32)
            middle = (level - high).astype(bf16).astype(f32)
            low = level - high - middle
            lane = iota((rows, LANES), 1)
            out = outs[old_at]
            packed = jnp.zeros((rows, LANES), f32)
            for member in range(GROUP):
                which = old_head * GROUP + member
                span = slice(member * rows, (member + 1) * rows)
                out[:, which * HEAD_DIM : (which + 1) * HEAD_DIM] = context[span]
                for piece, source in enumerate((high, middle, low)):
                    packed = jnp.where(lane == piece * heads + which, source[span], packed)
            tail = slice(heads * HEAD_DIM, heads * HEAD_DIM + LANES)
            if old_head:
                packed = packed + out[:, tail].astype(f32)
            out[:, tail] = packed.astype(bf16)


def attend(partners, cache, key_pos, selected, queries, earlier=()):
    _, shard, cols = cache.shape
    rows = queries[0].shape[0]
    kv_heads = cols // (2 * HEAD_DIM)
    out_cols = queries[0].shape[1] + LANES
    tall = GROUP * rows
    keys = 2 * shard
    count = len(queries)
    vmem = pl.BlockSpec(memory_space=pltpu.VMEM)
    out = pl.pallas_call(
        functools.partial(attend_kernel, partners, len(earlier)),
        out_shape=[jax.ShapeDtypeStruct((rows, out_cols), bf16)] * (len(earlier) + count),
        in_specs=[vmem] * (3 + count + len(earlier)),
        out_specs=[vmem] * (len(earlier) + count),
        scratch_shapes=[
            pltpu.VMEM((2, tall, keys), f32),
            pltpu.VMEM((tall, keys), bf16),
            pltpu.VMEM((2, keys, LANES), bf16),
        ],
        compiler_params=pltpu.CompilerParams(vmem_limit_bytes=24 * MIB),
        cost_estimate=pl.CostEstimate(flops=1000, bytes_accessed=1000, transcendentals=0),
        name="attend",
    )(cache, key_pos, selected, *queries, *earlier)
    return list(out)


def finish_kernel(count, size, *refs):
    parts = refs[:count]
    weights = refs[count]
    outs = refs[count + 1 : count + 1 + size]
    (context,) = refs[count + 1 + size :]
    feat = context.shape[1]
    heads = feat // HEAD_DIM
    width = weights.shape[1] // size
    me = lax.axis_index("head")
    tails = [part[:, feat : feat + LANES].astype(f32) for part in parts]
    for head in range(heads):
        levels = []
        for tail in tails:
            pieces = [tail[:, piece * heads + head : piece * heads + head + 1] for piece in range(3)]
            levels.append(pieces[0] + pieces[1] + pieces[2])
        top = functools.reduce(jnp.maximum, levels)
        shares = [jnp.exp2(level - top) for level in levels]
        whole = functools.reduce(jnp.add, shares)
        span = slice(head * HEAD_DIM, (head + 1) * HEAD_DIM)
        mixed = functools.reduce(
            jnp.add, [(share / whole) * part[:, span].astype(f32) for share, part in zip(shares, parts)]
        )
        context[:, span] = mixed.astype(bf16)
    for turn in range(size):
        start = (me ^ turn) * width
        step = 256 if width % 256 == 0 else width
        for at in range(0, width, step):
            part = weights[:, pl.ds(pl.multiple_of(start + at, step), step)]
            outs[turn][:, at : at + step] = jnp.dot(
                context[...], part, preferred_element_type=f32
            ).astype(outs[turn].dtype)


def finish(parts, w_out, size):
    rows = parts[0].shape[0]
    feat, cols = w_out.shape
    width = cols // size
    vmem = pl.BlockSpec(memory_space=pltpu.VMEM)
    return pl.pallas_call(
        functools.partial(finish_kernel, len(parts), size),
        out_shape=[jax.ShapeDtypeStruct((rows, width), f32 if turn == 0 else bf16) for turn in range(size)],
        in_specs=[vmem] * (len(parts) + 1),
        out_specs=[vmem] * size,
        scratch_shapes=[
            pltpu.VMEM((rows, feat), bf16),
        ],
        compiler_params=pltpu.CompilerParams(vmem_limit_bytes=24 * MIB),
        cost_estimate=pl.CostEstimate(
            flops=2 * rows * feat * cols, bytes_accessed=2 * feat * cols, transcendentals=0
        ),
        name="finish",
    )(*parts, w_out)


def swap(value, axis, turn, size):
    return lax.ppermute(value, axis, [(at, at ^ turn) for at in range(size)])


def body(
    hidden, norm_gain, w_query, w_key, w_value, w_out, stored_kv, selected, prompt_order, store_slot
):
    seq_count = lax.axis_size("seq")
    head_count = lax.axis_size("head")
    rows = hidden.shape[0]
    shard, _, local_kv, _ = stored_kv.shape
    stored = stored_kv.reshape(-1, HEAD_DIM)
    query, kv, table = project(hidden, norm_gain, selected, w_query, w_key, w_value)
    turns = sorted(range(2, seq_count, 2), key=lambda turn: (bin(turn).count("1"), turn))
    first, second = turns[:2]
    stored, kv = lax.optimization_barrier((stored, kv))
    stored_other, kv_other = (swap(value, "seq", 1, seq_count) for value in (stored, kv))
    queries = {turn: swap(query, "seq", turn, seq_count) for turn in (first, second)}
    cache, key_pos, late = merge(
        prompt_order, store_slot, table, stored, stored_other, kv, kv_other, query
    )
    queries |= {turn: swap(late, "seq", turn, seq_count) for turn in turns[2:]}
    parts = [attend((0,), cache, key_pos, table, [query])[0]]
    for turn in turns[2:]:
        (part,) = attend((turn,), cache, key_pos, table, [queries[turn]])
        parts.append(swap(part, "seq", turn, seq_count))
    done = attend((first,), cache, key_pos, table, [queries[first]])
    done = attend((second,), cache, key_pos, table, [queries[second]], done)
    parts += [swap(part, "seq", turn, seq_count) for turn, part in zip((first, second), done)]
    blocks = finish(parts, w_out, head_count)
    total = blocks[0]
    arrived = [
        swap(blocks[turn], "head", turn, head_count) for turn in (*range(2, head_count), 1)
    ]
    for block in arrived:
        total = total + block.astype(f32)
    new_kv = kv.reshape(rows, 2, local_kv, HEAD_DIM)
    return (total.astype(bf16), new_kv)


def solution(mesh):
    in_specs = (
        P("seq", None),
        P(),
        P(None, "head"),
        P(None, "head"),
        P(None, "head"),
        P("head", None),
        P("seq", None, "head", None),
        P(),
        P(),
        P(),
    )
    out_specs = (P("seq", "head"), P("seq", None, "head", None))
    return jax.shard_map(body, mesh=mesh, in_specs=in_specs, out_specs=out_specs, check_vma=False)
```

```python
import functools
import math

import jax
import jax.numpy as jnp
import numpy as np
from jax import lax
from jax.experimental import pallas as pl
from jax.experimental.pallas import tpu as pltpu
from jax.sharding import PartitionSpec as P

HEADS = 32
KV_HEADS = 8
HEAD_DIM = 128
PASSAGE = 4096
GROUP = HEADS // KV_HEADS
MASKED = -1e30
LANES = 128
MIB = 1024 * 1024

bf16 = jnp.bfloat16
f32 = jnp.float32
NT = (((1,), (1,)), ((), ()))


def iota(shape, dim):
    return lax.broadcasted_iota(jnp.int32, shape, dim)


def column_of(row):
    n = row.shape[1]
    eye = iota((n, n), 0) == iota((n, n), 1)
    return jnp.sum(jnp.where(eye, row.astype(f32), 0.0), 1, keepdims=True)


def project_kernel(
    width, hidden_any, gain_any, selected_any, freq_any, wq_any, wk_any, wv_any, query, kv, table,
    hidden, gain, selected, freq, normed, weights, first_sem, sem,
):
    rows, feat = hidden.shape
    q_cols, k_cols, v_cols = wq_any.shape[1], wk_any.shape[1], wv_any.shape[1]
    pairs = ((hidden_any, hidden), (gain_any, gain), (selected_any, selected), (freq_any, freq))
    firsts = [
        pltpu.make_async_copy(source, target, first_sem.at[number])
        for number, (source, target) in enumerate(pairs)
    ]
    for copy in firsts:
        copy.start()
    chunks = []
    for source, count, base in ((wk_any, k_cols, 0), (wq_any, q_cols, k_cols), (wv_any, v_cols, k_cols + q_cols)):
        for at in range(0, count, width):
            chunks.append((source, at, base + at))
    copies = []
    for number, (source, at, place) in enumerate(chunks):
        copy = pltpu.make_async_copy(
            source.at[:, at : at + width], weights.at[:, place : place + width], sem.at[number]
        )
        copy.start(priority=1)
        copies.append(copy)
    for copy in firsts[1:]:
        copy.wait()
    total = selected.shape[0]
    me = lax.axis_index("seq")
    mine = iota((rows, total), 1) == iota((rows, total), 0) + me * rows
    listed = selected[...].reshape(1, total)
    positions = jnp.sum(jnp.where(mine, listed.astype(f32), 0.0), 1, keepdims=True)
    table[...] = jnp.full(table.shape, -1, jnp.int32)
    for at in range(total // rows):
        table[at : at + 1, 0:rows] = listed[:, at * rows : (at + 1) * rows]
    angle = positions * freq[...]
    cosine = jnp.cos(angle)
    sine = jnp.sin(angle)
    sine = jnp.where(iota(sine.shape, 1) < HEAD_DIM // 2, -sine, sine)
    firsts[0].wait()
    step = 16
    for at in range(0, rows, step):
        wide = hidden[at : at + step, :].astype(f32)
        mean = jnp.sum(wide * wide, 1, keepdims=True) * (1.0 / feat)
        normed[at : at + step, :] = (wide * lax.rsqrt(mean + 1e-5) * gain[...]).astype(bf16)
    for (source, at, place), copy in zip(chunks, copies):
        copy.wait()
        out = jnp.dot(normed[...], weights[:, place : place + width], preferred_element_type=f32)
        for head in range(0, width, HEAD_DIM):
            part = out[:, head : head + HEAD_DIM]
            if source is not wv_any:
                part = part * cosine + pltpu.roll(part, HEAD_DIM // 2, 1) * sine
            part = part.astype(bf16)
            if source is wq_any:
                query[:, at + head : at + head + HEAD_DIM] = part
            else:
                col = at + head + (0 if source is wk_any else k_cols)
                kv[:, col : col + HEAD_DIM] = part


def project(hidden, gain, selected, wq, wk, wv):
    rows, feat = hidden.shape
    cols = wq.shape[1] + wk.shape[1] + wv.shape[1]
    width = math.gcd(math.gcd(wq.shape[1], wk.shape[1]), 256)
    freq = 500000.0 ** (-(np.arange(HEAD_DIM // 2, dtype=np.float32) * np.float32(2.0 / HEAD_DIM)))
    freq = jnp.asarray(np.concatenate([freq, freq])[None, :].astype(np.float32))
    vmem = pl.BlockSpec(memory_space=pltpu.VMEM)
    hbm = pl.BlockSpec(memory_space=pltpu.HBM)
    return pl.pallas_call(
        functools.partial(project_kernel, width),
        out_shape=(
            jax.ShapeDtypeStruct((rows, wq.shape[1]), bf16),
            jax.ShapeDtypeStruct((rows, wk.shape[1] + wv.shape[1]), bf16),
            jax.ShapeDtypeStruct((selected.shape[0] // rows, LANES), jnp.int32),
        ),
        in_specs=[hbm] * 7,
        out_specs=(vmem, vmem, vmem),
        scratch_shapes=[
            pltpu.VMEM((rows, feat), bf16),
            pltpu.VMEM((1, feat), f32),
            pltpu.VMEM(selected.shape, jnp.int32),
            pltpu.VMEM((1, HEAD_DIM), f32),
            pltpu.VMEM((rows, feat), bf16),
            pltpu.VMEM((feat, cols), bf16),
            pltpu.SemaphoreType.DMA((4,)),
            pltpu.SemaphoreType.DMA((cols // width,)),
        ],
        compiler_params=pltpu.CompilerParams(vmem_limit_bytes=48 * MIB),
        cost_estimate=pl.CostEstimate(
            flops=2 * rows * feat * cols, bytes_accessed=2 * feat * (cols + rows), transcendentals=0
        ),
        name="project",
    )(*[
        pltpu.with_memory_space_constraint(operand, pltpu.HBM)
        for operand in (hidden, gain.reshape(1, feat), selected, freq, wq, wk, wv)
    ])


def block_of(index, shard, order, slot):
    per = PASSAGE // shard
    own = index // per
    place = jnp.int32(0)
    for at in range(order.shape[0]):
        place = jnp.where(slot[order[at]] == own, at, place)
    return place * per + lax.rem(index, per)


def merge_kernel(
    order, slot, selected, stored, stored_other, kv, kv_other, query, cache, key_pos, passed, wide
):
    passed[...] = query[...]
    _, shard, cols = cache.shape
    kinds = cols // LANES
    rows = kv.shape[0]
    step = 128
    me = lax.axis_index("seq")
    for half in range(2):
        index = me ^ half
        block = block_of(index, shard, order, slot)
        holes = selected[pl.ds(block, 1), :] - block * shard
        offsets = column_of(selected[pl.ds(index, 1), :] - index * shard)
        high = jnp.floor(offsets * (1.0 / 32))
        low = offsets - 32 * high
        given = iota((LANES, 1), 0) < rows
        sources = [
            jnp.broadcast_to(jnp.where(given, value, 0.0), (LANES, LANES)).astype(bf16)
            for value in (high, low + 1)
        ]
        fresh = (kv, kv_other)[half][...]
        if rows < LANES:
            fresh = jnp.concatenate([fresh, jnp.zeros((LANES - rows, cols), bf16)], 0)
        source = jnp.concatenate(sources + [fresh], 1)
        for at in range(0, shard, step):
            places = iota((step, LANES), 0) + at
            hit = (places == holes).astype(f32).astype(bf16)
            picked = jnp.dot(hit, source, preferred_element_type=f32)
            mark = picked[:, LANES : 2 * LANES]
            hole = mark > 0.5
            key_pos[half * shard + at : half * shard + at + step, :] = jnp.where(
                hole,
                picked[:, :LANES] * 32 + (mark - 1) + (index * shard).astype(f32),
                (places + block * shard).astype(f32),
            )
            slot_at = (at // step) % 2
            wide[slot_at] = (stored, stored_other)[half][at * kinds : (at + step) * kinds, :].astype(f32)
            for kind in range(kinds):
                col = kind * LANES
                cache[half, at : at + step, col : col + LANES] = jnp.where(
                    hole,
                    picked[:, 2 * LANES + col : 3 * LANES + col],
                    wide[slot_at, pl.ds(kind, step, stride=kinds), :],
                ).astype(bf16)


def merge(order, slot, selected, stored, stored_other, kv, kv_other, query):
    cols = kv.shape[1]
    shard = stored.shape[0] * LANES // cols
    smem = pl.BlockSpec(memory_space=pltpu.SMEM)
    vmem = pl.BlockSpec(memory_space=pltpu.VMEM)
    return pl.pallas_call(
        merge_kernel,
        out_shape=(
            jax.ShapeDtypeStruct((2, shard, cols), bf16),
            jax.ShapeDtypeStruct((2 * shard, LANES), f32),
            jax.ShapeDtypeStruct(query.shape, query.dtype),
        ),
        in_specs=[smem, smem] + [vmem] * 6,
        out_specs=(vmem, vmem, vmem),
        scratch_shapes=[pltpu.VMEM((2, 128 * cols // LANES, LANES), f32)],
        compiler_params=pltpu.CompilerParams(vmem_limit_bytes=16 * MIB),
        cost_estimate=pl.CostEstimate(flops=1000, bytes_accessed=1000, transcendentals=0),
        name="merge",
    )(order, slot, selected, stored, stored_other, kv, kv_other, query)


def attend_kernel(partners, carried, *refs):
    count = len(partners)
    cache, key_pos, selected = refs[:3]
    queries = refs[3 : 3 + count]
    scores, weights, masks = refs[-3:]
    for source, target in zip(refs[3 + count :], refs[3 + count + carried : -3 - count]):
        target[...] = source[...]
    outs = refs[-3 - count : -3]
    _, shard, cols = cache.shape
    rows = queries[0].shape[0]
    kv_heads = cols // (2 * HEAD_DIM)
    heads = kv_heads * GROUP
    keys = 2 * shard
    step = 256
    scale = math.log2(math.e) / HEAD_DIM**0.5
    me = lax.axis_index("seq")
    one_hot = (iota((rows, LANES), 0) == iota((rows, LANES), 1)).astype(f32).astype(bf16)
    ones = jnp.ones((keys, LANES), bf16)

    def mask(at):
        even, odd = partners[at]
        row = selected[pl.ds(me ^ jnp.where(me & 1 == 1, odd, even), 1), :].astype(f32)
        for place in range(0, keys, step):
            masks[at % 2, place : place + step, :] = jnp.where(
                key_pos[place : place + step, :] <= row, 0.0, MASKED
            ).astype(bf16)

    def left(at, head):
        parts = []
        for member in range(GROUP):
            col = (head * GROUP + member) * HEAD_DIM
            parts.append(jnp.concatenate([queries[at][:, col : col + HEAD_DIM], one_hot], 1))
        return jnp.concatenate(parts, 0)

    def cached(place, size, kind, head):
        col = (kind * kv_heads + head) * HEAD_DIM
        return cache[place // shard, place % shard : place % shard + size, col : col + HEAD_DIM]

    units = [(at, head) for at in range(count) for head in range(kv_heads)]
    best = {}
    for number in range(len(units) + 1):
        if number < len(units):
            at, head = units[number]
            if head == 0:
                mask(at)
            stream = left(at, head)
        if number:
            old_at, old_head = units[number - 1]
            top = jnp.max(best.pop(number - 1), 1, keepdims=True) * scale
        running = None
        for place in range(0, keys, step):
            if number < len(units):
                right = jnp.concatenate(
                    [cached(place, step, 0, head), masks[at % 2, place : place + step, :]], 1
                )
                score = lax.dot_general(stream, right, NT, preferred_element_type=f32)
                scores[number % 2, :, place : place + step] = score
                for col in range(0, step, LANES):
                    part = score[:, col : col + LANES]
                    running = part if running is None else jnp.maximum(running, part)
            if number:
                slot = (number - 1) % 2
                weights[:, place : place + step] = jnp.exp2(
                    scores[slot, :, place : place + step] * scale - top
                ).astype(bf16)
        if number < len(units):
            best[number] = running
        if number:
            value = jnp.concatenate([cached(half * shard, shard, 1, old_head) for half in range(2)], 0)
            summed = jnp.dot(
                weights[...], jnp.concatenate([value, ones], 1), preferred_element_type=f32
            )
            total = summed[:, HEAD_DIM : HEAD_DIM + LANES]
            context = (summed[:, :HEAD_DIM] / total).astype(bf16)
            level = top + jnp.log2(total)
            high = level.astype(bf16).astype(f32)
            middle = (level - high).astype(bf16).astype(f32)
            low = level - high - middle
            lane = iota((rows, LANES), 1)
            out = outs[old_at]
            packed = jnp.zeros((rows, LANES), f32)
            for member in range(GROUP):
                which = old_head * GROUP + member
                span = slice(member * rows, (member + 1) * rows)
                out[:, which * HEAD_DIM : (which + 1) * HEAD_DIM] = context[span]
                for piece, source in enumerate((high, middle, low)):
                    packed = jnp.where(lane == piece * heads + which, source[span], packed)
            tail = slice(heads * HEAD_DIM, heads * HEAD_DIM + LANES)
            if old_head:
                packed = packed + out[:, tail].astype(f32)
            out[:, tail] = packed.astype(bf16)


def attend(partners, cache, key_pos, selected, queries, earlier=()):
    _, shard, cols = cache.shape
    rows = queries[0].shape[0]
    kv_heads = cols // (2 * HEAD_DIM)
    out_cols = queries[0].shape[1] + LANES
    tall = GROUP * rows
    keys = 2 * shard
    count = len(queries)
    vmem = pl.BlockSpec(memory_space=pltpu.VMEM)
    out = pl.pallas_call(
        functools.partial(attend_kernel, partners, len(earlier)),
        out_shape=[jax.ShapeDtypeStruct((rows, out_cols), bf16)] * (len(earlier) + count),
        in_specs=[vmem] * (3 + count + len(earlier)),
        out_specs=[vmem] * (len(earlier) + count),
        scratch_shapes=[
            pltpu.VMEM((2, tall, keys), f32),
            pltpu.VMEM((tall, keys), bf16),
            pltpu.VMEM((2, keys, LANES), bf16),
        ],
        compiler_params=pltpu.CompilerParams(vmem_limit_bytes=24 * MIB),
        cost_estimate=pl.CostEstimate(flops=1000, bytes_accessed=1000, transcendentals=0),
        name="attend",
    )(cache, key_pos, selected, *queries, *earlier)
    return list(out)


def finish_kernel(count, size, *refs):
    parts = refs[:count]
    weights = refs[count]
    outs = refs[count + 1 : count + 1 + size]
    (context,) = refs[count + 1 + size :]
    feat = context.shape[1]
    heads = feat // HEAD_DIM
    width = weights.shape[1] // size
    me = lax.axis_index("head")
    tails = [part[:, feat : feat + LANES].astype(f32) for part in parts]
    for head in range(heads):
        levels = []
        for tail in tails:
            pieces = [tail[:, piece * heads + head : piece * heads + head + 1] for piece in range(3)]
            levels.append(pieces[0] + pieces[1] + pieces[2])
        top = functools.reduce(jnp.maximum, levels)
        shares = [jnp.exp2(level - top) for level in levels]
        whole = functools.reduce(jnp.add, shares)
        span = slice(head * HEAD_DIM, (head + 1) * HEAD_DIM)
        mixed = functools.reduce(
            jnp.add, [(share / whole) * part[:, span].astype(f32) for share, part in zip(shares, parts)]
        )
        context[:, span] = mixed.astype(bf16)
    for turn in range(size):
        start = (me ^ turn) * width
        step = 256 if width % 256 == 0 else width
        for at in range(0, width, step):
            part = weights[:, pl.ds(pl.multiple_of(start + at, step), step)]
            outs[turn][:, at : at + step] = jnp.dot(
                context[...], part, preferred_element_type=f32
            ).astype(outs[turn].dtype)


def finish(parts, w_out, size):
    rows = parts[0].shape[0]
    feat, cols = w_out.shape
    width = cols // size
    vmem = pl.BlockSpec(memory_space=pltpu.VMEM)
    return pl.pallas_call(
        functools.partial(finish_kernel, len(parts), size),
        out_shape=[jax.ShapeDtypeStruct((rows, width), f32 if turn == 0 else bf16) for turn in range(size)],
        in_specs=[vmem] * (len(parts) + 1),
        out_specs=[vmem] * size,
        scratch_shapes=[
            pltpu.VMEM((rows, feat), bf16),
        ],
        compiler_params=pltpu.CompilerParams(vmem_limit_bytes=24 * MIB),
        cost_estimate=pl.CostEstimate(
            flops=2 * rows * feat * cols, bytes_accessed=2 * feat * cols, transcendentals=0
        ),
        name="finish",
    )(*parts, w_out)


def swap(value, axis, turn, size):
    even, odd = turn if isinstance(turn, tuple) else (turn, turn)
    return lax.ppermute(value, axis, [(at, at ^ (odd if at & 1 else even)) for at in range(size)])


def body(
    hidden, norm_gain, w_query, w_key, w_value, w_out, stored_kv, selected, prompt_order, store_slot
):
    seq_count = lax.axis_size("seq")
    head_count = lax.axis_size("head")
    rows = hidden.shape[0]
    shard, _, local_kv, _ = stored_kv.shape
    stored = stored_kv.reshape(-1, HEAD_DIM)
    query, kv, table = project(hidden, norm_gain, selected, w_query, w_key, w_value)
    turns = sorted(range(2, seq_count, 2), key=lambda turn: (bin(turn).count("1"), turn))
    near, across = turns[:2]
    first, second = (near, across), (across, near)
    rest = [(turn, turn) for turn in turns[2:]]
    stored, kv = lax.optimization_barrier((stored, kv))
    stored_other, kv_other = (swap(value, "seq", 1, seq_count) for value in (stored, kv))
    queries = {turn: swap(query, "seq", turn, seq_count) for turn in (first, second)}
    cache, key_pos, late = merge(
        prompt_order, store_slot, table, stored, stored_other, kv, kv_other, query
    )
    queries |= {turn: swap(late, "seq", turn, seq_count) for turn in rest}
    parts = [attend(((0, 0),), cache, key_pos, table, [query])[0]]
    for turn in rest:
        (part,) = attend((turn,), cache, key_pos, table, [queries[turn]])
        parts.append(swap(part, "seq", turn, seq_count))
    done = attend((first,), cache, key_pos, table, [queries[first]])
    done = attend((second,), cache, key_pos, table, [queries[second]], done)
    parts += [swap(part, "seq", turn, seq_count) for turn, part in zip((first, second), done)]
    blocks = finish(parts, w_out, head_count)
    total = blocks[0]
    arrived = [
        swap(blocks[turn], "head", turn, head_count) for turn in (*range(2, head_count), 1)
    ]
    for block in arrived:
        total = total + block.astype(f32)
    new_kv = kv.reshape(rows, 2, local_kv, HEAD_DIM)
    return (total.astype(bf16), new_kv)


def solution(mesh):
    in_specs = (
        P("seq", None),
        P(),
        P(None, "head"),
        P(None, "head"),
        P(None, "head"),
        P("head", None),
        P("seq", None, "head", None),
        P(),
        P(),
        P(),
    )
    out_specs = (P("seq", "head"), P("seq", None, "head", None))
    return jax.shard_map(body, mesh=mesh, in_specs=in_specs, out_specs=out_specs, check_vma=False)
```

```python
import functools
import math

import jax
import jax.numpy as jnp
import numpy as np
from jax import lax
from jax.experimental import pallas as pl
from jax.experimental.pallas import tpu as pltpu
from jax.sharding import PartitionSpec as P

HEADS = 32
KV_HEADS = 8
HEAD_DIM = 128
PASSAGE = 4096
GROUP = HEADS // KV_HEADS
MASKED = -1e30
LANES = 128
MIB = 1024 * 1024

bf16 = jnp.bfloat16
f32 = jnp.float32
NT = (((1,), (1,)), ((), ()))


def iota(shape, dim):
    return lax.broadcasted_iota(jnp.int32, shape, dim)


def column_of(row):
    n = row.shape[1]
    eye = iota((n, n), 0) == iota((n, n), 1)
    return jnp.sum(jnp.where(eye, row.astype(f32), 0.0), 1, keepdims=True)


def project_kernel(
    width, hidden_any, gain_any, selected_any, freq_any, wq_any, wk_any, wv_any, query, kv, table,
    hidden, gain, selected, freq, normed, weights, first_sem, sem,
):
    rows, feat = hidden.shape
    q_cols, k_cols, v_cols = wq_any.shape[1], wk_any.shape[1], wv_any.shape[1]
    pairs = ((hidden_any, hidden), (gain_any, gain), (selected_any, selected), (freq_any, freq))
    firsts = [
        pltpu.make_async_copy(source, target, first_sem.at[number])
        for number, (source, target) in enumerate(pairs)
    ]
    for copy in firsts:
        copy.start()
    chunks = []
    for source, count, base in ((wk_any, k_cols, 0), (wq_any, q_cols, k_cols), (wv_any, v_cols, k_cols + q_cols)):
        for at in range(0, count, width):
            chunks.append((source, at, base + at))
    copies = []
    for number, (source, at, place) in enumerate(chunks):
        copy = pltpu.make_async_copy(
            source.at[:, at : at + width], weights.at[:, place : place + width], sem.at[number]
        )
        copy.start(priority=1)
        copies.append(copy)
    for copy in firsts[1:]:
        copy.wait()
    total = selected.shape[0]
    me = lax.axis_index("seq")
    mine = iota((rows, total), 1) == iota((rows, total), 0) + me * rows
    listed = selected[...].reshape(1, total)
    positions = jnp.sum(jnp.where(mine, listed.astype(f32), 0.0), 1, keepdims=True)
    table[...] = jnp.full(table.shape, -1, jnp.int32)
    for at in range(total // rows):
        table[at : at + 1, 0:rows] = listed[:, at * rows : (at + 1) * rows]
    angle = positions * freq[...]
    cosine = jnp.cos(angle)
    sine = jnp.sin(angle)
    sine = jnp.where(iota(sine.shape, 1) < HEAD_DIM // 2, -sine, sine)
    firsts[0].wait()
    step = 16
    for at in range(0, rows, step):
        wide = hidden[at : at + step, :].astype(f32)
        mean = jnp.sum(wide * wide, 1, keepdims=True) * (1.0 / feat)
        normed[at : at + step, :] = (wide * lax.rsqrt(mean + 1e-5) * gain[...]).astype(bf16)
    for (source, at, place), copy in zip(chunks, copies):
        copy.wait()
        out = jnp.dot(normed[...], weights[:, place : place + width], preferred_element_type=f32)
        for head in range(0, width, HEAD_DIM):
            part = out[:, head : head + HEAD_DIM]
            if source is not wv_any:
                part = part * cosine + pltpu.roll(part, HEAD_DIM // 2, 1) * sine
            part = part.astype(bf16)
            if source is wq_any:
                query[:, at + head : at + head + HEAD_DIM] = part
            else:
                col = at + head + (0 if source is wk_any else k_cols)
                kv[:, col : col + HEAD_DIM] = part


def project(hidden, gain, selected, wq, wk, wv):
    rows, feat = hidden.shape
    cols = wq.shape[1] + wk.shape[1] + wv.shape[1]
    width = math.gcd(math.gcd(wq.shape[1], wk.shape[1]), 256)
    freq = 500000.0 ** (-(np.arange(HEAD_DIM // 2, dtype=np.float32) * np.float32(2.0 / HEAD_DIM)))
    freq = jnp.asarray(np.concatenate([freq, freq])[None, :].astype(np.float32))
    vmem = pl.BlockSpec(memory_space=pltpu.VMEM)
    hbm = pl.BlockSpec(memory_space=pltpu.HBM)
    return pl.pallas_call(
        functools.partial(project_kernel, width),
        out_shape=(
            jax.ShapeDtypeStruct((rows, wq.shape[1]), bf16),
            jax.ShapeDtypeStruct((rows, wk.shape[1] + wv.shape[1]), bf16),
            jax.ShapeDtypeStruct((selected.shape[0] // rows, LANES), jnp.int32),
        ),
        in_specs=[hbm] * 7,
        out_specs=(vmem, vmem, vmem),
        scratch_shapes=[
            pltpu.VMEM((rows, feat), bf16),
            pltpu.VMEM((1, feat), f32),
            pltpu.VMEM(selected.shape, jnp.int32),
            pltpu.VMEM((1, HEAD_DIM), f32),
            pltpu.VMEM((rows, feat), bf16),
            pltpu.VMEM((feat, cols), bf16),
            pltpu.SemaphoreType.DMA((4,)),
            pltpu.SemaphoreType.DMA((cols // width,)),
        ],
        compiler_params=pltpu.CompilerParams(vmem_limit_bytes=48 * MIB),
        cost_estimate=pl.CostEstimate(
            flops=2 * rows * feat * cols, bytes_accessed=2 * feat * (cols + rows), transcendentals=0
        ),
        name="project",
    )(*[
        pltpu.with_memory_space_constraint(operand, pltpu.HBM)
        for operand in (hidden, gain.reshape(1, feat), selected, freq, wq, wk, wv)
    ])


def block_of(index, shard, order, slot):
    per = PASSAGE // shard
    own = index // per
    place = jnp.int32(0)
    for at in range(order.shape[0]):
        place = jnp.where(slot[order[at]] == own, at, place)
    return place * per + lax.rem(index, per)


def merge_kernel(
    order, slot, selected, stored, stored_other, kv, kv_other, query, cache, key_pos, passed, wide
):
    passed[...] = query[...]
    _, shard, cols = cache.shape
    kinds = cols // LANES
    rows = kv.shape[0]
    step = 128
    me = lax.axis_index("seq")
    for half in range(2):
        index = me ^ half
        block = block_of(index, shard, order, slot)
        holes = selected[pl.ds(block, 1), :] - block * shard
        offsets = column_of(selected[pl.ds(index, 1), :] - index * shard)
        high = jnp.floor(offsets * (1.0 / 32))
        low = offsets - 32 * high
        given = iota((LANES, 1), 0) < rows
        sources = [
            jnp.broadcast_to(jnp.where(given, value, 0.0), (LANES, LANES)).astype(bf16)
            for value in (high, low + 1)
        ]
        fresh = (kv, kv_other)[half][...]
        if rows < LANES:
            fresh = jnp.concatenate([fresh, jnp.zeros((LANES - rows, cols), bf16)], 0)
        source = jnp.concatenate(sources + [fresh], 1)
        for at in range(0, shard, step):
            places = iota((step, LANES), 0) + at
            hit = (places == holes).astype(f32).astype(bf16)
            picked = jnp.dot(hit, source, preferred_element_type=f32)
            mark = picked[:, LANES : 2 * LANES]
            hole = mark > 0.5
            key_pos[half * shard + at : half * shard + at + step, :] = jnp.where(
                hole,
                picked[:, :LANES] * 32 + (mark - 1) + (index * shard).astype(f32),
                (places + block * shard).astype(f32),
            )
            slot_at = (at // step) % 2
            wide[slot_at] = (stored, stored_other)[half][at * kinds : (at + step) * kinds, :].astype(f32)
            for kind in range(kinds):
                col = kind * LANES
                cache[half, at : at + step, col : col + LANES] = jnp.where(
                    hole,
                    picked[:, 2 * LANES + col : 3 * LANES + col],
                    wide[slot_at, pl.ds(kind, step, stride=kinds), :],
                ).astype(bf16)


def merge(order, slot, selected, stored, stored_other, kv, kv_other, query):
    cols = kv.shape[1]
    shard = stored.shape[0] * LANES // cols
    smem = pl.BlockSpec(memory_space=pltpu.SMEM)
    vmem = pl.BlockSpec(memory_space=pltpu.VMEM)
    return pl.pallas_call(
        merge_kernel,
        out_shape=(
            jax.ShapeDtypeStruct((2, shard, cols), bf16),
            jax.ShapeDtypeStruct((2 * shard, LANES), f32),
            jax.ShapeDtypeStruct(query.shape, query.dtype),
        ),
        in_specs=[smem, smem] + [vmem] * 6,
        out_specs=(vmem, vmem, vmem),
        scratch_shapes=[pltpu.VMEM((2, 128 * cols // LANES, LANES), f32)],
        compiler_params=pltpu.CompilerParams(vmem_limit_bytes=16 * MIB),
        cost_estimate=pl.CostEstimate(flops=1000, bytes_accessed=1000, transcendentals=0),
        name="merge",
    )(order, slot, selected, stored, stored_other, kv, kv_other, query)


def attend_kernel(partners, carried, *refs):
    count = len(partners)
    cache, key_pos, selected = refs[:3]
    queries = refs[3 : 3 + count]
    scores, weights, masks = refs[-3:]
    for source, target in zip(refs[3 + count :], refs[3 + count + carried : -3 - count]):
        target[...] = source[...]
    outs = refs[-3 - count : -3]
    _, shard, cols = cache.shape
    rows = queries[0].shape[0]
    kv_heads = cols // (2 * HEAD_DIM)
    heads = kv_heads * GROUP
    keys = 2 * shard
    step = 256
    scale = math.log2(math.e) / HEAD_DIM**0.5
    me = lax.axis_index("seq")
    one_hot = (iota((rows, LANES), 0) == iota((rows, LANES), 1)).astype(f32).astype(bf16)
    ones = jnp.ones((keys, LANES), bf16)

    def mask(at):
        even, odd = partners[at]
        row = selected[pl.ds(me ^ jnp.where(me & 1 == 1, odd, even), 1), :].astype(f32)
        for place in range(0, keys, step):
            masks[at % 2, place : place + step, :] = jnp.where(
                key_pos[place : place + step, :] <= row, 0.0, MASKED
            ).astype(bf16)

    def left(at, head):
        parts = []
        for member in range(GROUP):
            col = (head * GROUP + member) * HEAD_DIM
            parts.append(jnp.concatenate([queries[at][:, col : col + HEAD_DIM], one_hot], 1))
        return jnp.concatenate(parts, 0)

    def cached(place, size, kind, head):
        col = (kind * kv_heads + head) * HEAD_DIM
        return cache[place // shard, place % shard : place % shard + size, col : col + HEAD_DIM]

    units = [(at, head) for at in range(count) for head in range(kv_heads)]
    best = {}
    for number in range(len(units) + 1):
        if number < len(units):
            at, head = units[number]
            if head == 0:
                mask(at)
            stream = left(at, head)
        if number:
            old_at, old_head = units[number - 1]
            top = jnp.max(best.pop(number - 1), 1, keepdims=True) * scale
        running = None
        for place in range(0, keys, step):
            if number < len(units):
                right = jnp.concatenate(
                    [cached(place, step, 0, head), masks[at % 2, place : place + step, :]], 1
                )
                score = lax.dot_general(stream, right, NT, preferred_element_type=f32)
                scores[number % 2, :, place : place + step] = score
                for col in range(0, step, LANES):
                    part = score[:, col : col + LANES]
                    running = part if running is None else jnp.maximum(running, part)
            if number:
                slot = (number - 1) % 2
                weights[:, place : place + step] = jnp.exp2(
                    scores[slot, :, place : place + step] * scale - top
                ).astype(bf16)
        if number < len(units):
            best[number] = running
        if number:
            value = jnp.concatenate([cached(half * shard, shard, 1, old_head) for half in range(2)], 0)
            summed = jnp.dot(
                weights[...], jnp.concatenate([value, ones], 1), preferred_element_type=f32
            )
            total = summed[:, HEAD_DIM : HEAD_DIM + LANES]
            context = (summed[:, :HEAD_DIM] / total).astype(bf16)
            level = top + jnp.log2(total)
            high = level.astype(bf16).astype(f32)
            middle = (level - high).astype(bf16).astype(f32)
            low = level - high - middle
            lane = iota((rows, LANES), 1)
            out = outs[old_at]
            packed = jnp.zeros((rows, LANES), f32)
            for member in range(GROUP):
                which = old_head * GROUP + member
                span = slice(member * rows, (member + 1) * rows)
                out[:, which * HEAD_DIM : (which + 1) * HEAD_DIM] = context[span]
                for piece, source in enumerate((high, middle, low)):
                    packed = jnp.where(lane == piece * heads + which, source[span], packed)
            tail = slice(heads * HEAD_DIM, heads * HEAD_DIM + LANES)
            if old_head:
                packed = packed + out[:, tail].astype(f32)
            out[:, tail] = packed.astype(bf16)


def attend(partners, cache, key_pos, selected, queries, earlier=()):
    _, shard, cols = cache.shape
    rows = queries[0].shape[0]
    kv_heads = cols // (2 * HEAD_DIM)
    out_cols = queries[0].shape[1] + LANES
    tall = GROUP * rows
    keys = 2 * shard
    count = len(queries)
    vmem = pl.BlockSpec(memory_space=pltpu.VMEM)
    out = pl.pallas_call(
        functools.partial(attend_kernel, partners, len(earlier)),
        out_shape=[jax.ShapeDtypeStruct((rows, out_cols), bf16)] * (len(earlier) + count),
        in_specs=[vmem] * (3 + count + len(earlier)),
        out_specs=[vmem] * (len(earlier) + count),
        scratch_shapes=[
            pltpu.VMEM((2, tall, keys), f32),
            pltpu.VMEM((tall, keys), bf16),
            pltpu.VMEM((2, keys, LANES), bf16),
        ],
        compiler_params=pltpu.CompilerParams(vmem_limit_bytes=24 * MIB),
        cost_estimate=pl.CostEstimate(flops=1000, bytes_accessed=1000, transcendentals=0),
        name="attend",
    )(cache, key_pos, selected, *queries, *earlier)
    return list(out)


def finish_kernel(count, size, *refs):
    parts = refs[:count]
    weights = refs[count]
    outs = refs[count + 1 : count + 1 + size]
    (context,) = refs[count + 1 + size :]
    feat = context.shape[1]
    heads = feat // HEAD_DIM
    width = weights.shape[1] // size
    me = lax.axis_index("head")
    tails = [part[:, feat : feat + LANES].astype(f32) for part in parts]
    for head in range(heads):
        levels = []
        for tail in tails:
            pieces = [tail[:, piece * heads + head : piece * heads + head + 1] for piece in range(3)]
            levels.append(pieces[0] + pieces[1] + pieces[2])
        top = functools.reduce(jnp.maximum, levels)
        shares = [jnp.exp2(level - top) for level in levels]
        whole = functools.reduce(jnp.add, shares)
        span = slice(head * HEAD_DIM, (head + 1) * HEAD_DIM)
        mixed = functools.reduce(
            jnp.add, [(share / whole) * part[:, span].astype(f32) for share, part in zip(shares, parts)]
        )
        context[:, span] = mixed.astype(bf16)
    for turn in range(size):
        start = (me ^ turn) * width
        step = 256 if width % 256 == 0 else width
        for at in range(0, width, step):
            part = weights[:, pl.ds(pl.multiple_of(start + at, step), step)]
            outs[turn][:, at : at + step] = jnp.dot(
                context[...], part, preferred_element_type=f32
            ).astype(outs[turn].dtype)


def finish(parts, w_out, size):
    rows = parts[0].shape[0]
    feat, cols = w_out.shape
    width = cols // size
    vmem = pl.BlockSpec(memory_space=pltpu.VMEM)
    return pl.pallas_call(
        functools.partial(finish_kernel, len(parts), size),
        out_shape=[jax.ShapeDtypeStruct((rows, width), f32 if turn == 0 else bf16) for turn in range(size)],
        in_specs=[vmem] * (len(parts) + 1),
        out_specs=[vmem] * size,
        scratch_shapes=[
            pltpu.VMEM((rows, feat), bf16),
        ],
        compiler_params=pltpu.CompilerParams(vmem_limit_bytes=24 * MIB),
        cost_estimate=pl.CostEstimate(
            flops=2 * rows * feat * cols, bytes_accessed=2 * feat * cols, transcendentals=0
        ),
        name="finish",
    )(*parts, w_out)


def swap(value, axis, turn, size):
    even, odd = turn if isinstance(turn, tuple) else (turn, turn)
    return lax.ppermute(value, axis, [(at, at ^ (odd if at & 1 else even)) for at in range(size)])


def sum_heads(blocks, size):
    if size != 4:
        arrived = [swap(blocks[turn], "head", turn, size) for turn in range(1, size)]
    else:
        me = lax.axis_index("head")
        ends = (me == 0) | (me == 3)
        far = lax.ppermute(blocks[3], "head", [(0, 3), (3, 0)])
        beside = swap(blocks[1], "head", 1, size)
        step = lax.ppermute(blocks[2], "head", [(0, 1), (1, 3), (3, 2), (2, 0)])
        both = (blocks[3].astype(f32) + step.astype(f32)).astype(bf16)
        middle = lax.ppermute(both, "head", [(1, 2), (2, 1)])
        arrived = [far, beside, jnp.where(ends, step, middle)]
    total = blocks[0]
    for block in arrived:
        total = total + block.astype(f32)
    return total.astype(bf16)


def body(
    hidden, norm_gain, w_query, w_key, w_value, w_out, stored_kv, selected, prompt_order, store_slot
):
    seq_count = lax.axis_size("seq")
    head_count = lax.axis_size("head")
    rows = hidden.shape[0]
    shard, _, local_kv, _ = stored_kv.shape
    stored = stored_kv.reshape(-1, HEAD_DIM)
    query, kv, table = project(hidden, norm_gain, selected, w_query, w_key, w_value)
    turns = sorted(range(2, seq_count, 2), key=lambda turn: (bin(turn).count("1"), turn))
    near, across = turns[:2]
    first, second = (near, across), (across, near)
    rest = [(turn, turn) for turn in turns[2:]]
    stored, kv = lax.optimization_barrier((stored, kv))
    stored_other, kv_other = (swap(value, "seq", 1, seq_count) for value in (stored, kv))
    queries = {turn: swap(query, "seq", turn, seq_count) for turn in (first, second)}
    cache, key_pos, late = merge(
        prompt_order, store_slot, table, stored, stored_other, kv, kv_other, query
    )
    queries |= {turn: swap(late, "seq", turn, seq_count) for turn in rest}
    parts = [attend(((0, 0),), cache, key_pos, table, [query])[0]]
    for turn in rest:
        (part,) = attend((turn,), cache, key_pos, table, [queries[turn]])
        parts.append(swap(part, "seq", turn, seq_count))
    done = attend((first,), cache, key_pos, table, [queries[first]])
    done = attend((second,), cache, key_pos, table, [queries[second]], done)
    parts += [swap(part, "seq", turn, seq_count) for turn, part in zip((first, second), done)]
    blocks = finish(parts, w_out, head_count)
    total = sum_heads(blocks, head_count)
    new_kv = kv.reshape(rows, 2, local_kv, HEAD_DIM)
    return (total, new_kv)


def solution(mesh):
    in_specs = (
        P("seq", None),
        P(),
        P(None, "head"),
        P(None, "head"),
        P(None, "head"),
        P("head", None),
        P("seq", None, "head", None),
        P(),
        P(),
        P(),
    )
    out_specs = (P("seq", "head"), P("seq", None, "head", None))
    return jax.shard_map(body, mesh=mesh, in_specs=in_specs, out_specs=out_specs, check_vma=False)
```

```python
import functools
import math

import jax
import jax.numpy as jnp
import numpy as np
from jax import lax
from jax.experimental import pallas as pl
from jax.experimental.pallas import tpu as pltpu
from jax.sharding import PartitionSpec as P

HEADS = 32
KV_HEADS = 8
HEAD_DIM = 128
PASSAGE = 4096
GROUP = HEADS // KV_HEADS
MASKED = -1e30
LANES = 128
MIB = 1024 * 1024

bf16 = jnp.bfloat16
f32 = jnp.float32
NT = (((1,), (1,)), ((), ()))


def iota(shape, dim):
    return lax.broadcasted_iota(jnp.int32, shape, dim)


def column_of(row):
    n = row.shape[1]
    eye = iota((n, n), 0) == iota((n, n), 1)
    return jnp.sum(jnp.where(eye, row.astype(f32), 0.0), 1, keepdims=True)


def project_kernel(
    width, hidden_any, gain_any, selected_any, freq_any, wq_any, wk_any, wv_any, query, kv, table,
    hidden, gain, selected, freq, normed, weights, first_sem, sem,
):
    rows, feat = hidden.shape
    q_cols, k_cols, v_cols = wq_any.shape[1], wk_any.shape[1], wv_any.shape[1]
    pairs = ((hidden_any, hidden), (gain_any, gain), (selected_any, selected), (freq_any, freq))
    firsts = [
        pltpu.make_async_copy(source, target, first_sem.at[number])
        for number, (source, target) in enumerate(pairs)
    ]
    for copy in firsts:
        copy.start()
    chunks = []
    for source, count, base in ((wk_any, k_cols, 0), (wq_any, q_cols, k_cols), (wv_any, v_cols, k_cols + q_cols)):
        for at in range(0, count, width):
            chunks.append((source, at, base + at))
    copies = []
    for number, (source, at, place) in enumerate(chunks):
        copy = pltpu.make_async_copy(
            source.at[:, at : at + width], weights.at[:, place : place + width], sem.at[number]
        )
        copy.start(priority=1)
        copies.append(copy)
    for copy in firsts[1:]:
        copy.wait()
    total = selected.shape[0]
    me = lax.axis_index("seq")
    mine = iota((rows, total), 1) == iota((rows, total), 0) + me * rows
    listed = selected[...].reshape(1, total)
    positions = jnp.sum(jnp.where(mine, listed.astype(f32), 0.0), 1, keepdims=True)
    table[...] = jnp.full(table.shape, -1, jnp.int32)
    for at in range(total // rows):
        table[at : at + 1, 0:rows] = listed[:, at * rows : (at + 1) * rows]
    angle = positions * freq[...]
    cosine = jnp.cos(angle)
    sine = jnp.sin(angle)
    sine = jnp.where(iota(sine.shape, 1) < HEAD_DIM // 2, -sine, sine)
    firsts[0].wait()
    step = 16
    for at in range(0, rows, step):
        wide = hidden[at : at + step, :].astype(f32)
        mean = jnp.sum(wide * wide, 1, keepdims=True) * (1.0 / feat)
        normed[at : at + step, :] = (wide * lax.rsqrt(mean + 1e-5) * gain[...]).astype(bf16)
    for (source, at, place), copy in zip(chunks, copies):
        copy.wait()
        out = jnp.dot(normed[...], weights[:, place : place + width], preferred_element_type=f32)
        for head in range(0, width, HEAD_DIM):
            part = out[:, head : head + HEAD_DIM]
            if source is not wv_any:
                part = part * cosine + pltpu.roll(part, HEAD_DIM // 2, 1) * sine
            part = part.astype(bf16)
            if source is wq_any:
                query[:, at + head : at + head + HEAD_DIM] = part
            else:
                col = at + head + (0 if source is wk_any else k_cols)
                kv[:, col : col + HEAD_DIM] = part


def project(hidden, gain, selected, wq, wk, wv):
    rows, feat = hidden.shape
    cols = wq.shape[1] + wk.shape[1] + wv.shape[1]
    width = math.gcd(math.gcd(wq.shape[1], wk.shape[1]), 256)
    freq = 500000.0 ** (-(np.arange(HEAD_DIM // 2, dtype=np.float32) * np.float32(2.0 / HEAD_DIM)))
    freq = jnp.asarray(np.concatenate([freq, freq])[None, :].astype(np.float32))
    vmem = pl.BlockSpec(memory_space=pltpu.VMEM)
    hbm = pl.BlockSpec(memory_space=pltpu.HBM)
    return pl.pallas_call(
        functools.partial(project_kernel, width),
        out_shape=(
            jax.ShapeDtypeStruct((rows, wq.shape[1]), bf16),
            jax.ShapeDtypeStruct((rows, wk.shape[1] + wv.shape[1]), bf16),
            jax.ShapeDtypeStruct((selected.shape[0] // rows, LANES), jnp.int32),
        ),
        in_specs=[hbm] * 7,
        out_specs=(vmem, vmem, vmem),
        scratch_shapes=[
            pltpu.VMEM((rows, feat), bf16),
            pltpu.VMEM((1, feat), f32),
            pltpu.VMEM(selected.shape, jnp.int32),
            pltpu.VMEM((1, HEAD_DIM), f32),
            pltpu.VMEM((rows, feat), bf16),
            pltpu.VMEM((feat, cols), bf16),
            pltpu.SemaphoreType.DMA((4,)),
            pltpu.SemaphoreType.DMA((cols // width,)),
        ],
        compiler_params=pltpu.CompilerParams(vmem_limit_bytes=48 * MIB),
        cost_estimate=pl.CostEstimate(
            flops=2 * rows * feat * cols, bytes_accessed=2 * feat * (cols + rows), transcendentals=0
        ),
        name="project",
    )(*[
        pltpu.with_memory_space_constraint(operand, pltpu.HBM)
        for operand in (hidden, gain.reshape(1, feat), selected, freq, wq, wk, wv)
    ])


def block_of(index, shard, order, slot):
    per = PASSAGE // shard
    own = index // per
    place = jnp.int32(0)
    for at in range(order.shape[0]):
        place = jnp.where(slot[order[at]] == own, at, place)
    return place * per + lax.rem(index, per)


def merge_kernel(
    order, slot, selected, stored, stored_other, kv, kv_other, query, cache, key_pos, passed, wide
):
    passed[...] = query[...]
    _, shard, cols = cache.shape
    kinds = cols // LANES
    rows = kv.shape[0]
    step = 128
    me = lax.axis_index("seq")
    for half in range(2):
        index = me ^ half
        block = block_of(index, shard, order, slot)
        holes = selected[pl.ds(block, 1), :] - block * shard
        offsets = column_of(selected[pl.ds(index, 1), :] - index * shard)
        high = jnp.floor(offsets * (1.0 / 32))
        low = offsets - 32 * high
        given = iota((LANES, 1), 0) < rows
        sources = [
            jnp.broadcast_to(jnp.where(given, value, 0.0), (LANES, LANES)).astype(bf16)
            for value in (high, low + 1)
        ]
        fresh = (kv, kv_other)[half][...]
        if rows < LANES:
            fresh = jnp.concatenate([fresh, jnp.zeros((LANES - rows, cols), bf16)], 0)
        source = jnp.concatenate(sources + [fresh], 1)
        for at in range(0, shard, step):
            places = iota((step, LANES), 0) + at
            hit = (places == holes).astype(f32).astype(bf16)
            picked = jnp.dot(hit, source, preferred_element_type=f32)
            mark = picked[:, LANES : 2 * LANES]
            hole = mark > 0.5
            key_pos[half * shard + at : half * shard + at + step, :] = jnp.where(
                hole,
                picked[:, :LANES] * 32 + (mark - 1) + (index * shard).astype(f32),
                (places + block * shard).astype(f32),
            )
            slot_at = (at // step) % 2
            wide[slot_at] = (stored, stored_other)[half][at * kinds : (at + step) * kinds, :].astype(f32)
            for kind in range(kinds):
                col = kind * LANES
                cache[half, at : at + step, col : col + LANES] = jnp.where(
                    hole,
                    picked[:, 2 * LANES + col : 3 * LANES + col],
                    wide[slot_at, pl.ds(kind, step, stride=kinds), :],
                ).astype(bf16)


def merge(order, slot, selected, stored, stored_other, kv, kv_other, query):
    cols = kv.shape[1]
    shard = stored.shape[0] * LANES // cols
    smem = pl.BlockSpec(memory_space=pltpu.SMEM)
    vmem = pl.BlockSpec(memory_space=pltpu.VMEM)
    return pl.pallas_call(
        merge_kernel,
        out_shape=(
            jax.ShapeDtypeStruct((2, shard, cols), bf16),
            jax.ShapeDtypeStruct((2 * shard, LANES), f32),
            jax.ShapeDtypeStruct(query.shape, query.dtype),
        ),
        in_specs=[smem, smem] + [vmem] * 6,
        out_specs=(vmem, vmem, vmem),
        scratch_shapes=[pltpu.VMEM((2, 128 * cols // LANES, LANES), f32)],
        compiler_params=pltpu.CompilerParams(vmem_limit_bytes=16 * MIB),
        cost_estimate=pl.CostEstimate(flops=1000, bytes_accessed=1000, transcendentals=0),
        name="merge",
    )(order, slot, selected, stored, stored_other, kv, kv_other, query)


def attend_kernel(partners, carried, *refs):
    count = len(partners)
    cache, key_pos, selected = refs[:3]
    queries = refs[3 : 3 + count]
    scores, weights, masks = refs[-3:]
    for source, target in zip(refs[3 + count :], refs[3 + count + carried : -3 - count]):
        target[...] = source[...]
    outs = refs[-3 - count : -3]
    _, shard, cols = cache.shape
    rows = queries[0].shape[0]
    kv_heads = cols // (2 * HEAD_DIM)
    heads = kv_heads * GROUP
    keys = 2 * shard
    step = 256
    scale = math.log2(math.e) / HEAD_DIM**0.5
    me = lax.axis_index("seq")
    one_hot = (iota((rows, LANES), 0) == iota((rows, LANES), 1)).astype(f32).astype(bf16)
    ones = jnp.ones((keys, LANES), bf16)

    def mask(at):
        even, odd = partners[at]
        row = selected[pl.ds(me ^ jnp.where(me & 1 == 1, odd, even), 1), :].astype(f32)
        for place in range(0, keys, step):
            masks[at % 2, place : place + step, :] = jnp.where(
                key_pos[place : place + step, :] <= row, 0.0, MASKED
            ).astype(bf16)

    def left(at, head):
        parts = []
        for member in range(GROUP):
            col = (head * GROUP + member) * HEAD_DIM
            parts.append(jnp.concatenate([queries[at][:, col : col + HEAD_DIM], one_hot], 1))
        return jnp.concatenate(parts, 0)

    def cached(place, size, kind, head):
        col = (kind * kv_heads + head) * HEAD_DIM
        return cache[place // shard, place % shard : place % shard + size, col : col + HEAD_DIM]

    units = [(at, head) for at in range(count) for head in range(kv_heads)]
    best = {}
    for number in range(len(units) + 1):
        if number < len(units):
            at, head = units[number]
            if head == 0:
                mask(at)
            stream = left(at, head)
        if number:
            old_at, old_head = units[number - 1]
            top = jnp.max(best.pop(number - 1), 1, keepdims=True) * scale
        running = None
        for place in range(0, keys, step):
            if number < len(units):
                right = jnp.concatenate(
                    [cached(place, step, 0, head), masks[at % 2, place : place + step, :]], 1
                )
                score = lax.dot_general(stream, right, NT, preferred_element_type=f32)
                scores[number % 2, :, place : place + step] = score
                for col in range(0, step, LANES):
                    part = score[:, col : col + LANES]
                    running = part if running is None else jnp.maximum(running, part)
            if number:
                slot = (number - 1) % 2
                weights[:, place : place + step] = jnp.exp2(
                    scores[slot, :, place : place + step] * scale - top
                ).astype(bf16)
        if number < len(units):
            best[number] = running
        if number:
            value = jnp.concatenate([cached(half * shard, shard, 1, old_head) for half in range(2)], 0)
            summed = jnp.dot(
                weights[...], jnp.concatenate([value, ones], 1), preferred_element_type=f32
            )
            total = summed[:, HEAD_DIM : HEAD_DIM + LANES]
            context = (summed[:, :HEAD_DIM] / total).astype(bf16)
            level = top + jnp.log2(total)
            high = level.astype(bf16).astype(f32)
            middle = (level - high).astype(bf16).astype(f32)
            low = level - high - middle
            lane = iota((rows, LANES), 1)
            out = outs[old_at]
            packed = jnp.zeros((rows, LANES), f32)
            for member in range(GROUP):
                which = old_head * GROUP + member
                span = slice(member * rows, (member + 1) * rows)
                out[:, which * HEAD_DIM : (which + 1) * HEAD_DIM] = context[span]
                for piece, source in enumerate((high, middle, low)):
                    packed = jnp.where(lane == piece * heads + which, source[span], packed)
            tail = slice(heads * HEAD_DIM, heads * HEAD_DIM + LANES)
            if old_head:
                packed = packed + out[:, tail].astype(f32)
            out[:, tail] = packed.astype(bf16)


def attend(partners, cache, key_pos, selected, queries, earlier=()):
    _, shard, cols = cache.shape
    rows = queries[0].shape[0]
    kv_heads = cols // (2 * HEAD_DIM)
    out_cols = queries[0].shape[1] + LANES
    tall = GROUP * rows
    keys = 2 * shard
    count = len(queries)
    vmem = pl.BlockSpec(memory_space=pltpu.VMEM)
    out = pl.pallas_call(
        functools.partial(attend_kernel, partners, len(earlier)),
        out_shape=[jax.ShapeDtypeStruct((rows, out_cols), bf16)] * (len(earlier) + count),
        in_specs=[vmem] * (3 + count + len(earlier)),
        out_specs=[vmem] * (len(earlier) + count),
        scratch_shapes=[
            pltpu.VMEM((2, tall, keys), f32),
            pltpu.VMEM((tall, keys), bf16),
            pltpu.VMEM((2, keys, LANES), bf16),
        ],
        compiler_params=pltpu.CompilerParams(vmem_limit_bytes=24 * MIB),
        cost_estimate=pl.CostEstimate(flops=1000, bytes_accessed=1000, transcendentals=0),
        name="attend",
    )(cache, key_pos, selected, *queries, *earlier)
    return list(out)


def finish_kernel(count, size, *refs):
    parts = refs[:count]
    weights = refs[count]
    outs = refs[count + 1 : count + 1 + size]
    (context,) = refs[count + 1 + size :]
    feat = context.shape[1]
    heads = feat // HEAD_DIM
    width = weights.shape[1] // size
    me = lax.axis_index("head")
    tails = [part[:, feat : feat + LANES].astype(f32) for part in parts]
    for head in range(heads):
        levels = []
        for tail in tails:
            pieces = [tail[:, piece * heads + head : piece * heads + head + 1] for piece in range(3)]
            levels.append(pieces[0] + pieces[1] + pieces[2])
        top = functools.reduce(jnp.maximum, levels)
        shares = [jnp.exp2(level - top) for level in levels]
        whole = functools.reduce(jnp.add, shares)
        span = slice(head * HEAD_DIM, (head + 1) * HEAD_DIM)
        mixed = functools.reduce(
            jnp.add, [(share / whole) * part[:, span].astype(f32) for share, part in zip(shares, parts)]
        )
        context[:, span] = mixed.astype(bf16)
    for turn in range(size):
        start = (me ^ turn) * width
        step = 256 if width % 256 == 0 else width
        for at in range(0, width, step):
            part = weights[:, pl.ds(pl.multiple_of(start + at, step), step)]
            outs[turn][:, at : at + step] = jnp.dot(
                context[...], part, preferred_element_type=f32
            ).astype(outs[turn].dtype)


def finish(parts, w_out, size):
    rows = parts[0].shape[0]
    feat, cols = w_out.shape
    width = cols // size
    vmem = pl.BlockSpec(memory_space=pltpu.VMEM)
    return pl.pallas_call(
        functools.partial(finish_kernel, len(parts), size),
        out_shape=[jax.ShapeDtypeStruct((rows, width), f32 if turn == 0 else bf16) for turn in range(size)],
        in_specs=[vmem] * (len(parts) + 1),
        out_specs=[vmem] * size,
        scratch_shapes=[
            pltpu.VMEM((rows, feat), bf16),
        ],
        compiler_params=pltpu.CompilerParams(vmem_limit_bytes=24 * MIB),
        cost_estimate=pl.CostEstimate(
            flops=2 * rows * feat * cols, bytes_accessed=2 * feat * cols, transcendentals=0
        ),
        name="finish",
    )(*parts, w_out)


def swap(value, axis, turn, size):
    even, odd = turn if isinstance(turn, tuple) else (turn, turn)
    return lax.ppermute(value, axis, [(at, at ^ (odd if at & 1 else even)) for at in range(size)])


def sum_heads(blocks, size):
    if size != 4:
        arrived = [swap(blocks[turn], "head", turn, size) for turn in range(1, size)]
    else:
        me = lax.axis_index("head")
        ends = (me == 0) | (me == 3)
        far = lax.ppermute(blocks[3], "head", [(0, 3), (3, 0)])
        step = lax.ppermute(blocks[2], "head", [(0, 1), (1, 3), (3, 2), (2, 0)])
        both = (blocks[3].astype(f32) + step.astype(f32)).astype(bf16)
        late, both = lax.optimization_barrier((blocks[1], both))
        middle = lax.ppermute(both, "head", [(1, 2), (2, 1)])
        beside = swap(late, "head", 1, size)
        arrived = [far, beside, jnp.where(ends, step, middle)]
    total = blocks[0]
    for block in arrived:
        total = total + block.astype(f32)
    return total.astype(bf16)


def body(
    hidden, norm_gain, w_query, w_key, w_value, w_out, stored_kv, selected, prompt_order, store_slot
):
    seq_count = lax.axis_size("seq")
    head_count = lax.axis_size("head")
    rows = hidden.shape[0]
    shard, _, local_kv, _ = stored_kv.shape
    stored = stored_kv.reshape(-1, HEAD_DIM)
    query, kv, table = project(hidden, norm_gain, selected, w_query, w_key, w_value)
    turns = sorted(range(2, seq_count, 2), key=lambda turn: (bin(turn).count("1"), turn))
    near, across = turns[:2]
    first, second = (near, across), (across, near)
    rest = [(turn, turn) for turn in turns[2:]]
    stored, kv = lax.optimization_barrier((stored, kv))
    stored_other, kv_other = (swap(value, "seq", 1, seq_count) for value in (stored, kv))
    queries = {turn: swap(query, "seq", turn, seq_count) for turn in (first, second)}
    cache, key_pos, late = merge(
        prompt_order, store_slot, table, stored, stored_other, kv, kv_other, query
    )
    queries |= {turn: swap(late, "seq", turn, seq_count) for turn in rest}
    parts = [attend(((0, 0),), cache, key_pos, table, [query])[0]]
    for turn in rest:
        (part,) = attend((turn,), cache, key_pos, table, [queries[turn]])
        parts.append(swap(part, "seq", turn, seq_count))
    done = attend((first,), cache, key_pos, table, [queries[first]])
    done = attend((second,), cache, key_pos, table, [queries[second]], done)
    parts += [swap(part, "seq", turn, seq_count) for turn, part in zip((first, second), done)]
    blocks = finish(parts, w_out, head_count)
    total = sum_heads(blocks, head_count)
    new_kv = kv.reshape(rows, 2, local_kv, HEAD_DIM)
    return (total, new_kv)


def solution(mesh):
    in_specs = (
        P("seq", None),
        P(),
        P(None, "head"),
        P(None, "head"),
        P(None, "head"),
        P("head", None),
        P("seq", None, "head", None),
        P(),
        P(),
        P(),
    )
    out_specs = (P("seq", "head"), P("seq", None, "head", None))
    return jax.shard_map(body, mesh=mesh, in_specs=in_specs, out_specs=out_specs, check_vma=False)
```

```python
import functools
import math

import jax
import jax.numpy as jnp
import numpy as np
from jax import lax
from jax.experimental import pallas as pl
from jax.experimental.pallas import tpu as pltpu
from jax.sharding import PartitionSpec as P

HEADS = 32
KV_HEADS = 8
HEAD_DIM = 128
PASSAGE = 4096
GROUP = HEADS // KV_HEADS
MASKED = -1e30
LANES = 128
MIB = 1024 * 1024

bf16 = jnp.bfloat16
f32 = jnp.float32
NT = (((1,), (1,)), ((), ()))


def iota(shape, dim):
    return lax.broadcasted_iota(jnp.int32, shape, dim)


def column_of(row):
    n = row.shape[1]
    eye = iota((n, n), 0) == iota((n, n), 1)
    return jnp.sum(jnp.where(eye, row.astype(f32), 0.0), 1, keepdims=True)


def project_kernel(
    width, hidden_any, gain_any, selected_any, freq_any, wq_any, wk_any, wv_any, query, kv, table,
    hidden, gain, selected, freq, normed, weights, first_sem, sem,
):
    rows, feat = hidden.shape
    q_cols, k_cols, v_cols = wq_any.shape[1], wk_any.shape[1], wv_any.shape[1]
    pairs = ((hidden_any, hidden), (gain_any, gain), (selected_any, selected), (freq_any, freq))
    firsts = [
        pltpu.make_async_copy(source, target, first_sem.at[number])
        for number, (source, target) in enumerate(pairs)
    ]
    for copy in firsts:
        copy.start()
    chunks = []
    for source, count, base in ((wk_any, k_cols, 0), (wq_any, q_cols, k_cols), (wv_any, v_cols, k_cols + q_cols)):
        for at in range(0, count, width):
            chunks.append((source, at, base + at))
    copies = []
    for number, (source, at, place) in enumerate(chunks):
        copy = pltpu.make_async_copy(
            source.at[:, at : at + width], weights.at[:, place : place + width], sem.at[number]
        )
        copy.start(priority=1)
        copies.append(copy)
    for copy in firsts[1:]:
        copy.wait()
    total = selected.shape[0]
    me = lax.axis_index("seq")
    mine = iota((rows, total), 1) == iota((rows, total), 0) + me * rows
    listed = selected[...].reshape(1, total)
    positions = jnp.sum(jnp.where(mine, listed.astype(f32), 0.0), 1, keepdims=True)
    table[...] = jnp.full(table.shape, -1, jnp.int32)
    for at in range(total // rows):
        table[at : at + 1, 0:rows] = listed[:, at * rows : (at + 1) * rows]
    angle = positions * freq[...]
    cosine = jnp.cos(angle)
    sine = jnp.sin(angle)
    sine = jnp.where(iota(sine.shape, 1) < HEAD_DIM // 2, -sine, sine)
    firsts[0].wait()
    step = 16
    for at in range(0, rows, step):
        wide = hidden[at : at + step, :].astype(f32)
        mean = jnp.sum(wide * wide, 1, keepdims=True) * (1.0 / feat)
        normed[at : at + step, :] = (wide * lax.rsqrt(mean + 1e-5) * gain[...]).astype(bf16)
    for (source, at, place), copy in zip(chunks, copies):
        copy.wait()
        out = jnp.dot(normed[...], weights[:, place : place + width], preferred_element_type=f32)
        for head in range(0, width, HEAD_DIM):
            part = out[:, head : head + HEAD_DIM]
            if source is not wv_any:
                part = part * cosine + pltpu.roll(part, HEAD_DIM // 2, 1) * sine
            part = part.astype(bf16)
            if source is wq_any:
                query[:, at + head : at + head + HEAD_DIM] = part
            else:
                col = at + head + (0 if source is wk_any else k_cols)
                kv[:, col : col + HEAD_DIM] = part


def project(hidden, gain, selected, wq, wk, wv):
    rows, feat = hidden.shape
    cols = wq.shape[1] + wk.shape[1] + wv.shape[1]
    width = math.gcd(math.gcd(wq.shape[1], wk.shape[1]), 256)
    freq = 500000.0 ** (-(np.arange(HEAD_DIM // 2, dtype=np.float32) * np.float32(2.0 / HEAD_DIM)))
    freq = jnp.asarray(np.concatenate([freq, freq])[None, :].astype(np.float32))
    vmem = pl.BlockSpec(memory_space=pltpu.VMEM)
    hbm = pl.BlockSpec(memory_space=pltpu.HBM)
    return pl.pallas_call(
        functools.partial(project_kernel, width),
        out_shape=(
            jax.ShapeDtypeStruct((rows, wq.shape[1]), bf16),
            jax.ShapeDtypeStruct((rows, wk.shape[1] + wv.shape[1]), bf16),
            jax.ShapeDtypeStruct((selected.shape[0] // rows, LANES), jnp.int32),
        ),
        in_specs=[hbm] * 7,
        out_specs=(vmem, vmem, vmem),
        scratch_shapes=[
            pltpu.VMEM((rows, feat), bf16),
            pltpu.VMEM((1, feat), f32),
            pltpu.VMEM(selected.shape, jnp.int32),
            pltpu.VMEM((1, HEAD_DIM), f32),
            pltpu.VMEM((rows, feat), bf16),
            pltpu.VMEM((feat, cols), bf16),
            pltpu.SemaphoreType.DMA((4,)),
            pltpu.SemaphoreType.DMA((cols // width,)),
        ],
        compiler_params=pltpu.CompilerParams(vmem_limit_bytes=48 * MIB),
        cost_estimate=pl.CostEstimate(
            flops=2 * rows * feat * cols, bytes_accessed=2 * feat * (cols + rows), transcendentals=0
        ),
        name="project",
    )(*[
        pltpu.with_memory_space_constraint(operand, pltpu.HBM)
        for operand in (hidden, gain.reshape(1, feat), selected, freq, wq, wk, wv)
    ])


def block_of(index, shard, order, slot):
    per = PASSAGE // shard
    own = index // per
    place = jnp.int32(0)
    for at in range(order.shape[0]):
        place = jnp.where(slot[order[at]] == own, at, place)
    return place * per + lax.rem(index, per)


def merge_kernel(
    order, slot, selected, stored, stored_other, kv, kv_other, query, cache, key_pos, passed, wide
):
    passed[...] = query[...]
    _, shard, cols = cache.shape
    kinds = cols // LANES
    rows = kv.shape[0]
    step = 128
    me = lax.axis_index("seq")
    for half in range(2):
        index = me ^ half
        block = block_of(index, shard, order, slot)
        holes = selected[pl.ds(block, 1), :] - block * shard
        offsets = column_of(selected[pl.ds(index, 1), :] - index * shard)
        high = jnp.floor(offsets * (1.0 / 32))
        low = offsets - 32 * high
        given = iota((LANES, 1), 0) < rows
        sources = [
            jnp.broadcast_to(jnp.where(given, value, 0.0), (LANES, LANES)).astype(bf16)
            for value in (high, low + 1)
        ]
        fresh = (kv, kv_other)[half][...]
        if rows < LANES:
            fresh = jnp.concatenate([fresh, jnp.zeros((LANES - rows, cols), bf16)], 0)
        source = jnp.concatenate(sources + [fresh], 1)
        for at in range(0, shard, step):
            places = iota((step, LANES), 0) + at
            hit = (places == holes).astype(f32).astype(bf16)
            picked = jnp.dot(hit, source, preferred_element_type=f32)
            mark = picked[:, LANES : 2 * LANES]
            hole = mark > 0.5
            key_pos[half * shard + at : half * shard + at + step, :] = jnp.where(
                hole,
                picked[:, :LANES] * 32 + (mark - 1) + (index * shard).astype(f32),
                (places + block * shard).astype(f32),
            )
            slot_at = (at // step) % 2
            wide[slot_at] = (stored, stored_other)[half][at * kinds : (at + step) * kinds, :].astype(f32)
            for kind in range(kinds):
                col = kind * LANES
                cache[half, at : at + step, col : col + LANES] = jnp.where(
                    hole,
                    picked[:, 2 * LANES + col : 3 * LANES + col],
                    wide[slot_at, pl.ds(kind, step, stride=kinds), :],
                ).astype(bf16)


def merge(order, slot, selected, stored, stored_other, kv, kv_other, query):
    cols = kv.shape[1]
    shard = stored.shape[0] * LANES // cols
    smem = pl.BlockSpec(memory_space=pltpu.SMEM)
    vmem = pl.BlockSpec(memory_space=pltpu.VMEM)
    return pl.pallas_call(
        merge_kernel,
        out_shape=(
            jax.ShapeDtypeStruct((2, shard, cols), bf16),
            jax.ShapeDtypeStruct((2 * shard, LANES), f32),
            jax.ShapeDtypeStruct(query.shape, query.dtype),
        ),
        in_specs=[smem, smem] + [vmem] * 6,
        out_specs=(vmem, vmem, vmem),
        scratch_shapes=[pltpu.VMEM((2, 128 * cols // LANES, LANES), f32)],
        compiler_params=pltpu.CompilerParams(vmem_limit_bytes=16 * MIB),
        cost_estimate=pl.CostEstimate(flops=1000, bytes_accessed=1000, transcendentals=0),
        name="merge",
    )(order, slot, selected, stored, stored_other, kv, kv_other, query)


def attend_kernel(partners, *refs):
    count = len(partners)
    cache, key_pos, selected = refs[:3]
    queries = refs[3 : 3 + count]
    outs = refs[3 + count : 3 + 2 * count]
    levels = refs[3 + 2 * count : 3 + 3 * count]
    scores, weights, masks = refs[3 + 3 * count :]
    _, shard, cols = cache.shape
    rows = queries[0].shape[0]
    kv_heads = cols // (2 * HEAD_DIM)
    heads = kv_heads * GROUP
    keys = 2 * shard
    step = 256
    scale = math.log2(math.e) / HEAD_DIM**0.5
    me = lax.axis_index("seq")
    diagonal = iota((rows, LANES), 0) == iota((rows, LANES), 1)
    one_hot = diagonal.astype(f32).astype(bf16)
    ones = jnp.ones((keys, LANES), bf16)

    def mask(at):
        even, odd = partners[at]
        row = selected[pl.ds(me ^ jnp.where(me & 1 == 1, odd, even), 1), :].astype(f32)
        for place in range(0, keys, step):
            masks[at % 2, place : place + step, :] = jnp.where(
                key_pos[place : place + step, :] <= row, 0.0, MASKED
            ).astype(bf16)

    def left(at, head):
        parts = []
        for member in range(GROUP):
            col = (head * GROUP + member) * HEAD_DIM
            parts.append(jnp.concatenate([queries[at][:, col : col + HEAD_DIM], one_hot], 1))
        return jnp.concatenate(parts, 0)

    def cached(place, size, kind, head):
        col = (kind * kv_heads + head) * HEAD_DIM
        return cache[place // shard, place % shard : place % shard + size, col : col + HEAD_DIM]

    units = [(at, head) for at in range(count) for head in range(kv_heads)]
    best = {}
    for number in range(len(units) + 1):
        if number < len(units):
            at, head = units[number]
            if head == 0:
                mask(at)
            stream = left(at, head)
        if number:
            old_at, old_head = units[number - 1]
            top = jnp.max(best.pop(number - 1), 1, keepdims=True) * scale
        running = None
        for place in range(0, keys, step):
            if number < len(units):
                right = jnp.concatenate(
                    [cached(place, step, 0, head), masks[at % 2, place : place + step, :]], 1
                )
                score = lax.dot_general(stream, right, NT, preferred_element_type=f32)
                scores[number % 2, :, place : place + step] = score
                for col in range(0, step, LANES):
                    part = score[:, col : col + LANES]
                    running = part if running is None else jnp.maximum(running, part)
            if number:
                slot = (number - 1) % 2
                weights[:, place : place + step] = jnp.exp2(
                    scores[slot, :, place : place + step] * scale - top
                ).astype(bf16)
        if number < len(units):
            best[number] = running
        if number:
            value = jnp.concatenate([cached(half * shard, shard, 1, old_head) for half in range(2)], 0)
            summed = jnp.dot(
                weights[...], jnp.concatenate([value, ones], 1), preferred_element_type=f32
            )
            total = summed[:, HEAD_DIM : HEAD_DIM + LANES]
            context = (summed[:, :HEAD_DIM] / total).astype(bf16)
            level = top + jnp.log2(total)
            for member in range(GROUP):
                which = old_head * GROUP + member
                span = slice(member * rows, (member + 1) * rows)
                outs[old_at][:, which * HEAD_DIM : (which + 1) * HEAD_DIM] = context[span]
                levels[old_at][which : which + 1, :] = jnp.sum(
                    jnp.where(diagonal, level[span], 0.0), 0, keepdims=True
                )


def attend(partners, cache, key_pos, selected, queries):
    _, shard, cols = cache.shape
    rows, q_cols = queries[0].shape
    tall = GROUP * rows
    keys = 2 * shard
    count = len(queries)
    vmem = pl.BlockSpec(memory_space=pltpu.VMEM)
    out = pl.pallas_call(
        functools.partial(attend_kernel, partners),
        out_shape=[jax.ShapeDtypeStruct((rows, q_cols), bf16)] * count
        + [jax.ShapeDtypeStruct((q_cols // HEAD_DIM, LANES), f32)] * count,
        in_specs=[vmem] * (3 + count),
        out_specs=[vmem] * (2 * count),
        scratch_shapes=[
            pltpu.VMEM((2, tall, keys), f32),
            pltpu.VMEM((tall, keys), bf16),
            pltpu.VMEM((2, keys, LANES), bf16),
        ],
        compiler_params=pltpu.CompilerParams(vmem_limit_bytes=24 * MIB),
        cost_estimate=pl.CostEstimate(flops=1000, bytes_accessed=1000, transcendentals=0),
        name="attend",
    )(cache, key_pos, selected, *queries)
    return list(zip(out[:count], out[count:]))


def finish_kernel(count, size, *refs):
    parts = refs[:count]
    levels = [ref[...] for ref in refs[count : 2 * count]]
    weights = refs[2 * count]
    outs = refs[2 * count + 1 : 2 * count + 1 + size]
    (context,) = refs[2 * count + 1 + size :]
    rows, feat = context.shape
    width = weights.shape[1] // size
    me = lax.axis_index("head")
    top = functools.reduce(jnp.maximum, levels)
    shares = [jnp.exp2(level - top) for level in levels]
    whole = functools.reduce(jnp.add, shares)
    shares = [jnp.transpose(share / whole) for share in shares]
    for head in range(feat // HEAD_DIM):
        span = slice(head * HEAD_DIM, (head + 1) * HEAD_DIM)
        mixed = functools.reduce(
            jnp.add,
            [share[:rows, head : head + 1] * part[:, span].astype(f32) for share, part in zip(shares, parts)],
        )
        context[:, span] = mixed.astype(bf16)
    for turn in range(size):
        start = (me ^ turn) * width
        step = 256 if width % 256 == 0 else width
        for at in range(0, width, step):
            part = weights[:, pl.ds(pl.multiple_of(start + at, step), step)]
            outs[turn][:, at : at + step] = jnp.dot(
                context[...], part, preferred_element_type=f32
            ).astype(outs[turn].dtype)


def finish(pairs, w_out, size):
    parts, levels = zip(*pairs)
    rows = parts[0].shape[0]
    feat, cols = w_out.shape
    width = cols // size
    vmem = pl.BlockSpec(memory_space=pltpu.VMEM)
    return pl.pallas_call(
        functools.partial(finish_kernel, len(parts), size),
        out_shape=[jax.ShapeDtypeStruct((rows, width), f32 if turn == 0 else bf16) for turn in range(size)],
        in_specs=[vmem] * (2 * len(parts) + 1),
        out_specs=[vmem] * size,
        scratch_shapes=[
            pltpu.VMEM((rows, feat), bf16),
        ],
        compiler_params=pltpu.CompilerParams(vmem_limit_bytes=24 * MIB),
        cost_estimate=pl.CostEstimate(
            flops=2 * rows * feat * cols, bytes_accessed=2 * feat * cols, transcendentals=0
        ),
        name="finish",
    )(*parts, *levels, w_out)


def swap(value, axis, turn, size):
    even, odd = turn if isinstance(turn, tuple) else (turn, turn)
    return lax.ppermute(value, axis, [(at, at ^ (odd if at & 1 else even)) for at in range(size)])


def sum_heads(blocks, size):
    if size != 4:
        arrived = [swap(blocks[turn], "head", turn, size) for turn in range(1, size)]
    else:
        me = lax.axis_index("head")
        ends = (me == 0) | (me == 3)
        step = lax.ppermute(blocks[2], "head", [(0, 1), (1, 3), (3, 2), (2, 0)])
        far = lax.ppermute(blocks[3], "head", [(0, 3), (3, 0)])
        beside = swap(blocks[1], "head", 1, size)
        both = (blocks[3].astype(f32) + step.astype(f32)).astype(bf16)
        middle = lax.ppermute(both, "head", [(1, 2), (2, 1)])
        arrived = [far, beside, jnp.where(ends, step, middle)]
    total = blocks[0]
    for block in arrived:
        total = total + block.astype(f32)
    return total.astype(bf16)


def body(
    hidden, norm_gain, w_query, w_key, w_value, w_out, stored_kv, selected, prompt_order, store_slot
):
    seq_count = lax.axis_size("seq")
    head_count = lax.axis_size("head")
    rows = hidden.shape[0]
    shard, _, local_kv, _ = stored_kv.shape
    stored = stored_kv.reshape(-1, HEAD_DIM)
    query, kv, table = project(hidden, norm_gain, selected, w_query, w_key, w_value)
    turns = sorted(range(2, seq_count, 2), key=lambda turn: (bin(turn).count("1"), turn))
    near, across = turns[:2]
    first, second = (near, across), (across, near)
    rest = [(turn, turn) for turn in turns[2:]]
    stored, kv = lax.optimization_barrier((stored, kv))
    stored_other, kv_other = (swap(value, "seq", 1, seq_count) for value in (stored, kv))
    queries = {turn: swap(query, "seq", turn, seq_count) for turn in (first, second)}
    cache, key_pos, late = merge(
        prompt_order, store_slot, table, stored, stored_other, kv, kv_other, query
    )
    queries |= {turn: swap(late, "seq", turn, seq_count) for turn in rest}
    pairs = attend(((0, 0),), cache, key_pos, table, [query])

    def give_back(turns):
        for turn, pair in zip(turns, attend(turns, cache, key_pos, table, [queries[turn] for turn in turns])):
            pairs.append(tuple(swap(value, "seq", turn, seq_count) for value in pair))

    for turn in rest:
        give_back((turn,))
    give_back((first, second))
    blocks = finish(pairs, w_out, head_count)
    total = sum_heads(blocks, head_count)
    new_kv = kv.reshape(rows, 2, local_kv, HEAD_DIM)
    return (total, new_kv)


def solution(mesh):
    in_specs = (
        P("seq", None),
        P(),
        P(None, "head"),
        P(None, "head"),
        P(None, "head"),
        P("head", None),
        P("seq", None, "head", None),
        P(),
        P(),
        P(),
    )
    out_specs = (P("seq", "head"), P("seq", None, "head", None))
    return jax.shard_map(body, mesh=mesh, in_specs=in_specs, out_specs=out_specs, check_vma=False)
```

```python
import functools
import math

import jax
import jax.numpy as jnp
import numpy as np
from jax import lax
from jax.experimental import pallas as pl
from jax.experimental.pallas import tpu as pltpu
from jax.sharding import PartitionSpec as P

HEADS = 32
KV_HEADS = 8
HEAD_DIM = 128
PASSAGE = 4096
GROUP = HEADS // KV_HEADS
MASKED = -1e30
LANES = 128
MIB = 1024 * 1024

bf16 = jnp.bfloat16
f32 = jnp.float32
NT = (((1,), (1,)), ((), ()))


def iota(shape, dim):
    return lax.broadcasted_iota(jnp.int32, shape, dim)


def column_of(row):
    n = row.shape[1]
    eye = iota((n, n), 0) == iota((n, n), 1)
    return jnp.sum(jnp.where(eye, row.astype(f32), 0.0), 1, keepdims=True)


def project_kernel(
    width, hidden_any, gain_any, selected_any, freq_any, wq_any, wk_any, wv_any, query, kv, table,
    hidden, gain, selected, freq, normed, weights, first_sem, sem,
):
    rows, feat = hidden.shape
    q_cols, k_cols, v_cols = wq_any.shape[1], wk_any.shape[1], wv_any.shape[1]
    pairs = ((hidden_any, hidden), (gain_any, gain), (selected_any, selected), (freq_any, freq))
    firsts = [
        pltpu.make_async_copy(source, target, first_sem.at[number])
        for number, (source, target) in enumerate(pairs)
    ]
    for copy in firsts:
        copy.start()
    chunks = []
    for source, count, base in ((wk_any, k_cols, 0), (wq_any, q_cols, k_cols), (wv_any, v_cols, k_cols + q_cols)):
        for at in range(0, count, width):
            chunks.append((source, at, base + at))
    copies = []
    for number, (source, at, place) in enumerate(chunks):
        copy = pltpu.make_async_copy(
            source.at[:, at : at + width], weights.at[:, place : place + width], sem.at[number]
        )
        copy.start(priority=1)
        copies.append(copy)
    for copy in firsts[1:]:
        copy.wait()
    total = selected.shape[0]
    me = lax.axis_index("seq")
    mine = iota((rows, total), 1) == iota((rows, total), 0) + me * rows
    listed = selected[...].reshape(1, total)
    positions = jnp.sum(jnp.where(mine, listed.astype(f32), 0.0), 1, keepdims=True)
    table[...] = jnp.full(table.shape, -1, jnp.int32)
    for at in range(total // rows):
        table[at : at + 1, 0:rows] = listed[:, at * rows : (at + 1) * rows]
    angle = positions * freq[...]
    cosine = jnp.cos(angle)
    sine = jnp.sin(angle)
    sine = jnp.where(iota(sine.shape, 1) < HEAD_DIM // 2, -sine, sine)
    firsts[0].wait()
    step = 16
    for at in range(0, rows, step):
        wide = hidden[at : at + step, :].astype(f32)
        mean = jnp.sum(wide * wide, 1, keepdims=True) * (1.0 / feat)
        normed[at : at + step, :] = (wide * lax.rsqrt(mean + 1e-5) * gain[...]).astype(bf16)
    for (source, at, place), copy in zip(chunks, copies):
        copy.wait()
        out = jnp.dot(normed[...], weights[:, place : place + width], preferred_element_type=f32)
        for head in range(0, width, HEAD_DIM):
            part = out[:, head : head + HEAD_DIM]
            if source is not wv_any:
                part = part * cosine + pltpu.roll(part, HEAD_DIM // 2, 1) * sine
            part = part.astype(bf16)
            if source is wq_any:
                query[:, at + head : at + head + HEAD_DIM] = part
            else:
                col = at + head + (0 if source is wk_any else k_cols)
                kv[:, col : col + HEAD_DIM] = part


def project(hidden, gain, selected, wq, wk, wv):
    rows, feat = hidden.shape
    cols = wq.shape[1] + wk.shape[1] + wv.shape[1]
    width = math.gcd(math.gcd(wq.shape[1], wk.shape[1]), 256)
    freq = 500000.0 ** (-(np.arange(HEAD_DIM // 2, dtype=np.float32) * np.float32(2.0 / HEAD_DIM)))
    freq = jnp.asarray(np.concatenate([freq, freq])[None, :].astype(np.float32))
    vmem = pl.BlockSpec(memory_space=pltpu.VMEM)
    hbm = pl.BlockSpec(memory_space=pltpu.HBM)
    return pl.pallas_call(
        functools.partial(project_kernel, width),
        out_shape=(
            jax.ShapeDtypeStruct((rows, wq.shape[1]), bf16),
            jax.ShapeDtypeStruct((rows, wk.shape[1] + wv.shape[1]), bf16),
            jax.ShapeDtypeStruct((selected.shape[0] // rows, LANES), jnp.int32),
        ),
        in_specs=[hbm] * 7,
        out_specs=(vmem, vmem, vmem),
        scratch_shapes=[
            pltpu.VMEM((rows, feat), bf16),
            pltpu.VMEM((1, feat), f32),
            pltpu.VMEM(selected.shape, jnp.int32),
            pltpu.VMEM((1, HEAD_DIM), f32),
            pltpu.VMEM((rows, feat), bf16),
            pltpu.VMEM((feat, cols), bf16),
            pltpu.SemaphoreType.DMA((4,)),
            pltpu.SemaphoreType.DMA((cols // width,)),
        ],
        compiler_params=pltpu.CompilerParams(vmem_limit_bytes=48 * MIB),
        cost_estimate=pl.CostEstimate(
            flops=2 * rows * feat * cols, bytes_accessed=2 * feat * (cols + rows), transcendentals=0
        ),
        name="project",
    )(*[
        pltpu.with_memory_space_constraint(operand, pltpu.HBM)
        for operand in (hidden, gain.reshape(1, feat), selected, freq, wq, wk, wv)
    ])


def block_of(index, shard, order, slot):
    per = PASSAGE // shard
    own = index // per
    place = jnp.int32(0)
    for at in range(order.shape[0]):
        place = jnp.where(slot[order[at]] == own, at, place)
    return place * per + lax.rem(index, per)


def merge_kernel(
    order, slot, selected, stored, stored_other, kv, kv_other, query, cache, key_pos, passed, wide
):
    passed[...] = query[...]
    _, shard, cols = cache.shape
    kinds = cols // LANES
    rows = kv.shape[0]
    step = 128
    me = lax.axis_index("seq")
    for half in range(2):
        index = me ^ half
        block = block_of(index, shard, order, slot)
        holes = selected[pl.ds(block, 1), :] - block * shard
        offsets = column_of(selected[pl.ds(index, 1), :] - index * shard)
        high = jnp.floor(offsets * (1.0 / 32))
        low = offsets - 32 * high
        given = iota((LANES, 1), 0) < rows
        sources = [
            jnp.broadcast_to(jnp.where(given, value, 0.0), (LANES, LANES)).astype(bf16)
            for value in (high, low + 1)
        ]
        fresh = (kv, kv_other)[half][...]
        if rows < LANES:
            fresh = jnp.concatenate([fresh, jnp.zeros((LANES - rows, cols), bf16)], 0)
        source = jnp.concatenate(sources + [fresh], 1)
        for at in range(0, shard, step):
            places = iota((step, LANES), 0) + at
            hit = (places == holes).astype(f32).astype(bf16)
            picked = jnp.dot(hit, source, preferred_element_type=f32)
            mark = picked[:, LANES : 2 * LANES]
            hole = mark > 0.5
            key_pos[half * shard + at : half * shard + at + step, :] = jnp.where(
                hole,
                picked[:, :LANES] * 32 + (mark - 1) + (index * shard).astype(f32),
                (places + block * shard).astype(f32),
            )
            slot_at = (at // step) % 2
            wide[slot_at] = (stored, stored_other)[half][at * kinds : (at + step) * kinds, :].astype(f32)
            for kind in range(kinds):
                col = kind * LANES
                cache[half, at : at + step, col : col + LANES] = jnp.where(
                    hole,
                    picked[:, 2 * LANES + col : 3 * LANES + col],
                    wide[slot_at, pl.ds(kind, step, stride=kinds), :],
                ).astype(bf16)


def merge(order, slot, selected, stored, stored_other, kv, kv_other, query):
    cols = kv.shape[1]
    shard = stored.shape[0] * LANES // cols
    smem = pl.BlockSpec(memory_space=pltpu.SMEM)
    vmem = pl.BlockSpec(memory_space=pltpu.VMEM)
    return pl.pallas_call(
        merge_kernel,
        out_shape=(
            jax.ShapeDtypeStruct((2, shard, cols), bf16),
            jax.ShapeDtypeStruct((2 * shard, LANES), f32),
            jax.ShapeDtypeStruct(query.shape, query.dtype),
        ),
        in_specs=[smem, smem] + [vmem] * 6,
        out_specs=(vmem, vmem, vmem),
        scratch_shapes=[pltpu.VMEM((2, 128 * cols // LANES, LANES), f32)],
        compiler_params=pltpu.CompilerParams(vmem_limit_bytes=16 * MIB),
        cost_estimate=pl.CostEstimate(flops=1000, bytes_accessed=1000, transcendentals=0),
        name="merge",
    )(order, slot, selected, stored, stored_other, kv, kv_other, query)


def attend_kernel(partners, carried, *refs):
    count = len(partners)
    cache, key_pos, selected = refs[:3]
    queries = refs[3 : 3 + count]
    scores, weights, masks = refs[-3:]
    for source, target in zip(refs[3 + count :], refs[3 + count + carried : -3 - count]):
        target[...] = source[...]
    outs = refs[-3 - count : -3]
    _, shard, cols = cache.shape
    rows = queries[0].shape[0]
    kv_heads = cols // (2 * HEAD_DIM)
    heads = kv_heads * GROUP
    keys = 2 * shard
    step = 256
    scale = math.log2(math.e) / HEAD_DIM**0.5
    me = lax.axis_index("seq")
    one_hot = (iota((rows, LANES), 0) == iota((rows, LANES), 1)).astype(f32).astype(bf16)
    ones = jnp.ones((keys, LANES), bf16)

    def mask(at):
        even, odd = partners[at]
        row = selected[pl.ds(me ^ jnp.where(me & 1 == 1, odd, even), 1), :].astype(f32)
        for place in range(0, keys, step):
            masks[at % 2, place : place + step, :] = jnp.where(
                key_pos[place : place + step, :] <= row, 0.0, MASKED
            ).astype(bf16)

    def left(at, head):
        parts = []
        for member in range(GROUP):
            col = (head * GROUP + member) * HEAD_DIM
            parts.append(jnp.concatenate([queries[at][:, col : col + HEAD_DIM], one_hot], 1))
        return jnp.concatenate(parts, 0)

    def cached(place, size, kind, head):
        col = (kind * kv_heads + head) * HEAD_DIM
        return cache[place // shard, place % shard : place % shard + size, col : col + HEAD_DIM]

    units = [(at, head) for at in range(count) for head in range(kv_heads)]
    best = {}
    for number in range(len(units) + 1):
        if number < len(units):
            at, head = units[number]
            if head == 0:
                mask(at)
            stream = left(at, head)
        if number:
            old_at, old_head = units[number - 1]
            top = jnp.max(best.pop(number - 1), 1, keepdims=True) * scale
        running = None
        for place in range(0, keys, step):
            if number < len(units):
                right = jnp.concatenate(
                    [cached(place, step, 0, head), masks[at % 2, place : place + step, :]], 1
                )
                score = lax.dot_general(stream, right, NT, preferred_element_type=f32)
                scores[number % 2, :, place : place + step] = score
                for col in range(0, step, LANES):
                    part = score[:, col : col + LANES]
                    running = part if running is None else jnp.maximum(running, part)
            if number:
                slot = (number - 1) % 2
                weights[:, place : place + step] = jnp.exp2(
                    scores[slot, :, place : place + step] * scale - top
                ).astype(bf16)
        if number < len(units):
            best[number] = running
        if number:
            value = jnp.concatenate([cached(half * shard, shard, 1, old_head) for half in range(2)], 0)
            summed = jnp.dot(
                weights[...], jnp.concatenate([value, ones], 1), preferred_element_type=f32
            )
            total = summed[:, HEAD_DIM : HEAD_DIM + LANES]
            context = (summed[:, :HEAD_DIM] / total).astype(bf16)
            level = top + jnp.log2(total)
            high = level.astype(bf16).astype(f32)
            middle = (level - high).astype(bf16).astype(f32)
            low = level - high - middle
            lane = iota((rows, LANES), 1)
            out = outs[old_at]
            packed = jnp.zeros((rows, LANES), f32)
            for member in range(GROUP):
                which = old_head * GROUP + member
                span = slice(member * rows, (member + 1) * rows)
                out[:, which * HEAD_DIM : (which + 1) * HEAD_DIM] = context[span]
                for piece, source in enumerate((high, middle, low)):
                    packed = jnp.where(lane == piece * heads + which, source[span], packed)
            tail = slice(heads * HEAD_DIM, heads * HEAD_DIM + LANES)
            if old_head:
                packed = packed + out[:, tail].astype(f32)
            out[:, tail] = packed.astype(bf16)


def attend(partners, cache, key_pos, selected, queries, earlier=()):
    _, shard, cols = cache.shape
    rows = queries[0].shape[0]
    kv_heads = cols // (2 * HEAD_DIM)
    out_cols = queries[0].shape[1] + LANES
    tall = GROUP * rows
    keys = 2 * shard
    count = len(queries)
    vmem = pl.BlockSpec(memory_space=pltpu.VMEM)
    out = pl.pallas_call(
        functools.partial(attend_kernel, partners, len(earlier)),
        out_shape=[jax.ShapeDtypeStruct((rows, out_cols), bf16)] * (len(earlier) + count),
        in_specs=[vmem] * (3 + count + len(earlier)),
        out_specs=[vmem] * (len(earlier) + count),
        scratch_shapes=[
            pltpu.VMEM((2, tall, keys), f32),
            pltpu.VMEM((tall, keys), bf16),
            pltpu.VMEM((2, keys, LANES), bf16),
        ],
        compiler_params=pltpu.CompilerParams(vmem_limit_bytes=24 * MIB),
        cost_estimate=pl.CostEstimate(flops=1000, bytes_accessed=1000, transcendentals=0),
        name="attend",
    )(cache, key_pos, selected, *queries, *earlier)
    return list(out)


def finish_kernel(count, size, *refs):
    parts = refs[:count]
    weights = refs[count]
    outs = refs[count + 1 : count + 1 + size]
    (context,) = refs[count + 1 + size :]
    feat = context.shape[1]
    heads = feat // HEAD_DIM
    width = weights.shape[1] // size
    me = lax.axis_index("head")
    tails = [part[:, feat : feat + LANES].astype(f32) for part in parts]
    for head in range(heads):
        levels = []
        for tail in tails:
            pieces = [tail[:, piece * heads + head : piece * heads + head + 1] for piece in range(3)]
            levels.append(pieces[0] + pieces[1] + pieces[2])
        top = functools.reduce(jnp.maximum, levels)
        shares = [jnp.exp2(level - top) for level in levels]
        whole = functools.reduce(jnp.add, shares)
        span = slice(head * HEAD_DIM, (head + 1) * HEAD_DIM)
        mixed = functools.reduce(
            jnp.add, [(share / whole) * part[:, span].astype(f32) for share, part in zip(shares, parts)]
        )
        context[:, span] = mixed.astype(bf16)
    for turn in range(size):
        start = (me ^ turn) * width
        step = 256 if width % 256 == 0 else width
        for at in range(0, width, step):
            part = weights[:, pl.ds(pl.multiple_of(start + at, step), step)]
            outs[turn][:, at : at + step] = jnp.dot(
                context[...], part, preferred_element_type=f32
            ).astype(outs[turn].dtype)


def finish(parts, w_out, size):
    rows = parts[0].shape[0]
    feat, cols = w_out.shape
    width = cols // size
    vmem = pl.BlockSpec(memory_space=pltpu.VMEM)
    return pl.pallas_call(
        functools.partial(finish_kernel, len(parts), size),
        out_shape=[jax.ShapeDtypeStruct((rows, width), f32 if turn == 0 else bf16) for turn in range(size)],
        in_specs=[vmem] * (len(parts) + 1),
        out_specs=[vmem] * size,
        scratch_shapes=[
            pltpu.VMEM((rows, feat), bf16),
        ],
        compiler_params=pltpu.CompilerParams(vmem_limit_bytes=24 * MIB),
        cost_estimate=pl.CostEstimate(
            flops=2 * rows * feat * cols, bytes_accessed=2 * feat * cols, transcendentals=0
        ),
        name="finish",
    )(*parts, w_out)


def swap(value, axis, turn, size):
    even, odd = turn if isinstance(turn, tuple) else (turn, turn)
    return lax.ppermute(value, axis, [(at, at ^ (odd if at & 1 else even)) for at in range(size)])


def sum_heads(blocks, size):
    if size != 4:
        arrived = [swap(blocks[turn], "head", turn, size) for turn in range(1, size)]
    else:
        me = lax.axis_index("head")
        ends = (me == 0) | (me == 3)
        far = lax.ppermute(blocks[3], "head", [(0, 3), (3, 0)])
        beside = swap(blocks[1], "head", 1, size)
        step = lax.ppermute(blocks[2], "head", [(0, 1), (1, 3), (3, 2), (2, 0)])
        both = (blocks[3].astype(f32) + step.astype(f32)).astype(bf16)
        middle = lax.ppermute(both, "head", [(1, 2), (2, 1)])
        arrived = [far, beside, jnp.where(ends, step, middle)]
    total = blocks[0]
    for block in arrived:
        total = total + block.astype(f32)
    return total.astype(bf16)


def body(
    hidden, norm_gain, w_query, w_key, w_value, w_out, stored_kv, selected, prompt_order, store_slot
):
    seq_count = lax.axis_size("seq")
    head_count = lax.axis_size("head")
    rows = hidden.shape[0]
    shard, _, local_kv, _ = stored_kv.shape
    stored = stored_kv.reshape(-1, HEAD_DIM)
    query, kv, table = project(hidden, norm_gain, selected, w_query, w_key, w_value)
    turns = sorted(range(2, seq_count, 2), key=lambda turn: (bin(turn).count("1"), turn))
    near, across = turns[:2]
    first, second = (near, across), (across, near)
    rest = [(turn, turn) for turn in turns[2:]]
    stored_other, kv_other = (swap(value, "seq", 1, seq_count) for value in (stored, kv))
    queries = {turn: swap(query, "seq", turn, seq_count) for turn in (first, second)}
    cache, key_pos, late = merge(
        prompt_order, store_slot, table, stored, stored_other, kv, kv_other, query
    )
    queries |= {turn: swap(late, "seq", turn, seq_count) for turn in rest}
    parts = [attend(((0, 0),), cache, key_pos, table, [query])[0]]
    for turn in rest:
        (part,) = attend((turn,), cache, key_pos, table, [queries[turn]])
        parts.append(swap(part, "seq", turn, seq_count))
    done = attend((first,), cache, key_pos, table, [queries[first]])
    done = attend((second,), cache, key_pos, table, [queries[second]], done)
    parts += [swap(part, "seq", turn, seq_count) for turn, part in zip((first, second), done)]
    blocks = finish(parts, w_out, head_count)
    total = sum_heads(blocks, head_count)
    new_kv = kv.reshape(rows, 2, local_kv, HEAD_DIM)
    return (total, new_kv)


def solution(mesh):
    in_specs = (
        P("seq", None),
        P(),
        P(None, "head"),
        P(None, "head"),
        P(None, "head"),
        P("head", None),
        P("seq", None, "head", None),
        P(),
        P(),
        P(),
    )
    out_specs = (P("seq", "head"), P("seq", None, "head", None))
    return jax.shard_map(body, mesh=mesh, in_specs=in_specs, out_specs=out_specs, check_vma=False)
```

```python
import functools
import math

import jax
import jax.numpy as jnp
import numpy as np
from jax import lax
from jax.experimental import pallas as pl
from jax.experimental.pallas import tpu as pltpu
from jax.sharding import PartitionSpec as P

HEADS = 32
KV_HEADS = 8
HEAD_DIM = 128
PASSAGE = 4096
GROUP = HEADS // KV_HEADS
MASKED = -1e30
LANES = 128
MIB = 1024 * 1024

bf16 = jnp.bfloat16
f32 = jnp.float32
NT = (((1,), (1,)), ((), ()))


def iota(shape, dim):
    return lax.broadcasted_iota(jnp.int32, shape, dim)


def column_of(row):
    n = row.shape[1]
    eye = iota((n, n), 0) == iota((n, n), 1)
    return jnp.sum(jnp.where(eye, row.astype(f32), 0.0), 1, keepdims=True)


def project_kernel(
    width, hidden_any, gain_any, selected_any, freq_any, wq_any, wk_any, wv_any, query, kv, table,
    hidden, gain, selected, freq, normed, weights, first_sem, sem,
):
    rows, feat = hidden.shape
    q_cols, k_cols, v_cols = wq_any.shape[1], wk_any.shape[1], wv_any.shape[1]
    pairs = ((hidden_any, hidden), (gain_any, gain), (selected_any, selected), (freq_any, freq))
    firsts = [
        pltpu.make_async_copy(source, target, first_sem.at[number])
        for number, (source, target) in enumerate(pairs)
    ]
    for copy in firsts:
        copy.start()
    chunks = []
    for source, count, base in ((wk_any, k_cols, 0), (wq_any, q_cols, k_cols), (wv_any, v_cols, k_cols + q_cols)):
        for at in range(0, count, width):
            chunks.append((source, at, base + at))
    copies = []
    for number, (source, at, place) in enumerate(chunks):
        copy = pltpu.make_async_copy(
            source.at[:, at : at + width], weights.at[:, place : place + width], sem.at[number]
        )
        copy.start(priority=1)
        copies.append(copy)
    for copy in firsts[1:]:
        copy.wait()
    total = selected.shape[0]
    me = lax.axis_index("seq")
    mine = iota((rows, total), 1) == iota((rows, total), 0) + me * rows
    listed = selected[...].reshape(1, total)
    positions = jnp.sum(jnp.where(mine, listed.astype(f32), 0.0), 1, keepdims=True)
    table[...] = jnp.full(table.shape, -1, jnp.int32)
    for at in range(total // rows):
        table[at : at + 1, 0:rows] = listed[:, at * rows : (at + 1) * rows]
    angle = positions * freq[...]
    cosine = jnp.cos(angle)
    sine = jnp.sin(angle)
    sine = jnp.where(iota(sine.shape, 1) < HEAD_DIM // 2, -sine, sine)
    firsts[0].wait()
    step = 16
    for at in range(0, rows, step):
        wide = hidden[at : at + step, :].astype(f32)
        mean = jnp.sum(wide * wide, 1, keepdims=True) * (1.0 / feat)
        normed[at : at + step, :] = (wide * lax.rsqrt(mean + 1e-5) * gain[...]).astype(bf16)
    for (source, at, place), copy in zip(chunks, copies):
        copy.wait()
        out = jnp.dot(normed[...], weights[:, place : place + width], preferred_element_type=f32)
        for head in range(0, width, HEAD_DIM):
            part = out[:, head : head + HEAD_DIM]
            if source is not wv_any:
                part = part * cosine + pltpu.roll(part, HEAD_DIM // 2, 1) * sine
            part = part.astype(bf16)
            if source is wq_any:
                query[:, at + head : at + head + HEAD_DIM] = part
            else:
                col = at + head + (0 if source is wk_any else k_cols)
                kv[:, col : col + HEAD_DIM] = part


def project(hidden, gain, selected, wq, wk, wv):
    rows, feat = hidden.shape
    cols = wq.shape[1] + wk.shape[1] + wv.shape[1]
    width = math.gcd(math.gcd(wq.shape[1], wk.shape[1]), 256)
    freq = 500000.0 ** (-(np.arange(HEAD_DIM // 2, dtype=np.float32) * np.float32(2.0 / HEAD_DIM)))
    freq = jnp.asarray(np.concatenate([freq, freq])[None, :].astype(np.float32))
    vmem = pl.BlockSpec(memory_space=pltpu.VMEM)
    hbm = pl.BlockSpec(memory_space=pltpu.HBM)
    return pl.pallas_call(
        functools.partial(project_kernel, width),
        out_shape=(
            jax.ShapeDtypeStruct((rows, wq.shape[1]), bf16),
            jax.ShapeDtypeStruct((rows, wk.shape[1] + wv.shape[1]), bf16),
            jax.ShapeDtypeStruct((selected.shape[0] // rows, LANES), jnp.int32),
        ),
        in_specs=[hbm] * 7,
        out_specs=(vmem, vmem, vmem),
        scratch_shapes=[
            pltpu.VMEM((rows, feat), bf16),
            pltpu.VMEM((1, feat), f32),
            pltpu.VMEM(selected.shape, jnp.int32),
            pltpu.VMEM((1, HEAD_DIM), f32),
            pltpu.VMEM((rows, feat), bf16),
            pltpu.VMEM((feat, cols), bf16),
            pltpu.SemaphoreType.DMA((4,)),
            pltpu.SemaphoreType.DMA((cols // width,)),
        ],
        compiler_params=pltpu.CompilerParams(vmem_limit_bytes=48 * MIB),
        cost_estimate=pl.CostEstimate(
            flops=2 * rows * feat * cols, bytes_accessed=2 * feat * (cols + rows), transcendentals=0
        ),
        name="project",
    )(*[
        pltpu.with_memory_space_constraint(operand, pltpu.HBM)
        for operand in (hidden, gain.reshape(1, feat), selected, freq, wq, wk, wv)
    ])


def block_of(index, shard, order, slot):
    per = PASSAGE // shard
    own = index // per
    place = jnp.int32(0)
    for at in range(order.shape[0]):
        place = jnp.where(slot[order[at]] == own, at, place)
    return place * per + lax.rem(index, per)


def merge_kernel(
    order, slot, selected, stored, stored_other, kv, kv_other, query, cache, key_pos, passed, wide
):
    passed[...] = query[...]
    _, shard, cols = cache.shape
    kinds = cols // LANES
    rows = kv.shape[0]
    step = 128
    me = lax.axis_index("seq")
    for half in range(2):
        index = me ^ half
        block = block_of(index, shard, order, slot)
        holes = selected[pl.ds(block, 1), :] - block * shard
        offsets = column_of(selected[pl.ds(index, 1), :] - index * shard)
        high = jnp.floor(offsets * (1.0 / 32))
        low = offsets - 32 * high
        given = iota((LANES, 1), 0) < rows
        sources = [
            jnp.broadcast_to(jnp.where(given, value, 0.0), (LANES, LANES)).astype(bf16)
            for value in (high, low + 1)
        ]
        fresh = (kv, kv_other)[half][...]
        if rows < LANES:
            fresh = jnp.concatenate([fresh, jnp.zeros((LANES - rows, cols), bf16)], 0)
        source = jnp.concatenate(sources + [fresh], 1)
        for at in range(0, shard, step):
            places = iota((step, LANES), 0) + at
            hit = (places == holes).astype(f32).astype(bf16)
            picked = jnp.dot(hit, source, preferred_element_type=f32)
            mark = picked[:, LANES : 2 * LANES]
            hole = mark > 0.5
            key_pos[half * shard + at : half * shard + at + step, :] = jnp.where(
                hole,
                picked[:, :LANES] * 32 + (mark - 1) + (index * shard).astype(f32),
                (places + block * shard).astype(f32),
            )
            slot_at = (at // step) % 2
            wide[slot_at] = (stored, stored_other)[half][at * kinds : (at + step) * kinds, :].astype(f32)
            for kind in range(kinds):
                col = kind * LANES
                cache[half, at : at + step, col : col + LANES] = jnp.where(
                    hole,
                    picked[:, 2 * LANES + col : 3 * LANES + col],
                    wide[slot_at, pl.ds(kind, step, stride=kinds), :],
                ).astype(bf16)


def merge(order, slot, selected, stored, stored_other, kv, kv_other, query):
    cols = kv.shape[1]
    shard = stored.shape[0] * LANES // cols
    smem = pl.BlockSpec(memory_space=pltpu.SMEM)
    vmem = pl.BlockSpec(memory_space=pltpu.VMEM)
    return pl.pallas_call(
        merge_kernel,
        out_shape=(
            jax.ShapeDtypeStruct((2, shard, cols), bf16),
            jax.ShapeDtypeStruct((2 * shard, LANES), f32),
            jax.ShapeDtypeStruct(query.shape, query.dtype),
        ),
        in_specs=[smem, smem] + [vmem] * 6,
        out_specs=(vmem, vmem, vmem),
        scratch_shapes=[pltpu.VMEM((2, 128 * cols // LANES, LANES), f32)],
        compiler_params=pltpu.CompilerParams(vmem_limit_bytes=16 * MIB),
        cost_estimate=pl.CostEstimate(flops=1000, bytes_accessed=1000, transcendentals=0),
        name="merge",
    )(order, slot, selected, stored, stored_other, kv, kv_other, query)


def attend_kernel(partners, carried, *refs):
    count = len(partners)
    cache, key_pos, selected = refs[:3]
    queries = refs[3 : 3 + count]
    scores, weights, masks = refs[-3:]
    for source, target in zip(refs[3 + count :], refs[3 + count + carried : -3 - count]):
        target[...] = source[...]
    outs = refs[-3 - count : -3]
    _, shard, cols = cache.shape
    rows = queries[0].shape[0]
    kv_heads = cols // (2 * HEAD_DIM)
    heads = kv_heads * GROUP
    keys = 2 * shard
    step = 256
    scale = math.log2(math.e) / HEAD_DIM**0.5
    me = lax.axis_index("seq")
    one_hot = (iota((rows, LANES), 0) == iota((rows, LANES), 1)).astype(f32).astype(bf16)
    ones = jnp.ones((keys, LANES), bf16)

    def mask(at):
        even, odd = partners[at]
        row = selected[pl.ds(me ^ jnp.where(me & 1 == 1, odd, even), 1), :].astype(f32)
        for place in range(0, keys, step):
            masks[at % 2, place : place + step, :] = jnp.where(
                key_pos[place : place + step, :] <= row, 0.0, MASKED
            ).astype(bf16)

    def left(at, head):
        parts = []
        for member in range(GROUP):
            col = (head * GROUP + member) * HEAD_DIM
            parts.append(jnp.concatenate([queries[at][:, col : col + HEAD_DIM], one_hot], 1))
        return jnp.concatenate(parts, 0)

    def cached(place, size, kind, head):
        col = (kind * kv_heads + head) * HEAD_DIM
        return cache[place // shard, place % shard : place % shard + size, col : col + HEAD_DIM]

    units = [(at, head) for at in range(count) for head in range(kv_heads)]
    best = {}
    for number in range(len(units) + 1):
        if number < len(units):
            at, head = units[number]
            if head == 0:
                mask(at)
            stream = left(at, head)
        if number:
            old_at, old_head = units[number - 1]
            top = jnp.max(best.pop(number - 1), 1, keepdims=True) * scale
        running = None
        for place in range(0, keys, step):
            if number < len(units):
                right = jnp.concatenate(
                    [cached(place, step, 0, head), masks[at % 2, place : place + step, :]], 1
                )
                score = lax.dot_general(stream, right, NT, preferred_element_type=f32)
                scores[number % 2, :, place : place + step] = score
                for col in range(0, step, LANES):
                    part = score[:, col : col + LANES]
                    running = part if running is None else jnp.maximum(running, part)
            if number:
                slot = (number - 1) % 2
                weights[:, place : place + step] = jnp.exp2(
                    scores[slot, :, place : place + step] * scale - top
                ).astype(bf16)
        if number < len(units):
            best[number] = running
        if number:
            value = jnp.concatenate([cached(half * shard, shard, 1, old_head) for half in range(2)], 0)
            summed = jnp.dot(
                weights[...], jnp.concatenate([value, ones], 1), preferred_element_type=f32
            )
            total = summed[:, HEAD_DIM : HEAD_DIM + LANES]
            context = (summed[:, :HEAD_DIM] / total).astype(bf16)
            level = top + jnp.log2(total)
            high = level.astype(bf16).astype(f32)
            middle = (level - high).astype(bf16).astype(f32)
            low = level - high - middle
            lane = iota((rows, LANES), 1)
            out = outs[old_at]
            packed = jnp.zeros((rows, LANES), f32)
            for member in range(GROUP):
                which = old_head * GROUP + member
                span = slice(member * rows, (member + 1) * rows)
                out[:, which * HEAD_DIM : (which + 1) * HEAD_DIM] = context[span]
                for piece, source in enumerate((high, middle, low)):
                    packed = jnp.where(lane == piece * heads + which, source[span], packed)
            tail = slice(heads * HEAD_DIM, heads * HEAD_DIM + LANES)
            if old_head:
                packed = packed + out[:, tail].astype(f32)
            out[:, tail] = packed.astype(bf16)


def attend(partners, cache, key_pos, selected, queries, earlier=()):
    _, shard, cols = cache.shape
    rows = queries[0].shape[0]
    kv_heads = cols // (2 * HEAD_DIM)
    out_cols = queries[0].shape[1] + LANES
    tall = GROUP * rows
    keys = 2 * shard
    count = len(queries)
    vmem = pl.BlockSpec(memory_space=pltpu.VMEM)
    out = pl.pallas_call(
        functools.partial(attend_kernel, partners, len(earlier)),
        out_shape=[jax.ShapeDtypeStruct((rows, out_cols), bf16)] * (len(earlier) + count),
        in_specs=[vmem] * (3 + count + len(earlier)),
        out_specs=[vmem] * (len(earlier) + count),
        scratch_shapes=[
            pltpu.VMEM((2, tall, keys), f32),
            pltpu.VMEM((tall, keys), bf16),
            pltpu.VMEM((2, keys, LANES), bf16),
        ],
        compiler_params=pltpu.CompilerParams(vmem_limit_bytes=24 * MIB),
        cost_estimate=pl.CostEstimate(flops=1000, bytes_accessed=1000, transcendentals=0),
        name="attend",
    )(cache, key_pos, selected, *queries, *earlier)
    return list(out)


def multiply(context, weights, turns, outs, size):
    width = weights.shape[1] // size
    step = 256 if width % 256 == 0 else width
    me = lax.axis_index("head")
    for turn, out in zip(turns, outs):
        start = (me ^ turn) * width
        for at in range(0, width, step):
            part = weights[:, pl.ds(pl.multiple_of(start + at, step), step)]
            out[:, at : at + step] = jnp.dot(
                context[...], part, preferred_element_type=f32
            ).astype(out.dtype)


def finish_kernel(count, turns, size, *refs):
    parts = refs[:count]
    weights = refs[count]
    context = refs[count + 1]
    feat = context.shape[1]
    heads = feat // HEAD_DIM
    tails = [part[:, feat : feat + LANES].astype(f32) for part in parts]
    for head in range(heads):
        levels = []
        for tail in tails:
            pieces = [tail[:, piece * heads + head : piece * heads + head + 1] for piece in range(3)]
            levels.append(pieces[0] + pieces[1] + pieces[2])
        top = functools.reduce(jnp.maximum, levels)
        shares = [jnp.exp2(level - top) for level in levels]
        whole = functools.reduce(jnp.add, shares)
        span = slice(head * HEAD_DIM, (head + 1) * HEAD_DIM)
        mixed = functools.reduce(
            jnp.add, [(share / whole) * part[:, span].astype(f32) for share, part in zip(shares, parts)]
        )
        context[:, span] = mixed.astype(bf16)
    multiply(context, weights, turns, refs[count + 2 :], size)


def more_kernel(turns, size, context, weights, *outs):
    multiply(context, weights, turns, outs, size)


def finish(parts, w_out, size):
    rows = parts[0].shape[0]
    feat, cols = w_out.shape
    vmem = pl.BlockSpec(memory_space=pltpu.VMEM)
    options = dict(
        compiler_params=pltpu.CompilerParams(vmem_limit_bytes=24 * MIB),
        cost_estimate=pl.CostEstimate(flops=1000, bytes_accessed=1000, transcendentals=0),
    )
    early, later = tuple(range(2, size)), (1, 0)

    def shape(turn):
        return jax.ShapeDtypeStruct((rows, cols // size), bf16 if turn else f32)

    context, *some = pl.pallas_call(
        functools.partial(finish_kernel, len(parts), early, size),
        out_shape=[jax.ShapeDtypeStruct((rows, feat), bf16)] + [shape(turn) for turn in early],
        in_specs=[vmem] * (len(parts) + 1),
        out_specs=[vmem] * (1 + len(early)),
        name="finish",
        **options,
    )(*parts, w_out)
    others = pl.pallas_call(
        functools.partial(more_kernel, later, size),
        out_shape=[shape(turn) for turn in later],
        in_specs=[vmem] * 2,
        out_specs=[vmem] * len(later),
        name="more",
        **options,
    )(context, w_out)
    return dict(zip(early + later, some + list(others)))


def swap(value, axis, turn, size):
    even, odd = turn if isinstance(turn, tuple) else (turn, turn)
    return lax.ppermute(value, axis, [(at, at ^ (odd if at & 1 else even)) for at in range(size)])


def sum_heads(blocks, size):
    if size != 4:
        arrived = [swap(blocks[turn], "head", turn, size) for turn in range(1, size)]
    else:
        me = lax.axis_index("head")
        ends = (me == 0) | (me == 3)
        far = lax.ppermute(blocks[3], "head", [(0, 3), (3, 0)])
        beside = swap(blocks[1], "head", 1, size)
        step = lax.ppermute(blocks[2], "head", [(0, 1), (1, 3), (3, 2), (2, 0)])
        both = (blocks[3].astype(f32) + step.astype(f32)).astype(bf16)
        middle = lax.ppermute(both, "head", [(1, 2), (2, 1)])
        arrived = [far, beside, jnp.where(ends, step, middle)]
    total = blocks[0]
    for block in arrived:
        total = total + block.astype(f32)
    return total.astype(bf16)


def body(
    hidden, norm_gain, w_query, w_key, w_value, w_out, stored_kv, selected, prompt_order, store_slot
):
    seq_count = lax.axis_size("seq")
    head_count = lax.axis_size("head")
    rows = hidden.shape[0]
    shard, _, local_kv, _ = stored_kv.shape
    stored = stored_kv.reshape(-1, HEAD_DIM)
    query, kv, table = project(hidden, norm_gain, selected, w_query, w_key, w_value)
    turns = sorted(range(2, seq_count, 2), key=lambda turn: (bin(turn).count("1"), turn))
    near, across = turns[:2]
    first, second = (near, across), (across, near)
    rest = [(turn, turn) for turn in turns[2:]]
    stored_other, kv_other = (swap(value, "seq", 1, seq_count) for value in (stored, kv))
    queries = {turn: swap(query, "seq", turn, seq_count) for turn in (first, second)}
    cache, key_pos, late = merge(
        prompt_order, store_slot, table, stored, stored_other, kv, kv_other, query
    )
    queries |= {turn: swap(late, "seq", turn, seq_count) for turn in rest}
    parts = [attend(((0, 0),), cache, key_pos, table, [query])[0]]
    for turn in rest:
        (part,) = attend((turn,), cache, key_pos, table, [queries[turn]])
        parts.append(swap(part, "seq", turn, seq_count))
    done = attend((first,), cache, key_pos, table, [queries[first]])
    done = attend((second,), cache, key_pos, table, [queries[second]], done)
    parts += [swap(part, "seq", turn, seq_count) for turn, part in zip((first, second), done)]
    blocks = finish(parts, w_out, head_count)
    total = sum_heads(blocks, head_count)
    new_kv = kv.reshape(rows, 2, local_kv, HEAD_DIM)
    return (total, new_kv)


def solution(mesh):
    in_specs = (
        P("seq", None),
        P(),
        P(None, "head"),
        P(None, "head"),
        P(None, "head"),
        P("head", None),
        P("seq", None, "head", None),
        P(),
        P(),
        P(),
    )
    out_specs = (P("seq", "head"), P("seq", None, "head", None))
    return jax.shard_map(body, mesh=mesh, in_specs=in_specs, out_specs=out_specs, check_vma=False)
```

```python
import functools
import math

import jax
import jax.numpy as jnp
import numpy as np
from jax import lax
from jax.experimental import pallas as pl
from jax.experimental.pallas import tpu as pltpu
from jax.sharding import PartitionSpec as P

HEADS = 32
KV_HEADS = 8
HEAD_DIM = 128
PASSAGE = 4096
GROUP = HEADS // KV_HEADS
MASKED = -1e30
LANES = 128
MIB = 1024 * 1024

bf16 = jnp.bfloat16
f32 = jnp.float32
NT = (((1,), (1,)), ((), ()))


def iota(shape, dim):
    return lax.broadcasted_iota(jnp.int32, shape, dim)


def column_of(row):
    n = row.shape[1]
    eye = iota((n, n), 0) == iota((n, n), 1)
    return jnp.sum(jnp.where(eye, row.astype(f32), 0.0), 1, keepdims=True)


def project_kernel(
    width, hidden_any, gain_any, selected_any, freq_any, wq_any, wk_any, wv_any, query, kv, table,
    hidden, gain, selected, freq, normed, weights, first_sem, sem,
):
    rows, feat = hidden.shape
    q_cols, k_cols, v_cols = wq_any.shape[1], wk_any.shape[1], wv_any.shape[1]
    pairs = ((hidden_any, hidden), (gain_any, gain), (selected_any, selected), (freq_any, freq))
    firsts = [
        pltpu.make_async_copy(source, target, first_sem.at[number])
        for number, (source, target) in enumerate(pairs)
    ]
    for copy in firsts:
        copy.start()
    chunks = []
    for source, count, base in ((wk_any, k_cols, 0), (wq_any, q_cols, k_cols), (wv_any, v_cols, k_cols + q_cols)):
        for at in range(0, count, width):
            chunks.append((source, at, base + at))
    copies = []
    for number, (source, at, place) in enumerate(chunks):
        copy = pltpu.make_async_copy(
            source.at[:, at : at + width], weights.at[:, place : place + width], sem.at[number]
        )
        copy.start(priority=1)
        copies.append(copy)
    for copy in firsts[1:]:
        copy.wait()
    total = selected.shape[0]
    me = lax.axis_index("seq")
    mine = iota((rows, total), 1) == iota((rows, total), 0) + me * rows
    listed = selected[...].reshape(1, total)
    positions = jnp.sum(jnp.where(mine, listed.astype(f32), 0.0), 1, keepdims=True)
    table[...] = jnp.full(table.shape, -1, jnp.int32)
    for at in range(total // rows):
        table[at : at + 1, 0:rows] = listed[:, at * rows : (at + 1) * rows]
    angle = positions * freq[...]
    cosine = jnp.cos(angle)
    sine = jnp.sin(angle)
    sine = jnp.where(iota(sine.shape, 1) < HEAD_DIM // 2, -sine, sine)
    firsts[0].wait()
    step = 16
    for at in range(0, rows, step):
        wide = hidden[at : at + step, :].astype(f32)
        mean = jnp.sum(wide * wide, 1, keepdims=True) * (1.0 / feat)
        normed[at : at + step, :] = (wide * lax.rsqrt(mean + 1e-5) * gain[...]).astype(bf16)
    for (source, at, place), copy in zip(chunks, copies):
        copy.wait()
        out = jnp.dot(normed[...], weights[:, place : place + width], preferred_element_type=f32)
        for head in range(0, width, HEAD_DIM):
            part = out[:, head : head + HEAD_DIM]
            if source is not wv_any:
                part = part * cosine + pltpu.roll(part, HEAD_DIM // 2, 1) * sine
            part = part.astype(bf16)
            if source is wq_any:
                query[:, at + head : at + head + HEAD_DIM] = part
            else:
                col = at + head + (0 if source is wk_any else k_cols)
                kv[:, col : col + HEAD_DIM] = part


def project(hidden, gain, selected, wq, wk, wv):
    rows, feat = hidden.shape
    cols = wq.shape[1] + wk.shape[1] + wv.shape[1]
    width = math.gcd(math.gcd(wq.shape[1], wk.shape[1]), 256)
    freq = 500000.0 ** (-(np.arange(HEAD_DIM // 2, dtype=np.float32) * np.float32(2.0 / HEAD_DIM)))
    freq = jnp.asarray(np.concatenate([freq, freq])[None, :].astype(np.float32))
    vmem = pl.BlockSpec(memory_space=pltpu.VMEM)
    hbm = pl.BlockSpec(memory_space=pltpu.HBM)
    return pl.pallas_call(
        functools.partial(project_kernel, width),
        out_shape=(
            jax.ShapeDtypeStruct((rows, wq.shape[1]), bf16),
            jax.ShapeDtypeStruct((rows, wk.shape[1] + wv.shape[1]), bf16),
            jax.ShapeDtypeStruct((selected.shape[0] // rows, LANES), jnp.int32),
        ),
        in_specs=[hbm] * 7,
        out_specs=(vmem, vmem, vmem),
        scratch_shapes=[
            pltpu.VMEM((rows, feat), bf16),
            pltpu.VMEM((1, feat), f32),
            pltpu.VMEM(selected.shape, jnp.int32),
            pltpu.VMEM((1, HEAD_DIM), f32),
            pltpu.VMEM((rows, feat), bf16),
            pltpu.VMEM((feat, cols), bf16),
            pltpu.SemaphoreType.DMA((4,)),
            pltpu.SemaphoreType.DMA((cols // width,)),
        ],
        compiler_params=pltpu.CompilerParams(vmem_limit_bytes=48 * MIB),
        cost_estimate=pl.CostEstimate(
            flops=2 * rows * feat * cols, bytes_accessed=2 * feat * (cols + rows), transcendentals=0
        ),
        name="project",
    )(*[
        pltpu.with_memory_space_constraint(operand, pltpu.HBM)
        for operand in (hidden, gain.reshape(1, feat), selected, freq, wq, wk, wv)
    ])


def block_of(index, shard, order, slot):
    per = PASSAGE // shard
    own = index // per
    place = jnp.int32(0)
    for at in range(order.shape[0]):
        place = jnp.where(slot[order[at]] == own, at, place)
    return place * per + lax.rem(index, per)


def merge_kernel(
    order, slot, selected, stored, stored_other, kv, kv_other, query, cache, key_pos, passed, wide
):
    passed[...] = query[...]
    _, shard, cols = cache.shape
    kinds = cols // LANES
    rows = kv.shape[0]
    step = 128
    me = lax.axis_index("seq")
    for half in range(2):
        index = me ^ half
        block = block_of(index, shard, order, slot)
        holes = selected[pl.ds(block, 1), :] - block * shard
        offsets = column_of(selected[pl.ds(index, 1), :] - index * shard)
        high = jnp.floor(offsets * (1.0 / 32))
        low = offsets - 32 * high
        given = iota((LANES, 1), 0) < rows
        sources = [
            jnp.broadcast_to(jnp.where(given, value, 0.0), (LANES, LANES)).astype(bf16)
            for value in (high, low + 1)
        ]
        fresh = (kv, kv_other)[half][...]
        if rows < LANES:
            fresh = jnp.concatenate([fresh, jnp.zeros((LANES - rows, cols), bf16)], 0)
        source = jnp.concatenate(sources + [fresh], 1)
        for at in range(0, shard, step):
            places = iota((step, LANES), 0) + at
            hit = (places == holes).astype(f32).astype(bf16)
            picked = jnp.dot(hit, source, preferred_element_type=f32)
            mark = picked[:, LANES : 2 * LANES]
            hole = mark > 0.5
            key_pos[half * shard + at : half * shard + at + step, :] = jnp.where(
                hole,
                picked[:, :LANES] * 32 + (mark - 1) + (index * shard).astype(f32),
                (places + block * shard).astype(f32),
            )
            slot_at = (at // step) % 2
            wide[slot_at] = (stored, stored_other)[half][at * kinds : (at + step) * kinds, :].astype(f32)
            for kind in range(kinds):
                col = kind * LANES
                cache[half, at : at + step, col : col + LANES] = jnp.where(
                    hole,
                    picked[:, 2 * LANES + col : 3 * LANES + col],
                    wide[slot_at, pl.ds(kind, step, stride=kinds), :],
                ).astype(bf16)


def merge(order, slot, selected, stored, stored_other, kv, kv_other, query):
    cols = kv.shape[1]
    shard = stored.shape[0] * LANES // cols
    smem = pl.BlockSpec(memory_space=pltpu.SMEM)
    vmem = pl.BlockSpec(memory_space=pltpu.VMEM)
    return pl.pallas_call(
        merge_kernel,
        out_shape=(
            jax.ShapeDtypeStruct((2, shard, cols), bf16),
            jax.ShapeDtypeStruct((2 * shard, LANES), f32),
            jax.ShapeDtypeStruct(query.shape, query.dtype),
        ),
        in_specs=[smem, smem] + [vmem] * 6,
        out_specs=(vmem, vmem, vmem),
        scratch_shapes=[pltpu.VMEM((2, 128 * cols // LANES, LANES), f32)],
        compiler_params=pltpu.CompilerParams(vmem_limit_bytes=16 * MIB),
        cost_estimate=pl.CostEstimate(flops=1000, bytes_accessed=1000, transcendentals=0),
        name="merge",
    )(order, slot, selected, stored, stored_other, kv, kv_other, query)


def attend_kernel(partners, carried, *refs):
    count = len(partners)
    cache, key_pos, selected = refs[:3]
    queries = refs[3 : 3 + count]
    scores, weights, masks = refs[-3:]
    for source, target in zip(refs[3 + count :], refs[3 + count + carried : -3 - count]):
        target[...] = source[...]
    outs = refs[-3 - count : -3]
    _, shard, cols = cache.shape
    rows = queries[0].shape[0]
    kv_heads = cols // (2 * HEAD_DIM)
    heads = kv_heads * GROUP
    keys = 2 * shard
    step = 256
    scale = math.log2(math.e) / HEAD_DIM**0.5
    me = lax.axis_index("seq")
    one_hot = (iota((rows, LANES), 0) == iota((rows, LANES), 1)).astype(f32).astype(bf16)
    ones = jnp.ones((keys, LANES), bf16)

    def mask(at):
        even, odd = partners[at]
        row = selected[pl.ds(me ^ jnp.where(me & 1 == 1, odd, even), 1), :].astype(f32)
        for place in range(0, keys, step):
            masks[at % 2, place : place + step, :] = jnp.where(
                key_pos[place : place + step, :] <= row, 0.0, MASKED
            ).astype(bf16)

    def left(at, head):
        parts = []
        for member in range(GROUP):
            col = (head * GROUP + member) * HEAD_DIM
            parts.append(jnp.concatenate([queries[at][:, col : col + HEAD_DIM], one_hot], 1))
        return jnp.concatenate(parts, 0)

    def cached(place, size, kind, head):
        col = (kind * kv_heads + head) * HEAD_DIM
        return cache[place // shard, place % shard : place % shard + size, col : col + HEAD_DIM]

    units = [(at, head) for at in range(count) for head in range(kv_heads)]
    best = {}
    for number in range(len(units) + 1):
        if number < len(units):
            at, head = units[number]
            if head == 0:
                mask(at)
            stream = left(at, head)
        if number:
            old_at, old_head = units[number - 1]
            top = jnp.max(best.pop(number - 1), 1, keepdims=True) * scale
        running = None
        for place in range(0, keys, step):
            if number < len(units):
                right = jnp.concatenate(
                    [cached(place, step, 0, head), masks[at % 2, place : place + step, :]], 1
                )
                score = lax.dot_general(stream, right, NT, preferred_element_type=f32)
                scores[number % 2, :, place : place + step] = score
                for col in range(0, step, LANES):
                    part = score[:, col : col + LANES]
                    running = part if running is None else jnp.maximum(running, part)
            if number:
                slot = (number - 1) % 2
                weights[:, place : place + step] = jnp.exp2(
                    scores[slot, :, place : place + step] * scale - top
                ).astype(bf16)
        if number < len(units):
            best[number] = running
        if number:
            value = jnp.concatenate([cached(half * shard, shard, 1, old_head) for half in range(2)], 0)
            summed = jnp.dot(
                weights[...], jnp.concatenate([value, ones], 1), preferred_element_type=f32
            )
            total = summed[:, HEAD_DIM : HEAD_DIM + LANES]
            context = (summed[:, :HEAD_DIM] / total).astype(bf16)
            level = top + jnp.log2(total)
            high = level.astype(bf16).astype(f32)
            middle = (level - high).astype(bf16).astype(f32)
            low = level - high - middle
            lane = iota((rows, LANES), 1)
            out = outs[old_at]
            packed = jnp.zeros((rows, LANES), f32)
            for member in range(GROUP):
                which = old_head * GROUP + member
                span = slice(member * rows, (member + 1) * rows)
                out[:, which * HEAD_DIM : (which + 1) * HEAD_DIM] = context[span]
                for piece, source in enumerate((high, middle, low)):
                    packed = jnp.where(lane == piece * heads + which, source[span], packed)
            tail = slice(heads * HEAD_DIM, heads * HEAD_DIM + LANES)
            if old_head:
                packed = packed + out[:, tail].astype(f32)
            out[:, tail] = packed.astype(bf16)


def attend(partners, cache, key_pos, selected, queries, earlier=()):
    _, shard, cols = cache.shape
    rows = queries[0].shape[0]
    kv_heads = cols // (2 * HEAD_DIM)
    out_cols = queries[0].shape[1] + LANES
    tall = GROUP * rows
    keys = 2 * shard
    count = len(queries)
    vmem = pl.BlockSpec(memory_space=pltpu.VMEM)
    out = pl.pallas_call(
        functools.partial(attend_kernel, partners, len(earlier)),
        out_shape=[jax.ShapeDtypeStruct((rows, out_cols), bf16)] * (len(earlier) + count),
        in_specs=[vmem] * (3 + count + len(earlier)),
        out_specs=[vmem] * (len(earlier) + count),
        scratch_shapes=[
            pltpu.VMEM((2, tall, keys), f32),
            pltpu.VMEM((tall, keys), bf16),
            pltpu.VMEM((2, keys, LANES), bf16),
        ],
        compiler_params=pltpu.CompilerParams(vmem_limit_bytes=24 * MIB),
        cost_estimate=pl.CostEstimate(flops=1000, bytes_accessed=1000, transcendentals=0),
        name="attend",
    )(cache, key_pos, selected, *queries, *earlier)
    return list(out)


def multiply(context, weights, turns, outs, size):
    width = weights.shape[1] // size
    step = 256 if width % 256 == 0 else width
    me = lax.axis_index("head")
    for turn, out in zip(turns, outs):
        start = (me ^ turn) * width
        for at in range(0, width, step):
            part = weights[:, pl.ds(pl.multiple_of(start + at, step), step)]
            out[:, at : at + step] = jnp.dot(
                context[...], part, preferred_element_type=f32
            ).astype(out.dtype)


def finish_kernel(count, turns, size, *refs):
    parts = refs[:count]
    weights = refs[count]
    context = refs[count + 1]
    feat = context.shape[1]
    heads = feat // HEAD_DIM
    tails = [part[:, feat : feat + LANES].astype(f32) for part in parts]
    for head in range(heads):
        levels = []
        for tail in tails:
            pieces = [tail[:, piece * heads + head : piece * heads + head + 1] for piece in range(3)]
            levels.append(pieces[0] + pieces[1] + pieces[2])
        top = functools.reduce(jnp.maximum, levels)
        shares = [jnp.exp2(level - top) for level in levels]
        whole = functools.reduce(jnp.add, shares)
        span = slice(head * HEAD_DIM, (head + 1) * HEAD_DIM)
        mixed = functools.reduce(
            jnp.add, [(share / whole) * part[:, span].astype(f32) for share, part in zip(shares, parts)]
        )
        context[:, span] = mixed.astype(bf16)
    multiply(context, weights, turns, refs[count + 2 :], size)


def more_kernel(turns, size, context, weights, *outs):
    multiply(context, weights, turns, outs, size)


def finish(parts, w_out, size):
    rows = parts[0].shape[0]
    feat, cols = w_out.shape
    vmem = pl.BlockSpec(memory_space=pltpu.VMEM)
    options = dict(
        compiler_params=pltpu.CompilerParams(vmem_limit_bytes=24 * MIB),
        cost_estimate=pl.CostEstimate(flops=1000, bytes_accessed=1000, transcendentals=0),
    )
    early, later = (2,), tuple(turn for turn in (3, 1, 0) if turn < size)

    def shape(turn):
        return jax.ShapeDtypeStruct((rows, cols // size), bf16 if turn else f32)

    context, *some = pl.pallas_call(
        functools.partial(finish_kernel, len(parts), early, size),
        out_shape=[jax.ShapeDtypeStruct((rows, feat), bf16)] + [shape(turn) for turn in early],
        in_specs=[vmem] * (len(parts) + 1),
        out_specs=[vmem] * (1 + len(early)),
        name="finish",
        **options,
    )(*parts, w_out)
    others = pl.pallas_call(
        functools.partial(more_kernel, later, size),
        out_shape=[shape(turn) for turn in later],
        in_specs=[vmem] * 2,
        out_specs=[vmem] * len(later),
        name="more",
        **options,
    )(context, w_out)
    return dict(zip(early + later, some + list(others)))


def swap(value, axis, turn, size):
    even, odd = turn if isinstance(turn, tuple) else (turn, turn)
    return lax.ppermute(value, axis, [(at, at ^ (odd if at & 1 else even)) for at in range(size)])


def sum_heads(blocks, size):
    if size != 4:
        arrived = [swap(blocks[turn], "head", turn, size) for turn in range(1, size)]
    else:
        me = lax.axis_index("head")
        ends = (me == 0) | (me == 3)
        far = lax.ppermute(blocks[3], "head", [(0, 3), (3, 0)])
        beside = swap(blocks[1], "head", 1, size)
        step = lax.ppermute(blocks[2], "head", [(0, 1), (1, 3), (3, 2), (2, 0)])
        both = (blocks[3].astype(f32) + step.astype(f32)).astype(bf16)
        middle = lax.ppermute(both, "head", [(1, 2), (2, 1)])
        arrived = [far, beside, jnp.where(ends, step, middle)]
    total = blocks[0]
    for block in arrived:
        total = total + block.astype(f32)
    return total.astype(bf16)


def body(
    hidden, norm_gain, w_query, w_key, w_value, w_out, stored_kv, selected, prompt_order, store_slot
):
    seq_count = lax.axis_size("seq")
    head_count = lax.axis_size("head")
    rows = hidden.shape[0]
    shard, _, local_kv, _ = stored_kv.shape
    stored = stored_kv.reshape(-1, HEAD_DIM)
    query, kv, table = project(hidden, norm_gain, selected, w_query, w_key, w_value)
    turns = sorted(range(2, seq_count, 2), key=lambda turn: (bin(turn).count("1"), turn))
    near, across = turns[:2]
    first, second = (near, across), (across, near)
    rest = [(turn, turn) for turn in turns[2:]]
    stored_other, kv_other = (swap(value, "seq", 1, seq_count) for value in (stored, kv))
    queries = {turn: swap(query, "seq", turn, seq_count) for turn in (first, second)}
    cache, key_pos, late = merge(
        prompt_order, store_slot, table, stored, stored_other, kv, kv_other, query
    )
    queries |= {turn: swap(late, "seq", turn, seq_count) for turn in rest}
    parts = [attend(((0, 0),), cache, key_pos, table, [query])[0]]
    for turn in rest:
        (part,) = attend((turn,), cache, key_pos, table, [queries[turn]])
        parts.append(swap(part, "seq", turn, seq_count))
    done = attend((first,), cache, key_pos, table, [queries[first]])
    done = attend((second,), cache, key_pos, table, [queries[second]], done)
    parts += [swap(part, "seq", turn, seq_count) for turn, part in zip((first, second), done)]
    blocks = finish(parts, w_out, head_count)
    total = sum_heads(blocks, head_count)
    new_kv = kv.reshape(rows, 2, local_kv, HEAD_DIM)
    return (total, new_kv)


def solution(mesh):
    in_specs = (
        P("seq", None),
        P(),
        P(None, "head"),
        P(None, "head"),
        P(None, "head"),
        P("head", None),
        P("seq", None, "head", None),
        P(),
        P(),
        P(),
    )
    out_specs = (P("seq", "head"), P("seq", None, "head", None))
    return jax.shard_map(body, mesh=mesh, in_specs=in_specs, out_specs=out_specs, check_vma=False)
```

```python
import functools
import math

import jax
import jax.numpy as jnp
import numpy as np
from jax import lax
from jax.experimental import pallas as pl
from jax.experimental.pallas import tpu as pltpu
from jax.sharding import PartitionSpec as P

HEADS = 32
KV_HEADS = 8
HEAD_DIM = 128
PASSAGE = 4096
GROUP = HEADS // KV_HEADS
MASKED = -1e30
LANES = 128
MIB = 1024 * 1024

bf16 = jnp.bfloat16
f32 = jnp.float32
NT = (((1,), (1,)), ((), ()))


def iota(shape, dim):
    return lax.broadcasted_iota(jnp.int32, shape, dim)


def column_of(row):
    n = row.shape[1]
    eye = iota((n, n), 0) == iota((n, n), 1)
    return jnp.sum(jnp.where(eye, row.astype(f32), 0.0), 1, keepdims=True)


def project_kernel(
    width, hidden_any, gain_any, selected_any, freq_any, wq_any, wk_any, wv_any, query, kv, table,
    hidden, gain, selected, freq, normed, weights, first_sem, sem,
):
    rows, feat = hidden.shape
    q_cols, k_cols, v_cols = wq_any.shape[1], wk_any.shape[1], wv_any.shape[1]
    pairs = ((hidden_any, hidden), (gain_any, gain), (selected_any, selected), (freq_any, freq))
    firsts = [
        pltpu.make_async_copy(source, target, first_sem.at[number])
        for number, (source, target) in enumerate(pairs)
    ]
    for copy in firsts:
        copy.start()
    chunks = []
    for source, count, base in ((wk_any, k_cols, 0), (wq_any, q_cols, k_cols), (wv_any, v_cols, k_cols + q_cols)):
        for at in range(0, count, width):
            chunks.append((source, at, base + at))
    copies = []
    for number, (source, at, place) in enumerate(chunks):
        copy = pltpu.make_async_copy(
            source.at[:, at : at + width], weights.at[:, place : place + width], sem.at[number]
        )
        copy.start(priority=1)
        copies.append(copy)
    for copy in firsts[1:]:
        copy.wait()
    total = selected.shape[0]
    me = lax.axis_index("seq")
    mine = iota((rows, total), 1) == iota((rows, total), 0) + me * rows
    listed = selected[...].reshape(1, total)
    positions = jnp.sum(jnp.where(mine, listed.astype(f32), 0.0), 1, keepdims=True)
    table[...] = jnp.full(table.shape, -1, jnp.int32)
    for at in range(total // rows):
        table[at : at + 1, 0:rows] = listed[:, at * rows : (at + 1) * rows]
    angle = positions * freq[...]
    cosine = jnp.cos(angle)
    sine = jnp.sin(angle)
    sine = jnp.where(iota(sine.shape, 1) < HEAD_DIM // 2, -sine, sine)
    firsts[0].wait()
    step = 16
    for at in range(0, rows, step):
        wide = hidden[at : at + step, :].astype(f32)
        mean = jnp.sum(wide * wide, 1, keepdims=True) * (1.0 / feat)
        normed[at : at + step, :] = (wide * lax.rsqrt(mean + 1e-5) * gain[...]).astype(bf16)
    for (source, at, place), copy in zip(chunks, copies):
        copy.wait()
        out = jnp.dot(normed[...], weights[:, place : place + width], preferred_element_type=f32)
        for head in range(0, width, HEAD_DIM):
            part = out[:, head : head + HEAD_DIM]
            if source is not wv_any:
                part = part * cosine + pltpu.roll(part, HEAD_DIM // 2, 1) * sine
            part = part.astype(bf16)
            if source is wq_any:
                query[:, at + head : at + head + HEAD_DIM] = part
            else:
                col = at + head + (0 if source is wk_any else k_cols)
                kv[:, col : col + HEAD_DIM] = part


def project(hidden, gain, selected, wq, wk, wv):
    rows, feat = hidden.shape
    cols = wq.shape[1] + wk.shape[1] + wv.shape[1]
    width = math.gcd(math.gcd(wq.shape[1], wk.shape[1]), 256)
    freq = 500000.0 ** (-(np.arange(HEAD_DIM // 2, dtype=np.float32) * np.float32(2.0 / HEAD_DIM)))
    freq = jnp.asarray(np.concatenate([freq, freq])[None, :].astype(np.float32))
    vmem = pl.BlockSpec(memory_space=pltpu.VMEM)
    hbm = pl.BlockSpec(memory_space=pltpu.HBM)
    return pl.pallas_call(
        functools.partial(project_kernel, width),
        out_shape=(
            jax.ShapeDtypeStruct((rows, wq.shape[1]), bf16),
            jax.ShapeDtypeStruct((rows, wk.shape[1] + wv.shape[1]), bf16),
            jax.ShapeDtypeStruct((selected.shape[0] // rows, LANES), jnp.int32),
        ),
        in_specs=[hbm] * 7,
        out_specs=(vmem, vmem, vmem),
        scratch_shapes=[
            pltpu.VMEM((rows, feat), bf16),
            pltpu.VMEM((1, feat), f32),
            pltpu.VMEM(selected.shape, jnp.int32),
            pltpu.VMEM((1, HEAD_DIM), f32),
            pltpu.VMEM((rows, feat), bf16),
            pltpu.VMEM((feat, cols), bf16),
            pltpu.SemaphoreType.DMA((4,)),
            pltpu.SemaphoreType.DMA((cols // width,)),
        ],
        compiler_params=pltpu.CompilerParams(vmem_limit_bytes=48 * MIB),
        cost_estimate=pl.CostEstimate(
            flops=2 * rows * feat * cols, bytes_accessed=2 * feat * (cols + rows), transcendentals=0
        ),
        name="project",
    )(*[
        pltpu.with_memory_space_constraint(operand, pltpu.HBM)
        for operand in (hidden, gain.reshape(1, feat), selected, freq, wq, wk, wv)
    ])


def block_of(index, shard, order, slot):
    per = PASSAGE // shard
    own = index // per
    place = jnp.int32(0)
    for at in range(order.shape[0]):
        place = jnp.where(slot[order[at]] == own, at, place)
    return place * per + lax.rem(index, per)


def merge_kernel(
    order, slot, selected, stored, stored_other, kv, kv_other, query, cache, key_pos, passed, wide
):
    passed[...] = query[...]
    _, shard, cols = cache.shape
    kinds = cols // LANES
    rows = kv.shape[0]
    step = 128
    me = lax.axis_index("seq")
    for half in range(2):
        index = me ^ half
        block = block_of(index, shard, order, slot)
        holes = selected[pl.ds(block, 1), :] - block * shard
        offsets = column_of(selected[pl.ds(index, 1), :] - index * shard)
        high = jnp.floor(offsets * (1.0 / 32))
        low = offsets - 32 * high
        given = iota((LANES, 1), 0) < rows
        sources = [
            jnp.broadcast_to(jnp.where(given, value, 0.0), (LANES, LANES)).astype(bf16)
            for value in (high, low + 1)
        ]
        fresh = (kv, kv_other)[half][...]
        if rows < LANES:
            fresh = jnp.concatenate([fresh, jnp.zeros((LANES - rows, cols), bf16)], 0)
        source = jnp.concatenate(sources + [fresh], 1)
        for at in range(0, shard, step):
            places = iota((step, LANES), 0) + at
            hit = (places == holes).astype(f32).astype(bf16)
            picked = jnp.dot(hit, source, preferred_element_type=f32)
            mark = picked[:, LANES : 2 * LANES]
            hole = mark > 0.5
            key_pos[half * shard + at : half * shard + at + step, :] = jnp.where(
                hole,
                picked[:, :LANES] * 32 + (mark - 1) + (index * shard).astype(f32),
                (places + block * shard).astype(f32),
            )
            slot_at = (at // step) % 2
            wide[slot_at, 0 : step * kinds, :] = (stored, stored_other)[half][
                at * kinds : (at + step) * kinds, :
            ].astype(f32)
            for kind in range(kinds):
                col = kind * LANES
                cache[half, at : at + step, col : col + LANES] = jnp.where(
                    hole,
                    picked[:, 2 * LANES + col : 3 * LANES + col],
                    wide[slot_at, pl.ds(kind, step, stride=kinds), :],
                ).astype(bf16)


def merge(order, slot, selected, stored, stored_other, kv, kv_other, query):
    cols = kv.shape[1]
    shard = stored.shape[0] * LANES // cols
    smem = pl.BlockSpec(memory_space=pltpu.SMEM)
    vmem = pl.BlockSpec(memory_space=pltpu.VMEM)
    return pl.pallas_call(
        merge_kernel,
        out_shape=(
            jax.ShapeDtypeStruct((2, shard, cols), bf16),
            jax.ShapeDtypeStruct((2 * shard, LANES), f32),
            jax.ShapeDtypeStruct(query.shape, query.dtype),
        ),
        in_specs=[smem, smem] + [vmem] * 6,
        out_specs=(vmem, vmem, vmem),
        scratch_shapes=[pltpu.VMEM((2, 128 * cols // LANES + 8, LANES), f32)],
        compiler_params=pltpu.CompilerParams(vmem_limit_bytes=16 * MIB),
        cost_estimate=pl.CostEstimate(flops=1000, bytes_accessed=1000, transcendentals=0),
        name="merge",
    )(order, slot, selected, stored, stored_other, kv, kv_other, query)


def attend_kernel(partners, carried, *refs):
    count = len(partners)
    cache, key_pos, selected = refs[:3]
    queries = refs[3 : 3 + count]
    scores, weights, masks = refs[-3:]
    for source, target in zip(refs[3 + count :], refs[3 + count + carried : -3 - count]):
        target[...] = source[...]
    outs = refs[-3 - count : -3]
    _, shard, cols = cache.shape
    rows = queries[0].shape[0]
    kv_heads = cols // (2 * HEAD_DIM)
    heads = kv_heads * GROUP
    keys = 2 * shard
    step = 256
    scale = math.log2(math.e) / HEAD_DIM**0.5
    me = lax.axis_index("seq")
    one_hot = (iota((rows, LANES), 0) == iota((rows, LANES), 1)).astype(f32).astype(bf16)
    ones = jnp.ones((keys, LANES), bf16)

    def mask(at):
        even, odd = partners[at]
        row = selected[pl.ds(me ^ jnp.where(me & 1 == 1, odd, even), 1), :].astype(f32)
        for place in range(0, keys, step):
            masks[at % 2, place : place + step, :] = jnp.where(
                key_pos[place : place + step, :] <= row, 0.0, MASKED
            ).astype(bf16)

    def left(at, head):
        parts = []
        for member in range(GROUP):
            col = (head * GROUP + member) * HEAD_DIM
            parts.append(jnp.concatenate([queries[at][:, col : col + HEAD_DIM], one_hot], 1))
        return jnp.concatenate(parts, 0)

    def cached(place, size, kind, head):
        col = (kind * kv_heads + head) * HEAD_DIM
        return cache[place // shard, place % shard : place % shard + size, col : col + HEAD_DIM]

    units = [(at, head) for at in range(count) for head in range(kv_heads)]
    best = {}
    for number in range(len(units) + 1):
        if number < len(units):
            at, head = units[number]
            if head == 0:
                mask(at)
            stream = left(at, head)
        if number:
            old_at, old_head = units[number - 1]
            top = jnp.max(best.pop(number - 1), 1, keepdims=True) * scale
        running = None
        for place in range(0, keys, step):
            if number < len(units):
                right = jnp.concatenate(
                    [cached(place, step, 0, head), masks[at % 2, place : place + step, :]], 1
                )
                score = lax.dot_general(stream, right, NT, preferred_element_type=f32)
                scores[number % 2, :, place : place + step] = score
                for col in range(0, step, LANES):
                    part = score[:, col : col + LANES]
                    running = part if running is None else jnp.maximum(running, part)
            if number:
                slot = (number - 1) % 2
                weights[:, place : place + step] = jnp.exp2(
                    scores[slot, :, place : place + step] * scale - top
                ).astype(bf16)
        if number < len(units):
            best[number] = running
        if number:
            value = jnp.concatenate([cached(half * shard, shard, 1, old_head) for half in range(2)], 0)
            summed = jnp.dot(
                weights[...], jnp.concatenate([value, ones], 1), preferred_element_type=f32
            )
            total = summed[:, HEAD_DIM : HEAD_DIM + LANES]
            context = (summed[:, :HEAD_DIM] / total).astype(bf16)
            level = top + jnp.log2(total)
            high = level.astype(bf16).astype(f32)
            middle = (level - high).astype(bf16).astype(f32)
            low = level - high - middle
            lane = iota((rows, LANES), 1)
            out = outs[old_at]
            packed = jnp.zeros((rows, LANES), f32)
            for member in range(GROUP):
                which = old_head * GROUP + member
                span = slice(member * rows, (member + 1) * rows)
                out[:, which * HEAD_DIM : (which + 1) * HEAD_DIM] = context[span]
                for piece, source in enumerate((high, middle, low)):
                    packed = jnp.where(lane == piece * heads + which, source[span], packed)
            tail = slice(heads * HEAD_DIM, heads * HEAD_DIM + LANES)
            if old_head:
                packed = packed + out[:, tail].astype(f32)
            out[:, tail] = packed.astype(bf16)


def attend(partners, cache, key_pos, selected, queries, earlier=()):
    _, shard, cols = cache.shape
    rows = queries[0].shape[0]
    kv_heads = cols // (2 * HEAD_DIM)
    out_cols = queries[0].shape[1] + LANES
    tall = GROUP * rows
    keys = 2 * shard
    count = len(queries)
    vmem = pl.BlockSpec(memory_space=pltpu.VMEM)
    out = pl.pallas_call(
        functools.partial(attend_kernel, partners, len(earlier)),
        out_shape=[jax.ShapeDtypeStruct((rows, out_cols), bf16)] * (len(earlier) + count),
        in_specs=[vmem] * (3 + count + len(earlier)),
        out_specs=[vmem] * (len(earlier) + count),
        scratch_shapes=[
            pltpu.VMEM((2, tall, keys), f32),
            pltpu.VMEM((tall, keys), bf16),
            pltpu.VMEM((2, keys, LANES), bf16),
        ],
        compiler_params=pltpu.CompilerParams(vmem_limit_bytes=24 * MIB),
        cost_estimate=pl.CostEstimate(flops=1000, bytes_accessed=1000, transcendentals=0),
        name="attend",
    )(cache, key_pos, selected, *queries, *earlier)
    return list(out)


def multiply(context, weights, turns, outs, size):
    width = weights.shape[1] // size
    step = 256 if width % 256 == 0 else width
    me = lax.axis_index("head")
    for turn, out in zip(turns, outs):
        start = (me ^ turn) * width
        for at in range(0, width, step):
            part = weights[:, pl.ds(pl.multiple_of(start + at, step), step)]
            out[:, at : at + step] = jnp.dot(
                context[...], part, preferred_element_type=f32
            ).astype(out.dtype)


def finish_kernel(count, turns, size, *refs):
    parts = refs[:count]
    weights = refs[count]
    context = refs[count + 1]
    feat = context.shape[1]
    heads = feat // HEAD_DIM
    tails = [part[:, feat : feat + LANES].astype(f32) for part in parts]
    for head in range(heads):
        levels = []
        for tail in tails:
            pieces = [tail[:, piece * heads + head : piece * heads + head + 1] for piece in range(3)]
            levels.append(pieces[0] + pieces[1] + pieces[2])
        top = functools.reduce(jnp.maximum, levels)
        shares = [jnp.exp2(level - top) for level in levels]
        whole = functools.reduce(jnp.add, shares)
        span = slice(head * HEAD_DIM, (head + 1) * HEAD_DIM)
        mixed = functools.reduce(
            jnp.add, [(share / whole) * part[:, span].astype(f32) for share, part in zip(shares, parts)]
        )
        context[:, span] = mixed.astype(bf16)
    multiply(context, weights, turns, refs[count + 2 :], size)


def more_kernel(turns, size, context, weights, *outs):
    multiply(context, weights, turns, outs, size)


def finish(parts, w_out, size):
    rows = parts[0].shape[0]
    feat, cols = w_out.shape
    vmem = pl.BlockSpec(memory_space=pltpu.VMEM)
    options = dict(
        compiler_params=pltpu.CompilerParams(vmem_limit_bytes=24 * MIB),
        cost_estimate=pl.CostEstimate(flops=1000, bytes_accessed=1000, transcendentals=0),
    )
    early, later = (2,), tuple(turn for turn in (3, 1, 0) if turn < size)

    def shape(turn):
        return jax.ShapeDtypeStruct((rows, cols // size), bf16 if turn else f32)

    context, *some = pl.pallas_call(
        functools.partial(finish_kernel, len(parts), early, size),
        out_shape=[jax.ShapeDtypeStruct((rows, feat), bf16)] + [shape(turn) for turn in early],
        in_specs=[vmem] * (len(parts) + 1),
        out_specs=[vmem] * (1 + len(early)),
        name="finish",
        **options,
    )(*parts, w_out)
    others = pl.pallas_call(
        functools.partial(more_kernel, later, size),
        out_shape=[shape(turn) for turn in later],
        in_specs=[vmem] * 2,
        out_specs=[vmem] * len(later),
        name="more",
        **options,
    )(context, w_out)
    return dict(zip(early + later, some + list(others)))


def swap(value, axis, turn, size):
    even, odd = turn if isinstance(turn, tuple) else (turn, turn)
    return lax.ppermute(value, axis, [(at, at ^ (odd if at & 1 else even)) for at in range(size)])


def sum_heads(blocks, size):
    if size != 4:
        arrived = [swap(blocks[turn], "head", turn, size) for turn in range(1, size)]
    else:
        me = lax.axis_index("head")
        ends = (me == 0) | (me == 3)
        far = lax.ppermute(blocks[3], "head", [(0, 3), (3, 0)])
        beside = swap(blocks[1], "head", 1, size)
        step = lax.ppermute(blocks[2], "head", [(0, 1), (1, 3), (3, 2), (2, 0)])
        both = (blocks[3].astype(f32) + step.astype(f32)).astype(bf16)
        middle = lax.ppermute(both, "head", [(1, 2), (2, 1)])
        arrived = [far, beside, jnp.where(ends, step, middle)]
    total = blocks[0]
    for block in arrived:
        total = total + block.astype(f32)
    return total.astype(bf16)


def body(
    hidden, norm_gain, w_query, w_key, w_value, w_out, stored_kv, selected, prompt_order, store_slot
):
    seq_count = lax.axis_size("seq")
    head_count = lax.axis_size("head")
    rows = hidden.shape[0]
    shard, _, local_kv, _ = stored_kv.shape
    stored = stored_kv.reshape(-1, HEAD_DIM)
    query, kv, table = project(hidden, norm_gain, selected, w_query, w_key, w_value)
    turns = sorted(range(2, seq_count, 2), key=lambda turn: (bin(turn).count("1"), turn))
    near, across = turns[:2]
    first, second = (near, across), (across, near)
    rest = [(turn, turn) for turn in turns[2:]]
    stored_other, kv_other = (swap(value, "seq", 1, seq_count) for value in (stored, kv))
    queries = {turn: swap(query, "seq", turn, seq_count) for turn in (first, second)}
    cache, key_pos, late = merge(
        prompt_order, store_slot, table, stored, stored_other, kv, kv_other, query
    )
    queries |= {turn: swap(late, "seq", turn, seq_count) for turn in rest}
    parts = [attend(((0, 0),), cache, key_pos, table, [query])[0]]
    for turn in rest:
        (part,) = attend((turn,), cache, key_pos, table, [queries[turn]])
        parts.append(swap(part, "seq", turn, seq_count))
    done = attend((first,), cache, key_pos, table, [queries[first]])
    done = attend((second,), cache, key_pos, table, [queries[second]], done)
    parts += [swap(part, "seq", turn, seq_count) for turn, part in zip((first, second), done)]
    blocks = finish(parts, w_out, head_count)
    total = sum_heads(blocks, head_count)
    new_kv = kv.reshape(rows, 2, local_kv, HEAD_DIM)
    return (total, new_kv)


def solution(mesh):
    in_specs = (
        P("seq", None),
        P(),
        P(None, "head"),
        P(None, "head"),
        P(None, "head"),
        P("head", None),
        P("seq", None, "head", None),
        P(),
        P(),
        P(),
    )
    out_specs = (P("seq", "head"), P("seq", None, "head", None))
    return jax.shard_map(body, mesh=mesh, in_specs=in_specs, out_specs=out_specs, check_vma=False)
```
